32 devices in a mesh: dp: 32 (over z, y, x, core).
Axes of the slice: x: 2, y: 2, z: 4, core: 2. Of those that a mesh axis runs over, the one named last changes fastest.
Arguments:
- tokens: bfloat16 [32768, 1024], P('dp'), may hold values from -6 to 6
- w_query: bfloat16 [1024, 1024], P('dp'), may hold values from -0.1875 to 0.1875
- w_key: bfloat16 [1024, 1024], P('dp'), may hold values from -0.1875 to 0.1875
- w_value: bfloat16 [1024, 1024], P('dp'), may hold values from -0.1875 to 0.1875
- w_out: bfloat16 [1024, 1024], P('dp'), may hold values from -0.75 to 0.75
- w_up: bfloat16 [1024, 4096], P('dp'), may hold values from -0.1875 to 0.1875
- w_down: bfloat16 [4096, 1024], P('dp'), may hold values from -0.09375 to 0.09375
- b_query: bfloat16 [1024], P('dp'), may hold values from -3 to 3
- b_value: bfloat16 [1024], P('dp'), may hold values from -3 to 3
- b_out: bfloat16 [1024], P('dp'), may hold values from -3 to 3
- b_up: bfloat16 [4096], P('dp'), may hold values from -3 to 3
- b_down: bfloat16 [1024], P('dp'), may hold values from -3 to 3
- gain_attn: bfloat16 [1024], P('dp'), may hold values from 0.25 to 1.75
- shift_attn: bfloat16 [1024], P('dp'), may hold values from -3 to 3
- gain_ffn: bfloat16 [1024], P('dp'), may hold values from 0.25 to 1.75
- shift_ffn: bfloat16 [1024], P('dp'), may hold values from -3 to 3
- cotangent: bfloat16 [32768, 1024], P('dp'), may hold values from -6 to 6
Outputs:
- layer_out: bfloat16 [32768, 1024], P('dp')
- grad_tokens: bfloat16 [32768, 1024], P('dp')
- grad_w_query: float32 [1024, 1024], P('dp')
- grad_w_key: float32 [1024, 1024], P('dp')
- grad_w_value: float32 [1024, 1024], P('dp')
- grad_w_out: float32 [1024, 1024], P('dp')
- grad_w_up: float32 [1024, 4096], P('dp')
- grad_w_down: float32 [4096, 1024], P('dp')
- grad_b_query: float32 [1024], P('dp')
- grad_b_value: float32 [1024], P('dp')
- grad_b_out: float32 [1024], P('dp')
- grad_b_up: float32 [4096], P('dp')
- grad_b_down: float32 [1024], P('dp')
- grad_gain_attn: float32 [1024], P('dp')
- grad_shift_attn: float32 [1024], P('dp')
- grad_gain_ffn: float32 [1024], P('dp')
- grad_shift_ffn: float32 [1024], P('dp')
The draws below stay inside these ranges and needn't reach their ends.
All inputs are finite; a program needn't handle non-finite values.
Results may differ from the reference program's by a relative error of at most 0.015.
Values may be sent and summed in bfloat16 or wider, within the bound.
No kernel may reach another device: no remote copies, remote signals or barrier semaphores. Data moves between devices by JAX's collectives and lax.ppermute only.
A program may use at most 256 MiB of HBM per device.

```python
import jax
import jax.numpy as jnp
from jax import lax

D = 1024
FF = 4096
HEADS = 16
LEN = 512
TOKENS = 32768


def spiked(drawn, own_key, source, target, blocks, factor):
    owner, partner = [(jnp.arange(drawn.shape[dim]) // (drawn.shape[dim] // blocks)).reshape([-1 if axis == dim else 1 for axis in range(drawn.ndim)]) for dim in (source, target)]
    chosen = jax.random.permutation(own_key, blocks)[partner]
    strong = (owner == chosen) | (owner == (partner + blocks // 2) % blocks)
    return jnp.where(strong, factor * drawn, drawn)


def level_of(rng, shape, shards, smallest, high):
    loudness, own = 1.0, jax.random.fold_in(rng, 6)
    for position, blocks in shards:
        draws = jnp.exp(jax.random.uniform(jax.random.fold_in(own, position), (blocks,), jnp.float32, smallest / len(shards), high / len(shards)))
        loudness = loudness * jnp.repeat(draws, shape[position] // blocks).reshape([-1 if axis == position else 1 for axis in range(len(shape))])
    return loudness


def centred(own_key, extent, scale, most, cuts=(), kind=jnp.bfloat16):
    array = jax.random.normal(own_key, extent, jnp.float32) * scale
    if len(cuts) > 0:
        array = level_of(own_key, extent, cuts, -0.22, 0.18) * array
    return jnp.clip(array, min=-most, max=most).astype(kind)


def heavy_noise(stream_key, extent, width, bound, split, heavy, kind=jnp.bfloat16):
    entries = width * jax.random.normal(stream_key, extent, jnp.float32)
    if split:
        entries = entries * level_of(stream_key, extent, split, -0.22, 0.18)
    return jnp.clip(spiked(entries, jax.random.fold_in(stream_key, 3), *heavy), -bound, bound).astype(kind)


def setup_inputs(seed: int = 0) -> dict:
    key_list = jax.random.split(jax.random.key(seed), 18)
    return {
        "tokens": centred(key_list[0], (TOKENS, D), 1.0, 6.0, ((0, 32),)),
        "w_query": centred(key_list[1], (D, D), D ** -0.5, 0.1875, ((0, 32),)),
        "w_key": centred(key_list[2], (D, D), D ** -0.5, 0.1875, ((0, 32),)),
        "w_value": centred(key_list[3], (D, D), D ** -0.5, 0.1875, ((0, 32),)),
        "w_out": centred(key_list[4], (D, D), (D // 16) ** -0.5, 0.75, ((0, 32),)),
        "w_up": centred(key_list[5], (D, FF), D ** -0.5, 0.1875, ((0, 32),)),
        "w_down": centred(key_list[6], (FF, D), FF ** -0.5, 0.09375, ((0, 32),)),
        "b_query": centred(key_list[7], (D,), 0.5, 3.0, ((0, 32),)),
        "b_value": centred(key_list[8], (D,), 0.5, 3.0, ((0, 32),)),
        "b_out": centred(key_list[9], (D,), 0.5, 3.0, ((0, 32),)),
        "b_up": centred(key_list[10], (FF,), 0.5, 3.0, ((0, 32),)),
        "b_down": centred(key_list[11], (D,), 0.5, 3.0, ((0, 32),)),
        "gain_attn": jnp.clip(1.0 + 0.15 * jax.random.normal(key_list[12], (D,), jnp.float32), 0.25, 1.75).astype(jnp.bfloat16),
        "shift_attn": centred(key_list[13], (D,), 0.5, 3.0, ((0, 32),)),
        "gain_ffn": jnp.clip(1.0 + 0.15 * jax.random.normal(key_list[14], (D,), jnp.float32), 0.25, 1.75).astype(jnp.bfloat16),
        "shift_ffn": centred(key_list[15], (D,), 0.5, 3.0, ((0, 32),)),
        "cotangent": heavy_noise(key_list[16], (TOKENS, D), 1.0, 6.0, ((0, 32),), (0, 1, 32, 2.75)),
    }


EPS = 1e-12
PRECISE = lax.Precision.HIGHEST

@jax.custom_vjp
def low(v):
    return lax.optimization_barrier(v.astype(jnp.bfloat16)).astype(jnp.float32)

@jax.custom_vjp
def low_back(v):
    return v

def low_keep(v):
    return (low(v), None)

def low_pass(kept, grad):
    return (grad,)

def back_keep(v):
    return (v, None)

def back_low(kept, grad):
    return (low(grad),)
low.defvjp(low_keep, low_pass)
low_back.defvjp(back_keep, back_low)

def precise_dot(left_side, right_side):
    return jnp.dot(left_side, right_side, precision=PRECISE, preferred_element_type=jnp.float32)

def layer_norm(summed, gain_vec, shift_vec):
    centre = lax.optimization_barrier(jnp.mean(summed, axis=-1, keepdims=True))
    centered = summed - centre
    spread = lax.optimization_barrier(jnp.mean(centered * centered, axis=-1, keepdims=True))
    return centered * lax.rsqrt(spread + EPS) * gain_vec + shift_vec

def forward(rows_in, params):
    w_query, w_key, w_value, w_out, w_up, w_down, b_query, b_value, b_out, b_up, b_down, gain_attn, shift_attn, gain_ffn, shift_ffn = params
    head_dim = D // HEADS
    score_scale = head_dim ** (-0.5)
    head_shape = (LEN, HEADS, head_dim)
    queries = low_back(low(precise_dot(rows_in, w_query) + b_query))
    key_rows = low_back(low(precise_dot(rows_in, w_key)))
    values = low_back(low(precise_dot(rows_in, w_value) + b_value))
    scores = low_back(score_scale * jnp.einsum('qhe,khe->hqk', queries.reshape(head_shape), key_rows.reshape(head_shape), precision=PRECISE))
    maxima = lax.optimization_barrier(jnp.max(scores, axis=-1, keepdims=True))
    exponent = jnp.exp(scores - maxima)
    attn_probs = low_back(low(exponent / lax.optimization_barrier(jnp.sum(exponent, axis=-1, keepdims=True))))
    mixed = jnp.einsum('hqk,khe->qhe', attn_probs, values.reshape(head_shape), precision=PRECISE)
    attn_rows = low_back(low(mixed.reshape(LEN, D)))
    branch = low_back(precise_dot(attn_rows, w_out) + b_out)
    first_out = layer_norm(rows_in + branch, gain_attn, shift_attn)
    pre_act = low_back(precise_dot(low(first_out), w_up) + b_up)
    hidden = low(jax.nn.gelu(pre_act, approximate=False))
    ffn_out = low_back(precise_dot(hidden, w_down) + b_down)
    return layer_norm(first_out + ffn_out, gain_ffn, shift_ffn)

def reference(tokens, w_query, w_key, w_value, w_out, w_up, w_down, b_query, b_value, b_out, b_up, b_down, gain_attn, shift_attn, gain_ffn, shift_ffn, cotangent):
    params = (w_query, w_key, w_value, w_out, w_up, w_down, b_query, b_value, b_out, b_up, b_down, gain_attn, shift_attn, gain_ffn, shift_ffn)
    floats = tuple((param_array.astype(jnp.float32) for param_array in params))
    seq_tokens = tokens.astype(jnp.float32).reshape(-1, LEN, D)
    seq_cots = cotangent.astype(jnp.float32).reshape(-1, LEN, D)

    def one_sequence(running, sequence):
        rows_in, cot_rows = sequence
        result, pull_back = jax.vjp(forward, rows_in, floats)
        grad_rows, grad_params = pull_back(cot_rows)
        running = tuple((running_sum + new_part for running_sum, new_part in zip(running, grad_params)))
        return (running, (result.astype(jnp.bfloat16), grad_rows.astype(jnp.bfloat16)))
    zero_sums = tuple((jnp.zeros(param_array.shape, jnp.float32) for param_array in floats))
    totals, (outputs, grad_rows) = lax.scan(one_sequence, zero_sums, (seq_tokens, seq_cots))
    return (outputs.reshape(-1, D), grad_rows.reshape(-1, D), totals[0], totals[1], totals[2], totals[3], totals[4], totals[5], totals[6], totals[7], totals[8], totals[9], totals[10], totals[11], totals[12], totals[13], totals[14])
```

```python
import jax
import jax.numpy as jnp
from jax import lax
from jax.sharding import PartitionSpec as P

D = 1024
HEADS = 16
LEN = 512
SPLIT = 640


EPS = 1e-12


def matmul(left_side, right_side):
    return jnp.dot(left_side, right_side, preferred_element_type=jnp.float32)


def layer_norm(summed, gain_vec, shift_vec):
    centre = jnp.mean(summed, axis=-1, keepdims=True)
    centered = summed - centre
    spread = jnp.mean(centered * centered, axis=-1, keepdims=True)
    inverse = lax.rsqrt(spread + EPS)
    normed = centered * inverse
    return (normed * gain_vec + shift_vec, normed, inverse)


def norm_back(upstream, gain_vec, normed, inverse):
    scaled = upstream * gain_vec
    mean_grad = jnp.mean(scaled, axis=-1, keepdims=True)
    mean_cross = jnp.mean(scaled * normed, axis=-1, keepdims=True)
    return inverse * (scaled - mean_grad - normed * mean_cross)


def exact_gelu(point):
    return jax.nn.gelu(point, approximate=False)


def column_sum(grad_rows):
    return jnp.sum(grad_rows.astype(jnp.float32), axis=0)


def forward_pass(rows_in, gathered):
    (
        w_query,
        w_key,
        w_value,
        w_out,
        w_up,
        w_down,
        b_query,
        b_value,
        b_out,
        b_up,
        b_down,
        gain_attn,
        shift_attn,
        gain_ffn,
        shift_ffn,
    ) = gathered
    row_count = rows_in.shape[0]
    seq_count = row_count // LEN
    head_dim = D // HEADS
    score_scale = head_dim ** (-0.5)
    head_shape = (seq_count, LEN, HEADS, head_dim)
    queries = (matmul(rows_in, w_query) + b_query.astype(jnp.float32)).astype(jnp.bfloat16)
    key_rows = matmul(rows_in, w_key).astype(jnp.bfloat16)
    values = (matmul(rows_in, w_value) + b_value.astype(jnp.float32)).astype(jnp.bfloat16)
    scores = score_scale * jnp.einsum(
        "sqhe,skhe->shqk",
        queries.reshape(head_shape),
        key_rows.reshape(head_shape),
        preferred_element_type=jnp.float32,
    )
    maxima = jnp.max(scores, axis=-1, keepdims=True)
    exponent = jnp.exp(scores - maxima)
    row_totals = jnp.sum(exponent, axis=-1, keepdims=True)
    attn_probs = exponent / row_totals
    logsum = maxima + jnp.log(row_totals)
    mixed = jnp.einsum(
        "shqk,skhe->sqhe",
        attn_probs.astype(jnp.bfloat16),
        values.reshape(head_shape),
        preferred_element_type=jnp.float32,
    )
    attn_rows = mixed.reshape(row_count, D).astype(jnp.bfloat16)
    branch = matmul(attn_rows, w_out) + b_out.astype(jnp.float32)
    first_out, first_normed, first_inverse = layer_norm(
        rows_in.astype(jnp.float32) + branch,
        gain_attn.astype(jnp.float32),
        shift_attn.astype(jnp.float32),
    )
    first_low = first_out.astype(jnp.bfloat16)
    pre_act = matmul(first_low, w_up) + b_up.astype(jnp.float32)
    hidden = exact_gelu(pre_act).astype(jnp.bfloat16)
    ffn_out = matmul(hidden, w_down) + b_down.astype(jnp.float32)
    result, second_normed, second_inverse = layer_norm(
        first_out + ffn_out, gain_ffn.astype(jnp.float32), shift_ffn.astype(jnp.float32)
    )
    stored = (
        queries,
        key_rows,
        values,
        logsum,
        attn_rows,
        first_normed,
        first_inverse,
        first_low,
        pre_act,
        hidden,
        second_normed,
        second_inverse,
    )
    return (result, stored)


def backward_pass(rows_in, cot_rows, gathered, stored):
    (
        w_query,
        w_key,
        w_value,
        w_out,
        w_up,
        w_down,
        b_query,
        b_value,
        b_out,
        b_up,
        b_down,
        gain_attn,
        shift_attn,
        gain_ffn,
        shift_ffn,
    ) = gathered
    (
        queries,
        key_rows,
        values,
        logsum,
        attn_rows,
        first_normed,
        first_inverse,
        first_low,
        pre_act,
        hidden,
        second_normed,
        second_inverse,
    ) = stored
    row_count = rows_in.shape[0]
    seq_count = row_count // LEN
    head_dim = D // HEADS
    score_scale = head_dim ** (-0.5)
    head_shape = (seq_count, LEN, HEADS, head_dim)
    upstream = cot_rows.astype(jnp.float32)
    d_gain_ffn = jnp.sum(upstream * second_normed, axis=0)
    d_shift_ffn = jnp.sum(upstream, axis=0)
    d_second = norm_back(upstream, gain_ffn.astype(jnp.float32), second_normed, second_inverse)
    d_ffn = d_second.astype(jnp.bfloat16)
    d_b_down = column_sum(d_ffn)
    d_w_down = jnp.einsum("tf,td->fd", hidden, d_ffn, preferred_element_type=jnp.float32)
    d_hidden = jnp.einsum("td,fd->tf", d_ffn, w_down, preferred_element_type=jnp.float32)
    gelu_pull = jax.vjp(exact_gelu, pre_act)[1]
    d_pre = gelu_pull(d_hidden)[0].astype(jnp.bfloat16)
    d_b_up = column_sum(d_pre)
    d_w_up = jnp.einsum("td,tf->df", first_low, d_pre, preferred_element_type=jnp.float32)
    d_first = d_second + jnp.einsum("tf,df->td", d_pre, w_up, preferred_element_type=jnp.float32)
    d_gain_attn = jnp.sum(d_first * first_normed, axis=0)
    d_shift_attn = jnp.sum(d_first, axis=0)
    d_resid = norm_back(d_first, gain_attn.astype(jnp.float32), first_normed, first_inverse)
    d_branch = d_resid.astype(jnp.bfloat16)
    d_b_out = column_sum(d_branch)
    d_w_out = jnp.einsum("ti,to->io", attn_rows, d_branch, preferred_element_type=jnp.float32)
    d_attn = jnp.einsum("to,io->ti", d_branch, w_out, preferred_element_type=jnp.float32).astype(
        jnp.bfloat16
    )
    query_heads = queries.reshape(head_shape)
    key_heads = key_rows.reshape(head_shape)
    value_heads = values.reshape(head_shape)
    grad_heads = d_attn.reshape(head_shape)
    scores = score_scale * jnp.einsum(
        "sqhe,skhe->shqk", query_heads, key_heads, preferred_element_type=jnp.float32
    )
    attn_probs = jnp.exp(scores - logsum)
    d_probs = jnp.einsum(
        "sqhe,skhe->shqk", grad_heads, value_heads, preferred_element_type=jnp.float32
    )
    d_probs = lax.optimization_barrier(d_probs.astype(jnp.bfloat16)).astype(jnp.float32)
    d_values = (
        jnp.einsum(
            "shqk,sqhe->skhe",
            attn_probs.astype(jnp.bfloat16),
            grad_heads,
            preferred_element_type=jnp.float32,
        )
        .reshape(row_count, D)
        .astype(jnp.bfloat16)
    )
    d_scores = (
        attn_probs * (d_probs - jnp.sum(d_probs * attn_probs, axis=-1, keepdims=True))
    ).astype(jnp.bfloat16)
    d_queries = (
        (
            score_scale
            * jnp.einsum("shqk,skhe->sqhe", d_scores, key_heads, preferred_element_type=jnp.float32)
        )
        .reshape(row_count, D)
        .astype(jnp.bfloat16)
    )
    d_keys = (
        (
            score_scale
            * jnp.einsum(
                "shqk,sqhe->skhe", d_scores, query_heads, preferred_element_type=jnp.float32
            )
        )
        .reshape(row_count, D)
        .astype(jnp.bfloat16)
    )
    d_b_query = column_sum(d_queries)
    d_b_value = column_sum(d_values)
    d_w_query = jnp.einsum("ti,to->io", rows_in, d_queries, preferred_element_type=jnp.float32)
    d_w_key = jnp.einsum("ti,to->io", rows_in, d_keys, preferred_element_type=jnp.float32)
    d_w_value = jnp.einsum("ti,to->io", rows_in, d_values, preferred_element_type=jnp.float32)
    grad_rows = d_resid + jnp.einsum(
        "to,io->ti", d_queries, w_query, preferred_element_type=jnp.float32
    )
    grad_rows = grad_rows + jnp.einsum(
        "to,io->ti", d_keys, w_key, preferred_element_type=jnp.float32
    )
    grad_rows = grad_rows + jnp.einsum(
        "to,io->ti", d_values, w_value, preferred_element_type=jnp.float32
    )
    gradients = (
        d_w_query,
        d_w_key,
        d_w_value,
        d_w_out,
        d_w_up,
        d_w_down,
        d_b_query,
        d_b_value,
        d_b_out,
        d_b_up,
        d_b_down,
        d_gain_attn,
        d_shift_attn,
        d_gain_ffn,
        d_shift_ffn,
    )
    return (gradients, grad_rows)


def ring_pairs(count):
    return [(place, (place + 8) % count) for place in range(count)]


def flip_pairs(count, bit):
    return [(place, place ^ bit) for place in range(count)]


FLIPS = {"c": 1, "x": 2, "y": 4}


def gather_part(shard, order, count):
    stack = shard[None]
    for dim in order + "c":
        if dim == "z":
            pieces = [stack]
            for _ in range(count // 8 - 1):
                pieces.append(lax.ppermute(pieces[-1], "dp", ring_pairs(count)))
        else:
            pieces = [stack, lax.ppermute(stack, "dp", flip_pairs(count, FLIPS[dim]))]
        stack = jnp.concatenate(pieces, axis=0)
    return stack


def add_low(left_side, right_side):
    return (left_side.astype(jnp.float32) + right_side.astype(jnp.float32)).astype(jnp.bfloat16)


def scatter_part(stack, order, count):
    for dim in "c" + order[::-1]:
        last = dim == order[0]
        if dim == "z":
            ring = count // 8
            blocks = stack.reshape((ring, stack.shape[0] // ring) + stack.shape[1:])
            moving = blocks[1]
            for step in range(2, ring):
                moving = add_low(lax.ppermute(moving, "dp", ring_pairs(count)), blocks[step])
            moving = lax.ppermute(moving, "dp", ring_pairs(count))
            kept = blocks[0]
        else:
            half = stack.shape[0] // 2
            moving = lax.ppermute(stack[half:], "dp", flip_pairs(count, FLIPS[dim]))
            kept = stack[:half]
        if last:
            return (kept.astype(jnp.float32) + moving.astype(jnp.float32))[0]
        stack = add_low(kept, moving)


def places(order, count):
    me = lax.axis_index("dp")
    other = jnp.arange(count, dtype=jnp.int32)
    digits = {
        "z": lax.rem(me // 8 - other // 8 + count // 8, count // 8),
        "y": (me // 4 % 2) ^ (other // 4 % 2),
        "x": (me // 2 % 2) ^ (other // 2 % 2),
        "c": (me % 2) ^ (other % 2),
    }
    weight, position = 1, jnp.zeros_like(other)
    for dim in order + "c":
        position = position + weight * digits[dim]
        weight = weight * (count // 8 if dim == "z" else 2)
    return position


ORDERS = ("zyx", "xzy")


def gather_rows(shard, count):
    sides = (shard[:, :SPLIT], shard[:, SPLIT:])
    stacks = [gather_part(side, order, count) for side, order in zip(sides, ORDERS)]
    ordered = [
        jnp.take(stack, places(order, count), axis=0) for stack, order in zip(stacks, ORDERS)
    ]
    return jnp.concatenate(ordered, axis=-1)


def scatter_rows(blocks, count):
    me_sides = (blocks[..., :SPLIT], blocks[..., SPLIT:])
    sums = []
    for side, order in zip(me_sides, ORDERS):
        position = places(order, count)
        relative = jnp.take(side, jnp.argsort(position), axis=0)
        sums.append(scatter_part(relative, order, count))
    return jnp.concatenate(sums, axis=-1)


def vector_rows(vectors, rows):
    flat = jnp.concatenate(vectors, axis=-1)
    width = flat.shape[-1]
    lead = flat.shape[:-1]
    flat = jnp.pad(flat, [(0, 0)] * len(lead) + [(0, rows * D - width)])
    return flat.reshape(lead + (rows, D))


def local(
    tokens,
    w_query,
    w_key,
    w_value,
    w_out,
    w_up,
    w_down,
    b_query,
    b_value,
    b_out,
    b_up,
    b_down,
    gain_attn,
    shift_attn,
    gain_ffn,
    shift_ffn,
    cotangent,
):
    count = D // w_query.shape[0]
    part = D // count
    vectors = (
        b_query, b_value, b_out, b_down, gain_attn, shift_attn, gain_ffn, shift_ffn, b_up,
    )
    up_cols = w_up.shape[1] // D
    first = jnp.concatenate([w_query, w_key, w_value, vector_rows(vectors, 16)], axis=0)
    second = jnp.concatenate([w_out] + [w_up[:, D * col : D * col + D] for col in range(up_cols)], axis=0)
    first = gather_rows(first, count)
    second = gather_rows(second, count)
    third = gather_rows(w_down, count)
    weight = lambda col: first[:, part * col : part * col + part].reshape(D, D)
    flat = first[:, 3 * part :].reshape(count, -1)
    vec = lambda col: flat[:, part * col : part * col + part].reshape(D)
    ff_part = b_up.shape[0]
    full = (
        weight(0), weight(1), weight(2),
        second[:, :part].reshape(D, D),
        second[:, part:].reshape(count, up_cols, part, D).transpose(0, 2, 1, 3).reshape(D, up_cols * D),
        third.reshape(-1, D),
        vec(0), vec(1), vec(2),
        flat[:, 8 * part : 8 * part + ff_part].reshape(-1),
        vec(3), vec(4), vec(5), vec(6), vec(7),
    )
    result, stored = forward_pass(tokens, full)
    gradients, grad_rows = backward_pass(tokens, cotangent, full, stored)
    (
        d_w_query, d_w_key, d_w_value, d_w_out, d_w_up, d_w_down,
        d_b_query, d_b_value, d_b_out, d_b_up, d_b_down,
        d_gain_attn, d_shift_attn, d_gain_ffn, d_shift_ffn,
    ) = gradients
    low = lambda grad: grad.astype(jnp.bfloat16)
    blocks = lambda grad: low(grad).reshape(count, -1, D)
    third = scatter_rows(blocks(d_w_down), count)
    up_blocks = low(d_w_up).reshape(count, part, up_cols, D).transpose(0, 2, 1, 3).reshape(count, -1, D)
    second = scatter_rows(jnp.concatenate([blocks(d_w_out), up_blocks], axis=1), count)
    vectors = (
        d_b_query, d_b_value, d_b_out, d_b_down, d_gain_attn, d_shift_attn, d_gain_ffn, d_shift_ffn, d_b_up,
    )
    packed = vector_rows([low(vector).reshape(count, -1) for vector in vectors], 16)
    first = scatter_rows(
        jnp.concatenate([blocks(d_w_query), blocks(d_w_key), blocks(d_w_value), packed], axis=1), count
    )
    flat = first[3 * part :].reshape(-1)
    vec = lambda col: flat[part * col : part * col + part]
    return (
        result.astype(jnp.bfloat16),
        grad_rows.astype(jnp.bfloat16),
        first[:part], first[part : 2 * part], first[2 * part : 3 * part],
        second[:part],
        second[part:].reshape(up_cols, part, D).transpose(1, 0, 2).reshape(part, up_cols * D),
        third,
        vec(0), vec(1), vec(2),
        flat[8 * part : 8 * part + ff_part],
        vec(3), vec(4), vec(5), vec(6), vec(7),
    )


def solution(mesh):
    placed = (
        P("dp", None),
        P("dp", None),
        P("dp", None),
        P("dp", None),
        P("dp", None),
        P("dp", None),
        P("dp", None),
        P("dp"),
        P("dp"),
        P("dp"),
        P("dp"),
        P("dp"),
        P("dp"),
        P("dp"),
        P("dp"),
        P("dp"),
        P("dp", None),
    )
    return jax.shard_map(
        local,
        mesh=mesh,
        in_specs=placed,
        out_specs=(
            P("dp", None),
            P("dp", None),
            P("dp", None),
            P("dp", None),
            P("dp", None),
            P("dp", None),
            P("dp", None),
            P("dp", None),
            P("dp"),
            P("dp"),
            P("dp"),
            P("dp"),
            P("dp"),
            P("dp"),
            P("dp"),
            P("dp"),
            P("dp"),
        ),
        check_vma=False,
    )
```

```python
import functools
import jax
import jax.numpy as jnp
from jax import lax
from jax.experimental import pallas as pl
from jax.experimental.pallas import tpu as pltpu
from jax.sharding import PartitionSpec as P

D = 1024
HEADS = 16
LEN = 512
EPS = 1e-12
LOW = jnp.bfloat16
FULL = jnp.float32
MIB = 1024 * 1024
WIDE = 512
STRIP = 256


def dot_nn(left_side, right_side):
    return lax.dot_general(left_side, right_side, (((1,), (0,)), ((), ())), preferred_element_type=FULL)


def dot_nt(left_side, right_side):
    return lax.dot_general(left_side, right_side, (((1,), (1,)), ((), ())), preferred_element_type=FULL)


def dot_tn(left_side, right_side):
    return lax.dot_general(left_side, right_side, (((0,), (0,)), ((), ())), preferred_element_type=FULL)


def head_mask(rows, head):
    lane = lax.broadcasted_iota(jnp.int32, (rows, 128), 1)
    return (lane // 64) == head


def attend_kernel(q_ref, k_ref, v_ref, probs_ref, rows_ref):
    scale = (D // HEADS) ** -0.5
    queries = (q_ref[...].astype(FULL) * scale).astype(LOW)
    keys, values = k_ref[...], v_ref[...]
    mixed = jnp.zeros((LEN, 128), FULL)
    for head in range(2):
        mask = head_mask(LEN, head)
        zero = jnp.zeros((), LOW)
        scores = dot_nt(queries, jnp.where(mask, keys, zero))
        maxima = jnp.max(scores, axis=-1, keepdims=True)
        exponent = jnp.exp(scores - maxima)
        total = jnp.sum(exponent, axis=-1, keepdims=True)
        probs = (exponent * (1.0 / total)).astype(LOW)
        probs_ref[0, head] = probs
        mixed = mixed + dot_nn(probs, jnp.where(mask, values, zero))
    rows_ref[...] = mixed.astype(LOW)


def placed(kernel, ins, count, *refs):
    kernel(*refs[:ins], *refs[ins + count :])


def continued(kernel, before, in_specs, out_specs, out_shape, **rest):
    aliases = {}
    if before:
        count = len(before)
        kernel = functools.partial(placed, kernel, len(in_specs), count)
        aliases = {len(in_specs) + index: index for index in range(count)}
        in_specs = list(in_specs) + [pl.BlockSpec(memory_space=pl.ANY)] * count
    call = pl.pallas_call(
        kernel, in_specs=in_specs, out_specs=out_specs, out_shape=out_shape, input_output_aliases=aliases, **rest
    )
    return lambda *operands: call(*operands, *before)


def attend(queries, keys, values, sequence, before=()):
    rows = queries.shape[0]
    column = pl.BlockSpec((LEN, 128), lambda p: (sequence, p))
    return continued(
        attend_kernel,
        before,
        grid=(HEADS // 2,),
        in_specs=[column] * 3,
        out_specs=[pl.BlockSpec((1, 2, LEN, LEN), lambda p: (sequence, p, 0, 0)), column],
        out_shape=[
            jax.ShapeDtypeStruct((rows // LEN, HEADS, LEN, LEN), LOW),
            jax.ShapeDtypeStruct((rows, D), LOW),
        ],
        compiler_params=pltpu.CompilerParams(vmem_limit_bytes=32 * MIB),
        cost_estimate=pl.CostEstimate(
            flops=12 * HEADS * LEN * LEN * 256, bytes_accessed=HEADS * LEN * LEN * 2 + LEN * D * 8,
            transcendentals=HEADS * LEN * LEN),
        name="attend",
    )(queries, keys, values)


def attend_back_kernel(q_ref, k_ref, v_ref, probs_ref, grad_ref, dq_ref, dk_ref, dv_ref):
    scale = (D // HEADS) ** -0.5
    queries, keys, values, grads = q_ref[...], k_ref[...], v_ref[...], grad_ref[...]
    zero = jnp.zeros((), LOW)
    d_queries = jnp.zeros((LEN, 128), FULL)
    d_keys = jnp.zeros((128, LEN), FULL)
    d_values = jnp.zeros((128, LEN), FULL)
    for head in range(2):
        mask = head_mask(LEN, head)
        probs = probs_ref[0, head]
        own_grads = jnp.where(mask, grads, zero)
        d_probs = dot_nt(own_grads, values).astype(LOW).astype(FULL)
        wide = probs.astype(FULL)
        product = d_probs * wide
        total = jnp.sum(product, axis=-1, keepdims=True)
        d_scores = (product - wide * total).astype(LOW)
        d_queries = d_queries + dot_nn(d_scores, jnp.where(mask, keys, zero))
        d_keys = d_keys + dot_tn(jnp.where(mask, queries, zero), d_scores)
        d_values = d_values + dot_tn(own_grads, probs)
    dq_ref[...] = (scale * d_queries).astype(LOW)
    dk_ref[...] = (scale * d_keys.T).astype(LOW)
    dv_ref[...] = d_values.T.astype(LOW)


def attend_back(queries, keys, values, probs, grads, sequence, before=()):
    rows = queries.shape[0]
    column = pl.BlockSpec((LEN, 128), lambda p: (sequence, p))
    return continued(
        attend_back_kernel,
        before,
        grid=(HEADS // 2,),
        in_specs=[column, column, column, pl.BlockSpec((1, 2, LEN, LEN), lambda p: (sequence, p, 0, 0)), column],
        out_specs=[column] * 3,
        out_shape=[jax.ShapeDtypeStruct((rows, D), LOW)] * 3,
        compiler_params=pltpu.CompilerParams(vmem_limit_bytes=32 * MIB),
        cost_estimate=pl.CostEstimate(
            flops=12 * HEADS * LEN * LEN * 256, bytes_accessed=HEADS * LEN * LEN * 2 + LEN * D * 14, transcendentals=0),
        name="attend_back",
    )(queries, keys, values, probs, grads)


def gelu_both(point):
    bell = jnp.exp(point * point * -0.5)
    ratio = 1.0 / (1.0 + (0.3275911 * 0.5**0.5) * jnp.abs(point))
    series = 0.5 * 1.061405429
    for factor in (-1.453152027, 1.421413741, -0.284496736, 0.254829592):
        series = series * ratio + 0.5 * factor
    below = series * ratio * bell
    normal = jnp.where(point < 0, below, 1.0 - below)
    return point * normal, normal + point * bell * 0.3989422804014327


def norm_rows(summed):
    centered = summed - jnp.mean(summed, axis=-1, keepdims=True)
    inverse = lax.rsqrt(jnp.mean(centered * centered, axis=-1, keepdims=True) + EPS)
    return centered * inverse, inverse


def norm_back_rows(scaled, normed, inverse):
    mean_grad = jnp.mean(scaled, axis=-1, keepdims=True)
    mean_cross = jnp.mean(scaled * normed, axis=-1, keepdims=True)
    return inverse * (scaled - mean_grad - normed * mean_cross)


def strips(rows, body):
    def step(index, carry):
        body(pl.ds(pl.multiple_of(index * STRIP, STRIP), STRIP))
        return carry

    lax.fori_loop(0, rows // STRIP, step, 0)


def fixed(array):
    return pl.BlockSpec(array.shape, lambda *place: (0,) * array.ndim, pipeline_mode=pl.Buffered(1))


def held(rows, cols):
    return pl.BlockSpec((rows, cols), lambda *place: (0, 0), pipeline_mode=pl.Buffered(1))


def branch_kernel(attn_ref, tokens_ref, wout_ref, bout_ref, gain_ref, shift_ref, normed_ref, inverse_ref, low_ref):
    summed = tokens_ref[...].astype(FULL) + dot_nn(attn_ref[...], wout_ref[...]) + bout_ref[...]
    normed, inverse = norm_rows(summed)
    normed_ref[...] = normed
    inverse_ref[...] = inverse
    low_ref[...] = (normed * gain_ref[...] + shift_ref[...]).astype(LOW)


def branch(attn_rows, tokens, w_out, b_out, gain, shift):
    rows = tokens.shape[0]
    strip = lambda cols: pl.BlockSpec((STRIP, cols), lambda i: (i, 0))
    return pl.pallas_call(
        branch_kernel,
        grid=(rows // STRIP,),
        in_specs=[strip(D), strip(D), fixed(w_out), fixed(b_out), fixed(gain), fixed(shift)],
        out_specs=[strip(D), strip(1), strip(D)],
        out_shape=[
            jax.ShapeDtypeStruct((rows, D), FULL), jax.ShapeDtypeStruct((rows, 1), FULL),
            jax.ShapeDtypeStruct((rows, D), LOW),
        ],
        compiler_params=pltpu.CompilerParams(vmem_limit_bytes=32 * MIB),
        cost_estimate=pl.CostEstimate(flops=4 * rows * D * D, bytes_accessed=rows * D * 10 + D * D * 2, transcendentals=0),
        name="branch",
    )(attn_rows, tokens, w_out, b_out, gain, shift)


def widen_kernel(low_ref, wup_ref, bup_ref, hidden_ref, slope_ref):
    def strip(rows):
        point = dot_nn(low_ref[rows, :], wup_ref[...]) + bup_ref[...]
        hidden, slope = gelu_both(point)
        hidden_ref[rows, :] = hidden.astype(LOW)
        slope_ref[rows, :] = slope.astype(LOW)

    strips(low_ref.shape[0], strip)


def widen(first_low, w_up, b_up, first, last, before=()):
    rows, width = first_low.shape[0], w_up.shape[1]
    chunk = lambda height: pl.BlockSpec((height, WIDE), lambda i: (0, i + first))
    return continued(
        widen_kernel,
        before,
        grid=(last - first,),
        in_specs=[fixed(first_low), chunk(D), chunk(1)],
        out_specs=[chunk(rows), chunk(rows)],
        out_shape=[jax.ShapeDtypeStruct((rows, width), LOW)] * 2,
        compiler_params=pltpu.CompilerParams(vmem_limit_bytes=32 * MIB),
        cost_estimate=pl.CostEstimate(
            flops=6 * rows * D * WIDE * (last - first), bytes_accessed=WIDE * (last - first) * (D * 2 + rows * 4),
            transcendentals=rows * WIDE * (last - first)),
        name="widen",
    )(first_low, w_up, b_up)


def fall_kernel(hidden_ref, wdown_ref, normed_ref, cot_ref, bdown_ref, gain1_ref, shift1_ref, gain2_ref, shift2_ref,
                out_ref, second_ref, ffn_ref, sums_ref, total):
    step = pl.program_id(0)

    @pl.when(step == 0)
    def _():
        total[...] = dot_nn(hidden_ref[...], wdown_ref[...])

    @pl.when(step > 0)
    def _():
        total[...] += dot_nn(hidden_ref[...], wdown_ref[...])

    @pl.when(step == pl.num_programs(0) - 1)
    def _():
        sums_ref[...] = jnp.zeros_like(sums_ref)

        def finish(rows):
            first_out = normed_ref[rows, :] * gain1_ref[...] + shift1_ref[...]
            normed, inverse = norm_rows(first_out + total[rows, :] + bdown_ref[...])
            out_ref[rows, :] = (normed * gain2_ref[...] + shift2_ref[...]).astype(LOW)
            upstream = cot_ref[rows, :].astype(FULL)
            second = norm_back_rows(upstream * gain2_ref[...], normed, inverse)
            low = second.astype(LOW)
            second_ref[rows, :] = second
            ffn_ref[rows, :] = low
            sums_ref[...] += jnp.concatenate([
                jnp.sum(part, axis=0, keepdims=True) for part in (upstream * normed, upstream, low.astype(FULL))
            ], axis=0)

        strips(out_ref.shape[0], finish)


def fall(hidden, w_down, normed, cotangent, b_down, gain1, shift1, gain2, shift2, chunk=1024):
    rows, width = hidden.shape
    return pl.pallas_call(
        fall_kernel,
        grid=(width // chunk,),
        in_specs=[
            pl.BlockSpec((rows, chunk), lambda i: (0, i)), pl.BlockSpec((chunk, D), lambda i: (i, 0)),
        ] + [fixed(a) for a in (normed, cotangent, b_down, gain1, shift1, gain2, shift2)],
        out_specs=[held(rows, D), held(rows, D), held(rows, D), held(3, D)],
        out_shape=[
            jax.ShapeDtypeStruct((rows, D), LOW), jax.ShapeDtypeStruct((rows, D), FULL),
            jax.ShapeDtypeStruct((rows, D), LOW), jax.ShapeDtypeStruct((3, D), FULL),
        ],
        scratch_shapes=[pltpu.VMEM((rows, D), FULL)],
        compiler_params=pltpu.CompilerParams(vmem_limit_bytes=40 * MIB),
        cost_estimate=pl.CostEstimate(
            flops=2 * rows * D * width, bytes_accessed=rows * (D * 14 + width * 2) + D * width * 2, transcendentals=0),
        name="fall",
    )(hidden, w_down, normed, cotangent, b_down, gain1, shift1, gain2, shift2)


def narrow_kernel(ffn_ref, slope_ref, wdown_ref, wup_ref, so_far_ref, pre_ref, wide_ref, total_ref):
    @pl.when(pl.program_id(0) == 0)
    def _():
        total_ref[...] = so_far_ref[...]

    wide_ref[...] = jnp.zeros_like(wide_ref)

    def strip(rows):
        d_hidden = dot_nt(ffn_ref[rows, :], wdown_ref[...])
        d_pre = (slope_ref[rows, :].astype(FULL) * d_hidden).astype(LOW)
        pre_ref[rows, :] = d_pre
        wide_ref[...] += jnp.sum(d_pre.astype(FULL), axis=0, keepdims=True)
        total_ref[rows, :] += dot_nt(d_pre, wup_ref[...])

    strips(ffn_ref.shape[0], strip)


def narrow(d_ffn, slope, w_down, w_up, so_far, first, last, before=()):
    rows, width = slope.shape
    chunk = lambda height: pl.BlockSpec((height, WIDE), lambda i: (0, i + first))
    return continued(
        narrow_kernel,
        before,
        grid=(last - first,),
        in_specs=[
            fixed(d_ffn), chunk(rows), pl.BlockSpec((WIDE, D), lambda i: (i + first, 0)), chunk(D), fixed(so_far),
        ],
        out_specs=[chunk(rows), chunk(1), held(rows, D)],
        out_shape=[
            jax.ShapeDtypeStruct((rows, width), LOW), jax.ShapeDtypeStruct((1, width), FULL),
            jax.ShapeDtypeStruct((rows, D), FULL),
        ],
        compiler_params=pltpu.CompilerParams(vmem_limit_bytes=40 * MIB),
        cost_estimate=pl.CostEstimate(
            flops=6 * rows * D * WIDE * (last - first), bytes_accessed=WIDE * (last - first) * (D * 4 + rows * 4) + rows * D * 10,
            transcendentals=0),
        name="narrow",
    )(d_ffn, slope, w_down, w_up, so_far)


def resid_kernel(first_ref, normed_ref, inverse_ref, gain_ref, wout_ref, resid_ref, branch_ref, attn_ref, sums_ref):
    d_first, normed = first_ref[...], normed_ref[...]
    resid = norm_back_rows(d_first * gain_ref[...], normed, inverse_ref[...])
    low = resid.astype(LOW)
    resid_ref[...] = resid
    branch_ref[...] = low
    attn_ref[...] = dot_nt(low, wout_ref[...]).astype(LOW)
    sums = jnp.concatenate([
        jnp.sum(part, axis=0, keepdims=True) for part in (d_first * normed, d_first, low.astype(FULL))
    ], axis=0)

    @pl.when(pl.program_id(0) == 0)
    def _():
        sums_ref[...] = sums

    @pl.when(pl.program_id(0) > 0)
    def _():
        sums_ref[...] += sums


def resid_back(d_first, normed, inverse, gain, w_out):
    rows = d_first.shape[0]
    strip = lambda cols: pl.BlockSpec((STRIP, cols), lambda i: (i, 0))
    return pl.pallas_call(
        resid_kernel,
        grid=(rows // STRIP,),
        in_specs=[strip(D), strip(D), strip(1), fixed(gain), fixed(w_out)],
        out_specs=[strip(D), strip(D), strip(D), held(3, D)],
        out_shape=[
            jax.ShapeDtypeStruct((rows, D), FULL), jax.ShapeDtypeStruct((rows, D), LOW),
            jax.ShapeDtypeStruct((rows, D), LOW), jax.ShapeDtypeStruct((3, D), FULL),
        ],
        compiler_params=pltpu.CompilerParams(vmem_limit_bytes=32 * MIB),
        cost_estimate=pl.CostEstimate(flops=4 * rows * D * D, bytes_accessed=rows * D * 16 + D * D * 2, transcendentals=0),
        name="resid_back",
    )(d_first, normed, inverse, gain, w_out)


def tall_kernel(cut, left_ref, right_ref, keep1_ref, send1_ref, keep2_ref, send2_ref, product):
    core = lax.axis_index("dp") % 2
    product[...] = dot_tn(left_ref[...], right_ref[...]).astype(LOW).reshape(product.shape)
    for keep, send, low, high in ((keep1_ref, send1_ref, 0, cut), (keep2_ref, send2_ref, cut, product.shape[-1])):
        for pair in range(2):
            keep[pair] = product[pair, core, :, low:high]
            send[pair] = product[pair, 1 - core, :, low:high]


def outer_tall(left, right, cut, count):
    rows, width = left.shape
    cols, part = right.shape[1], width // count
    out = lambda size: pl.BlockSpec((2, part, size), lambda i: (i, 0, 0))
    shape = lambda size: jax.ShapeDtypeStruct((count // 2, part, size), LOW)
    sizes = (cut, cut, cols - cut, cols - cut)
    return pl.pallas_call(
        functools.partial(tall_kernel, cut),
        grid=(count // 4,),
        in_specs=[pl.BlockSpec((rows, 4 * part), lambda i: (0, i)), fixed(right)],
        out_specs=[out(size) for size in sizes],
        out_shape=[shape(size) for size in sizes],
        scratch_shapes=[pltpu.VMEM((2, 2, part, cols), LOW)],
        compiler_params=pltpu.CompilerParams(vmem_limit_bytes=32 * MIB),
        cost_estimate=pl.CostEstimate(
            flops=2 * rows * width * cols, bytes_accessed=2 * (rows * (width + cols) + width * cols), transcendentals=0),
        name="outer_tall",
    )(left, right)


def wide_kernel(starts, first, *refs):
    pairs = len(starts) - 1
    lefts, rights, outs, product = refs[:pairs], refs[pairs : 2 * pairs], refs[2 * pairs : -1], refs[-1]
    step = pl.program_id(0)
    core = lax.axis_index("dp") % 2
    for left, right, low, high in zip(lefts, rights, starts, starts[1:]):
        @pl.when((step >= low) & (step < high))
        def _():
            product[...] = dot_tn(left[...], right[...]).astype(LOW).reshape(product.shape)

    for keep, send, wanted in ((outs[0], outs[1], step < first), (outs[2], outs[3], step >= first)):
        @pl.when(wanted)
        def _():
            keep[...] = product[:, core]
            send[...] = product[:, 1 - core]


def outer_wide(lefts, rights, first, count):
    rows, height = lefts[0].shape
    part = height // count
    starts = [0]
    for right in rights:
        starts.append(starts[-1] + right.shape[1] // WIDE)
    total = starts[-1]

    def strip(low, high):
        return pl.BlockSpec((rows, WIDE), lambda i: (0, jnp.clip(i - low, 0, high - low - 1)))

    def out(low, high):
        return pl.BlockSpec((count // 2, part, WIDE), lambda i: (0, 0, jnp.clip(i - low, 0, high - low - 1)))

    ranges = ((0, first), (0, first), (first, total), (first, total))
    return pl.pallas_call(
        functools.partial(wide_kernel, starts, first),
        grid=(total,),
        in_specs=[fixed(left) for left in lefts] + [strip(low, high) for low, high in zip(starts, starts[1:])],
        out_specs=[out(low, high) for low, high in ranges],
        out_shape=[jax.ShapeDtypeStruct((count // 2, part, WIDE * (high - low)), LOW) for low, high in ranges],
        scratch_shapes=[pltpu.VMEM((count // 2, 2, part, WIDE), LOW)],
        compiler_params=pltpu.CompilerParams(vmem_limit_bytes=32 * MIB),
        cost_estimate=pl.CostEstimate(
            flops=2 * rows * height * WIDE * total,
            bytes_accessed=2 * (rows * (height * len(lefts) + WIDE * total) + height * WIDE * total), transcendentals=0),
        name="outer_wide",
    )(*lefts, *rights)


FLIPS = {"c": 1, "x": 2, "y": 4}
ORDERS = ("zyx", "xzy")


def ring_pairs(count):
    return [(place, (place + 8) % count) for place in range(count)]


def hop(array, dim, count):
    if dim == "z":
        return lax.ppermute(array, "dp", ring_pairs(count))
    return lax.ppermute(array, "dp", [(place, place ^ FLIPS[dim]) for place in range(count)])


def after(value, *earlier):
    return lax.optimization_barrier((value, earlier))[0]


def mine_of(count):
    me = lax.axis_index("dp")
    return {"z": lax.shift_right_logical(me, 3), "y": lax.shift_right_logical(me, 2) & 1,
            "x": lax.shift_right_logical(me, 1) & 1, "c": me & 1}


def gather_part(shard, order, count, marks):
    stack = after(shard, marks[-1])[None] if marks else shard[None]
    for dim in order[:2]:
        pieces = [stack]
        for _ in range(count // 8 - 1 if dim == "z" else 1):
            pieces.append(hop(pieces[-1], dim, count))
        stack = jnp.concatenate(pieces, axis=0)
        if dim == "z":
            marks.append(pieces[-1])
    across = hop(stack, order[2], count)
    return (stack, across, hop(stack, "c", count), hop(across, "c", count))


def place_kernel(count, cuts, bases, rows, *refs):
    pieces, outs, sem = refs[:8], refs[8:-1], refs[-1]
    ring = count // 8
    mine = mine_of(count)

    def owner(digits):
        z = lax.rem(mine["z"] + ring - digits["z"], ring)
        low = [1 - mine[dim] if digits[dim] else mine[dim] for dim in "yxc"]
        return z * 8 + low[0] * 4 + low[1] * 2 + low[2]

    for part, order in enumerate(ORDERS):
        left, right = cuts[part], cuts[part + 1]
        for which in range(4):
            for slot in range(count // 4):
                digits = {"c": which // 2, order[2]: which % 2}
                rest = slot
                for dim in order[:2]:
                    size = ring if dim == "z" else 2
                    digits[dim] = rest % size
                    rest = rest // size
                row = pl.ds(pl.multiple_of(owner(digits) * rows, rows), rows)
                for out, base, stop in zip(outs, bases, bases[1:]):
                    low, high = max(left, base), min(right, stop)
                    if low < high:
                        pltpu.make_async_copy(
                            pieces[4 * part + which].at[slot, :, pl.ds(low - left, high - low)],
                            out.at[row, pl.ds(low - base, high - low)],
                            sem,
                        ).start()
    for out in outs:
        pltpu.make_async_copy(out, out, sem).wait()


def gather(shard, widths, cut, count, marks):
    rows, total = shard.shape
    bases = [sum(widths[:index]) for index in range(len(widths) + 1)]
    if count != 32:
        full = lax.all_gather(shard, "dp", axis=0, tiled=True)
        return [full[:, low:high] for low, high in zip(bases, bases[1:])]
    cuts = (0, cut, total)
    pieces = []
    for order, low, high, own_marks in zip(ORDERS, cuts, cuts[1:], marks):
        pieces.extend(gather_part(shard[:, low:high], order, count, own_marks))
    return pl.pallas_call(
        functools.partial(place_kernel, count, cuts, bases, rows),
        in_specs=[pl.BlockSpec(memory_space=pl.ANY)] * 8,
        out_specs=[pl.BlockSpec(memory_space=pl.ANY)] * len(widths),
        out_shape=[jax.ShapeDtypeStruct((count * rows, width), LOW) for width in widths],
        scratch_shapes=[pltpu.SemaphoreType.DMA(())],
        cost_estimate=pl.CostEstimate(flops=0, bytes_accessed=4 * count * rows * total, transcendentals=0),
        name="place",
    )(*pieces)


def add_low(left_side, right_side, kind=LOW):
    return (left_side.astype(FULL) + right_side.astype(FULL)).astype(kind)


def take(blocks, axis, index):
    return lax.dynamic_index_in_dim(blocks, index, axis, keepdims=False, allow_negative_indices=False)


def scatter_steps(keep, send, order, count):
    ring = count // 8
    mine = mine_of(count)
    dims = ["z", "y", "x"]
    shape = (ring, 2, 2) + keep.shape[1:]
    yield send
    held = [keep.reshape(shape), hop(send, "c", count).reshape(shape)]

    def pick(dim, index):
        axis = dims.index(dim)
        return add_low(take(held[0], axis, index), take(held[1], axis, index))

    for dim in order[::-1]:
        own = mine[dim]
        if dim == "z":
            moving = pick("z", (own + ring - 1) & (ring - 1))
            for step in range(2, ring + 1):
                yield moving
                moving = hop(moving, "z", count)
                if step < ring:
                    moving = add_low(moving, pick("z", (own + ring - step) & (ring - 1)))
        else:
            moving = pick(dim, 1 - own)
            yield moving
            moving = hop(moving, dim, count)
        held = [pick(dim, own), moving]
        dims.remove(dim)
    yield add_low(held[0], held[1], FULL)


class Sums:
    def __init__(self, parts, count):
        self.chains = [scatter_steps(keep, send, order, count) for (keep, send), order in zip(parts, ORDERS)]
        self.last = [None] * len(parts)

    def move(self, which):
        self.last[which] = next(self.chains[which])
        return self.last[which]

    def result(self):
        for which, chain in enumerate(self.chains):
            for value in chain:
                self.last[which] = value
        return jnp.concatenate(self.last, axis=-1)


def local(
    tokens,
    w_query,
    w_key,
    w_value,
    w_out,
    w_up,
    w_down,
    b_query,
    b_value,
    b_out,
    b_up,
    b_down,
    gain_attn,
    shift_attn,
    gain_ffn,
    shift_ffn,
    cotangent,
):
    count = D // w_query.shape[0]
    part = D // count
    wide = w_up.shape[1]
    vectors = (b_query, b_value, b_out, b_down, gain_attn, shift_attn, gain_ffn, shift_ffn, b_up)
    packed = jnp.concatenate(vectors)
    packed = jnp.pad(packed, (0, part * 128 - packed.shape[0])).reshape(part, 128)
    marks = ([], [])
    w_query, w_key, w_value, packed = gather(
        jnp.concatenate([w_query, w_key, w_value, packed], axis=1), (D, D, D, 128), 2 * D, count, marks
    )
    w_up, w_out = gather(jnp.concatenate([w_up, w_out], axis=1), (wide, D), 3328, count, marks)
    (w_down,) = gather(w_down, (D,), 640, count, marks)
    flat = packed.reshape(count, part * 128)
    vector = lambda col: flat[:, part * col : part * col + part].reshape(1, D).astype(FULL)
    b_query, b_value, b_out, b_down, gain_attn, shift_attn, gain_ffn, shift_ffn = map(vector, range(8))
    b_up = flat[:, 8 * part : 8 * part + wide // count].reshape(1, wide).astype(FULL)
    chunks = wide // WIDE
    sequences = tokens.shape[0] // LEN

    queries = (dot_nn(tokens, w_query) + b_query).astype(LOW)
    keys = dot_nn(tokens, w_key).astype(LOW)
    values = (dot_nn(tokens, w_value) + b_value).astype(LOW)
    seen = ()
    for sequence in range(sequences):
        seen = attend(queries, keys, values, sequence, seen)
    probs, attn_rows = seen
    normed, inverse, first_low = branch(attn_rows, tokens, w_out, b_out, gain_attn, shift_attn)
    half = widen(first_low, w_up, b_up, 0, chunks // 2)
    hidden, slope = widen(first_low, w_up, b_up, chunks // 2, chunks, half)
    result, second, d_ffn, sums_ffn = fall(
        hidden, w_down, normed, cotangent, b_down, gain_attn, shift_attn, gain_ffn, shift_ffn
    )

    custom = count == 32
    down, up, first = None, None, None

    def then(value, *moves):
        if not custom:
            return value
        return after(value, *[sums.move(which) for sums, which in moves])

    if custom:
        parts = outer_tall(hidden, d_ffn, 640, count)
        down = Sums((parts[:2], parts[2:]), count)
    d_ffn = then(d_ffn, (down, 0), (down, 1))
    d_pre, d_b_up, d_first = narrow(d_ffn, slope, w_down, w_up, second, 0, 2)
    d_first = then(d_first, (down, 0), (down, 1))
    d_pre, d_b_up, d_first = narrow(d_ffn, slope, w_down, w_up, d_first, 2, 5, (d_pre, d_b_up, d_first)[:2])
    d_first = then(d_first, (down, 1))
    d_pre, d_b_up, d_first = narrow(d_ffn, slope, w_down, w_up, d_first, 5, chunks, (d_pre, d_b_up, d_first)[:2])
    d_resid, d_branch, d_attn, sums_attn = resid_back(d_first, normed, inverse, gain_attn, w_out)
    d_branch = then(d_branch, (down, 0), (down, 1))
    if custom:
        parts = outer_wide([first_low, attn_rows], [d_pre, d_branch], 6, count)
        up = Sums((parts[:2], parts[2:]), count)
    d_attn = then(d_attn, (down, 0), (down, 1), (up, 0), (up, 1))
    seen = attend_back(queries, keys, values, probs, d_attn, 0)
    d_attn = then(d_attn, (up, 0), (up, 1), (down, 0), (down, 1))
    for sequence in range(1, sequences):
        seen = attend_back(queries, keys, values, probs, d_attn, sequence, seen)
    d_queries, d_keys, d_values = seen
    d_queries = then(d_queries, (down, 0), (down, 1))
    column_sum = lambda rows: jnp.sum(rows.astype(FULL), axis=0)
    sums = (
        column_sum(d_queries), column_sum(d_values), sums_attn[2], sums_ffn[2],
        sums_attn[0], sums_attn[1], sums_ffn[0], sums_ffn[1], d_b_up[0],
    )
    packed = jnp.concatenate([total.astype(LOW).reshape(count, -1) for total in sums], axis=1)
    packed = jnp.pad(packed, ((0, 0), (0, part * 128 - packed.shape[1]))).reshape(count // 2, 2, part, 128)
    if custom:
        parts = outer_wide([tokens, tokens, tokens], [d_queries, d_keys, d_values], 4, count)
        send = jnp.concatenate([parts[3], take(packed, 1, 1 - mine_of(count)["c"])], axis=-1)
        keep = jnp.concatenate([parts[2], take(packed, 1, mine_of(count)["c"])], axis=-1)
        first = Sums((parts[:2], (keep, send)), count)
    d_queries = then(d_queries, (first, 0), (first, 1), (up, 1), (down, 0))
    grad_rows = d_resid + dot_nt(d_queries, w_query)
    d_keys = then(d_keys, (first, 0), (first, 1))
    grad_rows = grad_rows + dot_nt(d_keys, w_key)
    d_values = then(d_values, (up, 0), (up, 1))
    grad_rows = (grad_rows + dot_nt(d_values, w_value)).astype(LOW)

    if custom:
        d_w_down = down.result()
        second = up.result()
        first = first.result()
    else:
        total = lambda grad: lax.psum_scatter(grad.astype(LOW), "dp", scatter_dimension=0, tiled=True).astype(FULL)
        d_w_down = total(dot_tn(hidden, d_ffn))
        second = total(jnp.concatenate([dot_tn(first_low, d_pre), dot_tn(attn_rows, d_branch)], axis=1))
        first = [dot_tn(tokens, grad) for grad in (d_queries, d_keys, d_values)]
        first = total(jnp.concatenate(first + [packed.reshape(D, 128)], axis=1))
    flat = first[:, 3 * D :].reshape(-1)
    vector = lambda col: flat[part * col : part * col + part]
    return (
        result,
        grad_rows,
        first[:, :D],
        first[:, D : 2 * D],
        first[:, 2 * D : 3 * D],
        second[:, wide:],
        second[:, :wide],
        d_w_down,
        vector(0),
        vector(1),
        vector(2),
        flat[8 * part : 8 * part + wide // count],
        vector(3),
        vector(4),
        vector(5),
        vector(6),
        vector(7),
    )


def solution(mesh):
    placed = (
        P("dp", None),
        P("dp", None),
        P("dp", None),
        P("dp", None),
        P("dp", None),
        P("dp", None),
        P("dp", None),
        P("dp"),
        P("dp"),
        P("dp"),
        P("dp"),
        P("dp"),
        P("dp"),
        P("dp"),
        P("dp"),
        P("dp"),
        P("dp", None),
    )
    return jax.shard_map(
        local,
        mesh=mesh,
        in_specs=placed,
        out_specs=(
            P("dp", None),
            P("dp", None),
            P("dp", None),
            P("dp", None),
            P("dp", None),
            P("dp", None),
            P("dp", None),
            P("dp", None),
            P("dp"),
            P("dp"),
            P("dp"),
            P("dp"),
            P("dp"),
            P("dp"),
            P("dp"),
            P("dp"),
            P("dp"),
        ),
        check_vma=False,
    )
```

```python
import functools
import jax
import jax.numpy as jnp
from jax import lax
from jax.experimental import pallas as pl
from jax.experimental.pallas import tpu as pltpu
from jax.sharding import PartitionSpec as P

D = 1024
HEADS = 16
LEN = 512
EPS = 1e-12
LOW = jnp.bfloat16
FULL = jnp.float32
MIB = 1024 * 1024
WIDE = 512
STRIP = 256


def dot_nn(left_side, right_side):
    return lax.dot_general(left_side, right_side, (((1,), (0,)), ((), ())), preferred_element_type=FULL)


def dot_nt(left_side, right_side):
    return lax.dot_general(left_side, right_side, (((1,), (1,)), ((), ())), preferred_element_type=FULL)


def dot_tn(left_side, right_side):
    return lax.dot_general(left_side, right_side, (((0,), (0,)), ((), ())), preferred_element_type=FULL)


def head_mask(rows, head):
    lane = lax.broadcasted_iota(jnp.int32, (rows, 128), 1)
    return (lane // 64) == head


def attend_kernel(q_ref, k_ref, v_ref, probs_ref, rows_ref):
    scale = (D // HEADS) ** -0.5
    queries = (q_ref[...].astype(FULL) * scale).astype(LOW)
    keys, values = k_ref[...], v_ref[...]
    mixed = jnp.zeros((LEN, 128), FULL)
    for head in range(2):
        mask = head_mask(LEN, head)
        zero = jnp.zeros((), LOW)
        scores = dot_nt(queries, jnp.where(mask, keys, zero))
        maxima = jnp.max(scores, axis=-1, keepdims=True)
        exponent = jnp.exp(scores - maxima)
        total = jnp.sum(exponent, axis=-1, keepdims=True)
        probs = (exponent * (1.0 / total)).astype(LOW)
        probs_ref[0, head] = probs
        mixed = mixed + dot_nn(probs, jnp.where(mask, values, zero))
    rows_ref[...] = mixed.astype(LOW)


def placed(kernel, ins, count, *refs):
    kernel(*refs[:ins], *refs[ins + count :])


def continued(kernel, before, in_specs, out_specs, out_shape, **rest):
    aliases = {}
    if before:
        count = len(before)
        kernel = functools.partial(placed, kernel, len(in_specs), count)
        aliases = {len(in_specs) + index: index for index in range(count)}
        in_specs = list(in_specs) + [pl.BlockSpec(memory_space=pl.ANY)] * count
    call = pl.pallas_call(
        kernel, in_specs=in_specs, out_specs=out_specs, out_shape=out_shape, input_output_aliases=aliases, **rest
    )
    return lambda *operands: call(*operands, *before)


def attend(queries, keys, values, sequence, before=()):
    rows = queries.shape[0]
    column = pl.BlockSpec((LEN, 128), lambda p: (sequence, p))
    return continued(
        attend_kernel,
        before,
        grid=(HEADS // 2,),
        in_specs=[column] * 3,
        out_specs=[pl.BlockSpec((1, 2, LEN, LEN), lambda p: (sequence, p, 0, 0)), column],
        out_shape=[
            jax.ShapeDtypeStruct((rows // LEN, HEADS, LEN, LEN), LOW),
            jax.ShapeDtypeStruct((rows, D), LOW),
        ],
        compiler_params=pltpu.CompilerParams(vmem_limit_bytes=32 * MIB),
        cost_estimate=pl.CostEstimate(
            flops=12 * HEADS * LEN * LEN * 256, bytes_accessed=HEADS * LEN * LEN * 2 + LEN * D * 8,
            transcendentals=HEADS * LEN * LEN),
        name="attend",
    )(queries, keys, values)


def attend_back_kernel(q_ref, k_ref, v_ref, probs_ref, grad_ref, dq_ref, dk_ref, dv_ref):
    scale = (D // HEADS) ** -0.5
    queries, keys, values, grads = q_ref[...], k_ref[...], v_ref[...], grad_ref[...]
    zero = jnp.zeros((), LOW)
    d_queries = jnp.zeros((LEN, 128), FULL)
    d_keys = jnp.zeros((128, LEN), FULL)
    d_values = jnp.zeros((128, LEN), FULL)
    for head in range(2):
        mask = head_mask(LEN, head)
        probs = probs_ref[0, head]
        own_grads = jnp.where(mask, grads, zero)
        d_probs = dot_nt(own_grads, values).astype(LOW).astype(FULL)
        wide = probs.astype(FULL)
        product = d_probs * wide
        total = jnp.sum(product, axis=-1, keepdims=True)
        d_scores = (product - wide * total).astype(LOW)
        d_queries = d_queries + dot_nn(d_scores, jnp.where(mask, keys, zero))
        d_keys = d_keys + dot_tn(jnp.where(mask, queries, zero), d_scores)
        d_values = d_values + dot_tn(own_grads, probs)
    dq_ref[...] = (scale * d_queries).astype(LOW)
    dk_ref[...] = (scale * d_keys.T).astype(LOW)
    dv_ref[...] = d_values.T.astype(LOW)


def attend_back(queries, keys, values, probs, grads, sequence, before=()):
    rows = queries.shape[0]
    column = pl.BlockSpec((LEN, 128), lambda p: (sequence, p))
    return continued(
        attend_back_kernel,
        before,
        grid=(HEADS // 2,),
        in_specs=[column, column, column, pl.BlockSpec((1, 2, LEN, LEN), lambda p: (sequence, p, 0, 0)), column],
        out_specs=[column] * 3,
        out_shape=[jax.ShapeDtypeStruct((rows, D), LOW)] * 3,
        compiler_params=pltpu.CompilerParams(vmem_limit_bytes=32 * MIB),
        cost_estimate=pl.CostEstimate(
            flops=12 * HEADS * LEN * LEN * 256, bytes_accessed=HEADS * LEN * LEN * 2 + LEN * D * 14, transcendentals=0),
        name="attend_back",
    )(queries, keys, values, probs, grads)


def gelu_both(point):
    bell = jnp.exp(point * point * -0.5)
    ratio = 1.0 / (1.0 + (0.3275911 * 0.5**0.5) * jnp.abs(point))
    series = 0.5 * 1.061405429
    for factor in (-1.453152027, 1.421413741, -0.284496736, 0.254829592):
        series = series * ratio + 0.5 * factor
    below = series * ratio * bell
    normal = jnp.where(point < 0, below, 1.0 - below)
    return point * normal, normal + point * bell * 0.3989422804014327


def norm_rows(summed):
    centered = summed - jnp.mean(summed, axis=-1, keepdims=True)
    inverse = lax.rsqrt(jnp.mean(centered * centered, axis=-1, keepdims=True) + EPS)
    return centered * inverse, inverse


def norm_back_rows(scaled, normed, inverse):
    mean_grad = jnp.mean(scaled, axis=-1, keepdims=True)
    mean_cross = jnp.mean(scaled * normed, axis=-1, keepdims=True)
    return inverse * (scaled - mean_grad - normed * mean_cross)


def strips(rows, body):
    def step(index, carry):
        body(pl.ds(pl.multiple_of(index * STRIP, STRIP), STRIP))
        return carry

    lax.fori_loop(0, rows // STRIP, step, 0)


def fixed(array):
    return pl.BlockSpec(array.shape, lambda *place: (0,) * array.ndim, pipeline_mode=pl.Buffered(1))


def held(rows, cols):
    return pl.BlockSpec((rows, cols), lambda *place: (0, 0), pipeline_mode=pl.Buffered(1))


def branch_kernel(attn_ref, tokens_ref, wout_ref, bout_ref, gain_ref, shift_ref, normed_ref, inverse_ref, low_ref):
    summed = tokens_ref[...].astype(FULL) + dot_nn(attn_ref[...], wout_ref[...]) + bout_ref[...]
    normed, inverse = norm_rows(summed)
    normed_ref[...] = normed
    inverse_ref[...] = inverse
    low_ref[...] = (normed * gain_ref[...] + shift_ref[...]).astype(LOW)


def branch(attn_rows, tokens, w_out, b_out, gain, shift):
    rows = tokens.shape[0]
    strip = lambda cols: pl.BlockSpec((STRIP, cols), lambda i: (i, 0))
    return pl.pallas_call(
        branch_kernel,
        grid=(rows // STRIP,),
        in_specs=[strip(D), strip(D), fixed(w_out), fixed(b_out), fixed(gain), fixed(shift)],
        out_specs=[strip(D), strip(1), strip(D)],
        out_shape=[
            jax.ShapeDtypeStruct((rows, D), FULL), jax.ShapeDtypeStruct((rows, 1), FULL),
            jax.ShapeDtypeStruct((rows, D), LOW),
        ],
        compiler_params=pltpu.CompilerParams(vmem_limit_bytes=32 * MIB),
        cost_estimate=pl.CostEstimate(flops=4 * rows * D * D, bytes_accessed=rows * D * 10 + D * D * 2, transcendentals=0),
        name="branch",
    )(attn_rows, tokens, w_out, b_out, gain, shift)


def widen_kernel(low_ref, wup_ref, bup_ref, hidden_ref, slope_ref):
    def strip(rows):
        point = dot_nn(low_ref[rows, :], wup_ref[...]) + bup_ref[...]
        hidden, slope = gelu_both(point)
        hidden_ref[rows, :] = hidden.astype(LOW)
        slope_ref[rows, :] = slope.astype(LOW)

    strips(low_ref.shape[0], strip)


def widen(first_low, w_up, b_up, first, last, before=()):
    rows, width = first_low.shape[0], w_up.shape[1]
    chunk = lambda height: pl.BlockSpec((height, WIDE), lambda i: (0, i + first))
    return continued(
        widen_kernel,
        before,
        grid=(last - first,),
        in_specs=[fixed(first_low), chunk(D), chunk(1)],
        out_specs=[chunk(rows), chunk(rows)],
        out_shape=[jax.ShapeDtypeStruct((rows, width), LOW)] * 2,
        compiler_params=pltpu.CompilerParams(vmem_limit_bytes=32 * MIB),
        cost_estimate=pl.CostEstimate(
            flops=6 * rows * D * WIDE * (last - first), bytes_accessed=WIDE * (last - first) * (D * 2 + rows * 4),
            transcendentals=rows * WIDE * (last - first)),
        name="widen",
    )(first_low, w_up, b_up)


def fall_kernel(hidden_ref, wdown_ref, normed_ref, cot_ref, bdown_ref, gain1_ref, shift1_ref, gain2_ref, shift2_ref,
                out_ref, second_ref, ffn_ref, sums_ref, total):
    step = pl.program_id(0)

    @pl.when(step == 0)
    def _():
        total[...] = dot_nn(hidden_ref[...], wdown_ref[...])

    @pl.when(step > 0)
    def _():
        total[...] += dot_nn(hidden_ref[...], wdown_ref[...])

    @pl.when(step == pl.num_programs(0) - 1)
    def _():
        sums_ref[...] = jnp.zeros_like(sums_ref)

        def finish(rows):
            first_out = normed_ref[rows, :] * gain1_ref[...] + shift1_ref[...]
            normed, inverse = norm_rows(first_out + total[rows, :] + bdown_ref[...])
            out_ref[rows, :] = (normed * gain2_ref[...] + shift2_ref[...]).astype(LOW)
            upstream = cot_ref[rows, :].astype(FULL)
            second = norm_back_rows(upstream * gain2_ref[...], normed, inverse)
            low = second.astype(LOW)
            second_ref[rows, :] = second
            ffn_ref[rows, :] = low
            sums_ref[...] += jnp.concatenate([
                jnp.sum(part, axis=0, keepdims=True) for part in (upstream * normed, upstream, low.astype(FULL))
            ], axis=0)

        strips(out_ref.shape[0], finish)


def fall(hidden, w_down, normed, cotangent, b_down, gain1, shift1, gain2, shift2, chunk=1024):
    rows, width = hidden.shape
    return pl.pallas_call(
        fall_kernel,
        grid=(width // chunk,),
        in_specs=[
            pl.BlockSpec((rows, chunk), lambda i: (0, i)), pl.BlockSpec((chunk, D), lambda i: (i, 0)),
        ] + [fixed(a) for a in (normed, cotangent, b_down, gain1, shift1, gain2, shift2)],
        out_specs=[held(rows, D), held(rows, D), held(rows, D), held(3, D)],
        out_shape=[
            jax.ShapeDtypeStruct((rows, D), LOW), jax.ShapeDtypeStruct((rows, D), FULL),
            jax.ShapeDtypeStruct((rows, D), LOW), jax.ShapeDtypeStruct((3, D), FULL),
        ],
        scratch_shapes=[pltpu.VMEM((rows, D), FULL)],
        compiler_params=pltpu.CompilerParams(vmem_limit_bytes=40 * MIB),
        cost_estimate=pl.CostEstimate(
            flops=2 * rows * D * width, bytes_accessed=rows * (D * 14 + width * 2) + D * width * 2, transcendentals=0),
        name="fall",
    )(hidden, w_down, normed, cotangent, b_down, gain1, shift1, gain2, shift2)


def narrow_kernel(ffn_ref, slope_ref, wdown_ref, wup_ref, so_far_ref, pre_ref, wide_ref, total_ref):
    @pl.when(pl.program_id(0) == 0)
    def _():
        total_ref[...] = so_far_ref[...]

    wide_ref[...] = jnp.zeros_like(wide_ref)

    def strip(rows):
        d_hidden = dot_nt(ffn_ref[rows, :], wdown_ref[...])
        d_pre = (slope_ref[rows, :].astype(FULL) * d_hidden).astype(LOW)
        pre_ref[rows, :] = d_pre
        wide_ref[...] += jnp.sum(d_pre.astype(FULL), axis=0, keepdims=True)
        total_ref[rows, :] += dot_nt(d_pre, wup_ref[...])

    strips(ffn_ref.shape[0], strip)


def narrow(d_ffn, slope, w_down, w_up, so_far, first, last):
    rows, width = slope.shape[0], WIDE * (last - first)
    own = lambda height: pl.BlockSpec((height, WIDE), lambda i: (0, i))
    chunk = lambda height: pl.BlockSpec((height, WIDE), lambda i: (0, i + first))
    return pl.pallas_call(
        narrow_kernel,
        grid=(last - first,),
        in_specs=[
            fixed(d_ffn), chunk(rows), pl.BlockSpec((WIDE, D), lambda i: (i + first, 0)), chunk(D), fixed(so_far),
        ],
        out_specs=[own(rows), own(1), held(rows, D)],
        out_shape=[
            jax.ShapeDtypeStruct((rows, width), LOW), jax.ShapeDtypeStruct((1, width), FULL),
            jax.ShapeDtypeStruct((rows, D), FULL),
        ],
        compiler_params=pltpu.CompilerParams(vmem_limit_bytes=40 * MIB),
        cost_estimate=pl.CostEstimate(
            flops=6 * rows * D * WIDE * (last - first), bytes_accessed=WIDE * (last - first) * (D * 4 + rows * 4) + rows * D * 10,
            transcendentals=0),
        name="narrow",
    )(d_ffn, slope, w_down, w_up, so_far)


def resid_kernel(first_ref, normed_ref, inverse_ref, gain_ref, wout_ref, resid_ref, branch_ref, attn_ref, sums_ref):
    d_first, normed = first_ref[...], normed_ref[...]
    resid = norm_back_rows(d_first * gain_ref[...], normed, inverse_ref[...])
    low = resid.astype(LOW)
    resid_ref[...] = resid
    branch_ref[...] = low
    attn_ref[...] = dot_nt(low, wout_ref[...]).astype(LOW)
    sums = jnp.concatenate([
        jnp.sum(part, axis=0, keepdims=True) for part in (d_first * normed, d_first, low.astype(FULL))
    ], axis=0)

    @pl.when(pl.program_id(0) == 0)
    def _():
        sums_ref[...] = sums

    @pl.when(pl.program_id(0) > 0)
    def _():
        sums_ref[...] += sums


def resid_back(d_first, normed, inverse, gain, w_out):
    rows = d_first.shape[0]
    strip = lambda cols: pl.BlockSpec((STRIP, cols), lambda i: (i, 0))
    return pl.pallas_call(
        resid_kernel,
        grid=(rows // STRIP,),
        in_specs=[strip(D), strip(D), strip(1), fixed(gain), fixed(w_out)],
        out_specs=[strip(D), strip(D), strip(D), held(3, D)],
        out_shape=[
            jax.ShapeDtypeStruct((rows, D), FULL), jax.ShapeDtypeStruct((rows, D), LOW),
            jax.ShapeDtypeStruct((rows, D), LOW), jax.ShapeDtypeStruct((3, D), FULL),
        ],
        compiler_params=pltpu.CompilerParams(vmem_limit_bytes=32 * MIB),
        cost_estimate=pl.CostEstimate(flops=4 * rows * D * D, bytes_accessed=rows * D * 16 + D * D * 2, transcendentals=0),
        name="resid_back",
    )(d_first, normed, inverse, gain, w_out)


def tall_kernel(cut, left_ref, right_ref, keep1_ref, send1_ref, keep2_ref, send2_ref, product):
    core = lax.axis_index("dp") % 2
    product[...] = dot_tn(left_ref[...], right_ref[...]).astype(LOW).reshape(product.shape)
    for keep, send, low, high in ((keep1_ref, send1_ref, 0, cut), (keep2_ref, send2_ref, cut, product.shape[-1])):
        for pair in range(2):
            keep[pair] = product[pair, core, :, low:high]
            send[pair] = product[pair, 1 - core, :, low:high]


def outer_tall(left, right, cut, count):
    rows, width = left.shape
    cols, part = right.shape[1], width // count
    out = lambda size: pl.BlockSpec((2, part, size), lambda i: (i, 0, 0))
    shape = lambda size: jax.ShapeDtypeStruct((count // 2, part, size), LOW)
    sizes = (cut, cut, cols - cut, cols - cut)
    return pl.pallas_call(
        functools.partial(tall_kernel, cut),
        grid=(count // 4,),
        in_specs=[pl.BlockSpec((rows, 4 * part), lambda i: (0, i)), fixed(right)],
        out_specs=[out(size) for size in sizes],
        out_shape=[shape(size) for size in sizes],
        scratch_shapes=[pltpu.VMEM((2, 2, part, cols), LOW)],
        compiler_params=pltpu.CompilerParams(vmem_limit_bytes=32 * MIB),
        cost_estimate=pl.CostEstimate(
            flops=2 * rows * width * cols, bytes_accessed=2 * (rows * (width + cols) + width * cols), transcendentals=0),
        name="outer_tall",
    )(left, right)


def wide_kernel(starts, cuts, *refs):
    pairs = len(starts) - 1
    lefts, rights, outs, product = refs[:pairs], refs[pairs : 2 * pairs], refs[2 * pairs : -1], refs[-1]
    step = pl.program_id(0)
    core = lax.axis_index("dp") % 2
    for left, right, low, high in zip(lefts, rights, starts, starts[1:]):
        @pl.when((step >= low) & (step < high))
        def _():
            product[...] = dot_tn(left[...], right[...]).astype(LOW).reshape(product.shape)

    for keep, send, low, high in zip(outs[::2], outs[1::2], cuts, cuts[1:]):
        @pl.when((step >= low) & (step < high))
        def _():
            keep[...] = product[:, core]
            send[...] = product[:, 1 - core]


def outer_wide(lefts, rights, cuts, count):
    rows, height = lefts[0].shape
    part = height // count
    starts = [0]
    for right in rights:
        starts.append(starts[-1] + right.shape[1] // WIDE)
    total = starts[-1]

    def strip(low, high):
        return pl.BlockSpec((rows, WIDE), lambda i: (0, jnp.clip(i - low, 0, high - low - 1)))

    def out(low, high):
        return pl.BlockSpec((count // 2, part, WIDE), lambda i: (0, 0, jnp.clip(i - low, 0, high - low - 1)))

    ranges = [part_range for part_range in zip(cuts, cuts[1:]) for _ in range(2)]
    return pl.pallas_call(
        functools.partial(wide_kernel, starts, cuts),
        grid=(total,),
        in_specs=[fixed(left) for left in lefts] + [strip(low, high) for low, high in zip(starts, starts[1:])],
        out_specs=[out(low, high) for low, high in ranges],
        out_shape=[jax.ShapeDtypeStruct((count // 2, part, WIDE * (high - low)), LOW) for low, high in ranges],
        scratch_shapes=[pltpu.VMEM((count // 2, 2, part, WIDE), LOW)],
        compiler_params=pltpu.CompilerParams(vmem_limit_bytes=32 * MIB),
        cost_estimate=pl.CostEstimate(
            flops=2 * rows * height * WIDE * total,
            bytes_accessed=2 * (rows * (height * len(lefts) + WIDE * total) + height * WIDE * total), transcendentals=0),
        name="outer_wide",
    )(*lefts, *rights)


FLIPS = {"c": 1, "x": 2, "y": 4}
TWO_WAYS = ("zyx", "xzy")
EARLY_WAYS = ("zyx", "xzy", "yzx")
THREE_WAYS = ("zyx", "xzy", "yxz")


def ring_pairs(count):
    return [(place, (place + 8) % count) for place in range(count)]


def hop(array, dim, count):
    if dim == "z":
        return lax.ppermute(array, "dp", ring_pairs(count))
    return lax.ppermute(array, "dp", [(place, place ^ FLIPS[dim]) for place in range(count)])


def after(value, *earlier):
    return lax.optimization_barrier((value, earlier))[0] if earlier else value


def mine_of():
    me = lax.axis_index("dp")
    return {
        "z": lax.shift_right_logical(me, 3),
        "y": lax.shift_right_logical(me, 2) & 1,
        "x": lax.shift_right_logical(me, 1) & 1,
        "c": me & 1,
    }


def gather_part(shard, order, count, first=(), second=(), third=()):
    stack = shard[None]
    mark = None
    for dim, earlier in zip(order[:2], (first, second)):
        stack = after(stack, *earlier)
        pieces = [stack]
        for _ in range(count // 8 - 1 if dim == "z" else 1):
            pieces.append(hop(pieces[-1], dim, count))
        stack = jnp.concatenate(pieces, axis=0)
        if dim == "z":
            mark = pieces[-1]
    across = hop(after(stack, *third), order[2], count)
    return (stack, across, hop(stack, "c", count), hop(across, "c", count)), mark


def place_kernel(count, orders, cuts, bases, rows, *refs):
    pieces, outs = refs[: 4 * len(orders)], refs[4 * len(orders) :]
    ring = count // 8
    mine = mine_of()
    slot = pl.program_id(0)
    for part, order in enumerate(orders):
        left, right = cuts[part], cuts[part + 1]
        for which in range(4):
            digits = {"c": which // 2, order[2]: which % 2}
            rest = slot
            for dim in order[:2]:
                size = ring if dim == "z" else 2
                digits[dim] = lax.rem(rest, size)
                rest = lax.div(rest, size)
            owner = lax.rem(mine["z"] + ring - digits["z"], ring) * 8
            for dim, weight in (("y", 4), ("x", 2), ("c", 1)):
                owner = owner + weight * (mine[dim] ^ digits[dim])
            row = pl.ds(pl.multiple_of(owner * rows, rows), rows)
            for out, base, stop in zip(outs, bases, bases[1:]):
                low, high = max(left, base), min(right, stop)
                if low < high:
                    out[row, low - base : high - base] = pieces[4 * part + which][0, :, low - left : high - left]


def place(pieces, orders, cuts, widths, rows, count):
    bases = [sum(widths[:index]) for index in range(len(widths) + 1)]
    size = count * rows
    return pl.pallas_call(
        functools.partial(place_kernel, count, orders, cuts, bases, rows),
        grid=(count // 4,),
        in_specs=[pl.BlockSpec((1, rows, piece.shape[2]), lambda i: (i, 0, 0)) for piece in pieces],
        out_specs=[held(size, width) for width in widths],
        out_shape=[jax.ShapeDtypeStruct((size, width), LOW) for width in widths],
        compiler_params=pltpu.CompilerParams(vmem_limit_bytes=32 * MIB),
        cost_estimate=pl.CostEstimate(flops=0, bytes_accessed=4 * size * bases[-1], transcendentals=0),
        name="place",
    )(*pieces)


def whole_arrays(shard, widths):
    full = lax.all_gather(shard, "dp", axis=0, tiled=True)
    bases = [sum(widths[:index]) for index in range(len(widths) + 1)]
    return [full[:, low:high] for low, high in zip(bases, bases[1:])]


def gather_all(first, second, third, wide, count):
    first_widths, second_widths, third_widths = (D, D, D, 128), (wide, D), (D,)
    if count != 32:
        return whole_arrays(first, first_widths) + whole_arrays(second, second_widths) + whole_arrays(third, third_widths)

    def pieces_of(shard, cuts, orders, ties):
        pieces, marks = [], []
        for order, low, high, tie in zip(orders, cuts, cuts[1:], ties):
            four, mark = gather_part(shard[:, low:high], order, count, *tie)
            pieces.append(four)
            marks.append(mark)
        return pieces, marks

    cuts = (0, D, 2 * D, 3 * D + 128)
    early, marks = pieces_of(first, cuts, EARLY_WAYS, [()] * 3)
    placed_first = place(sum(early, ()), EARLY_WAYS, cuts, first_widths, first.shape[0], count)
    cuts = (0, 3328, wide + D)
    ties = [((marks[0],), (early[0][1],)), ((marks[1],), (), (early[1][1],))]
    pieces, _ = pieces_of(second, cuts, TWO_WAYS, ties)
    placed_second = place(sum(pieces, ()), TWO_WAYS, cuts, second_widths, second.shape[0], count)
    cuts = (0, 640, D)
    ties = [((placed_first[0],),), ((placed_first[0],),)]
    pieces, _ = pieces_of(third, cuts, TWO_WAYS, ties)
    placed_third = place(sum(pieces, ()), TWO_WAYS, cuts, third_widths, third.shape[0], count)
    return list(placed_first) + list(placed_second) + list(placed_third)


def add_low(left_side, right_side, kind=LOW):
    return (left_side.astype(FULL) + right_side.astype(FULL)).astype(kind)


def take(blocks, axis, index):
    return lax.dynamic_index_in_dim(blocks, index, axis, keepdims=False, allow_negative_indices=False)


def scatter_steps(keep, send, order, count):
    ring = count // 8
    mine = mine_of()
    dims = ["z", "y", "x"]
    shape = (ring, 2, 2) + keep.shape[1:]

    def hopped(array, dim, gate):
        return after(hop(array, dim, count), *gate)

    gate = yield send
    held_sums = [keep.reshape(shape), hopped(send, "c", gate).reshape(shape)]

    def pick(dim, index):
        axis = dims.index(dim)
        return add_low(take(held_sums[0], axis, index), take(held_sums[1], axis, index))

    for dim in order[::-1]:
        own = mine[dim]
        if dim == "z":
            moving = pick("z", (own + ring - 1) & (ring - 1))
            for step in range(2, ring + 1):
                gate = yield moving
                moving = hopped(moving, "z", gate)
                if step < ring:
                    moving = add_low(moving, pick("z", (own + ring - step) & (ring - 1)))
        else:
            moving = pick(dim, 1 - own)
            gate = yield moving
            moving = hopped(moving, dim, gate)
        held_sums = [pick(dim, own), moving]
        dims.remove(dim)
    yield add_low(held_sums[0], held_sums[1], FULL)


class Sums:
    def __init__(self, parts, orders, count):
        pairs = zip(parts[::2], parts[1::2])
        self.chains = [scatter_steps(keep, send, order, count) for (keep, send), order in zip(pairs, orders)]
        self.last = [next(chain) for chain in self.chains]

    def move(self, which, *gate):
        self.last[which] = self.chains[which].send(gate)
        return self.last[which]

    def results(self):
        for which, chain in enumerate(self.chains):
            while self.last[which].dtype != FULL:
                self.move(which)
        return self.last


def local(
    tokens,
    w_query,
    w_key,
    w_value,
    w_out,
    w_up,
    w_down,
    b_query,
    b_value,
    b_out,
    b_up,
    b_down,
    gain_attn,
    shift_attn,
    gain_ffn,
    shift_ffn,
    cotangent,
):
    count = D // w_query.shape[0]
    part = D // count
    wide = w_up.shape[1]
    vectors = (b_query, b_value, b_out, b_down, gain_attn, shift_attn, gain_ffn, shift_ffn, b_up)
    packed = jnp.concatenate(vectors)
    packed = jnp.pad(packed, (0, part * 128 - packed.shape[0])).reshape(part, 128)
    w_query, w_key, w_value, packed, w_up, w_out, w_down = gather_all(
        jnp.concatenate([w_query, w_key, w_value, packed], axis=1),
        jnp.concatenate([w_up, w_out], axis=1),
        w_down,
        wide,
        count,
    )
    flat = packed.reshape(count, part * 128)
    vector = lambda col: flat[:, part * col : part * col + part].reshape(1, D).astype(FULL)
    b_query, b_value, b_out, b_down, gain_attn, shift_attn, gain_ffn, shift_ffn = map(vector, range(8))
    b_up = flat[:, 8 * part : 8 * part + wide // count].reshape(1, wide).astype(FULL)
    chunks = wide // WIDE
    sequences = tokens.shape[0] // LEN

    queries = (dot_nn(tokens, w_query) + b_query).astype(LOW)
    keys = dot_nn(tokens, w_key).astype(LOW)
    values = (dot_nn(tokens, w_value) + b_value).astype(LOW)
    seen = ()
    for sequence in range(sequences):
        seen = attend(queries, keys, values, sequence, seen)
    probs, attn_rows = seen
    normed, inverse, first_low = branch(attn_rows, tokens, w_out, b_out, gain_attn, shift_attn)
    half = widen(first_low, w_up, b_up, 0, chunks // 2)
    hidden, slope = widen(first_low, w_up, b_up, chunks // 2, chunks, half)
    result, second, d_ffn, sums_ffn = fall(
        hidden, w_down, normed, cotangent, b_down, gain_attn, shift_attn, gain_ffn, shift_ffn
    )

    custom = count == 32

    def then(value, gate, *moves):
        if not custom:
            return value
        return after(value, *[sums.move(which, gate) for sums, which in moves])

    if custom:
        down = Sums(outer_tall(hidden, d_ffn, 640, count), TWO_WAYS, count)
        second = after(second, *down.last)
    pre_1, wide_1, d_first = narrow(d_ffn, slope, w_down, w_up, second, 0, 2)
    d_first = then(d_first, wide_1, (down, 0), (down, 1)) if custom else d_first
    pre_2, wide_2, d_first = narrow(d_ffn, slope, w_down, w_up, d_first, 2, 5)
    if custom:
        parts = outer_wide([first_low, first_low], [pre_1, pre_2], (0, 3, 5), count)
        up_1 = Sums(parts, TWO_WAYS, count)
        d_first = after(then(d_first, parts[2], (down, 1)), *up_1.last)
    pre_3, wide_3, d_first = narrow(d_ffn, slope, w_down, w_up, d_first, 5, chunks)
    if custom:
        d_first = then(d_first, wide_3, (down, 0), (down, 1), (up_1, 0), (up_1, 1))
    d_resid, d_branch, d_attn, sums_attn = resid_back(d_first, normed, inverse, gain_attn, w_out)
    if custom:
        d_branch = then(d_branch, sums_attn, (down, 1))
        parts = outer_wide([first_low, attn_rows], [pre_3, d_branch], (0, 3, 5), count)
        up_2 = Sums(parts, TWO_WAYS, count)
        d_attn = after(then(d_attn, parts[2], (down, 0), (down, 1)), *up_2.last)
    seen = attend_back(queries, keys, values, probs, d_attn, 0)
    if custom:
        d_attn = then(
            d_attn, seen[0], (down, 0), (down, 1), (up_1, 0), (up_1, 1), (up_2, 0), (up_2, 1)
        )
    for sequence in range(1, sequences):
        seen = attend_back(queries, keys, values, probs, d_attn, sequence, seen)
    d_queries, d_keys, d_values = seen
    if custom:
        d_queries = then(d_queries, d_values, (down, 0), (up_1, 0), (up_1, 1), (up_2, 1))
    column_sum = lambda rows: jnp.sum(rows.astype(FULL), axis=0)
    sums = (
        column_sum(d_queries), column_sum(d_values), sums_attn[2], sums_ffn[2],
        sums_attn[0], sums_attn[1], sums_ffn[0], sums_ffn[1],
        jnp.concatenate([wide_1[0], wide_2[0], wide_3[0]]),
    )
    packed = jnp.concatenate([total.astype(LOW).reshape(count, -1) for total in sums], axis=1)
    packed = jnp.pad(packed, ((0, 0), (0, part * 128 - packed.shape[1]))).reshape(count // 2, 2, part, 128)
    if custom:
        parts = outer_wide([tokens, tokens, tokens], [d_queries, d_keys, d_values], (0, 2, 4, 6), count)
        core = mine_of()["c"]
        keep = jnp.concatenate([parts[4], take(packed, 1, core)], axis=-1)
        send = jnp.concatenate([parts[5], take(packed, 1, 1 - core)], axis=-1)
        first = Sums(list(parts[:4]) + [keep, send], THREE_WAYS, count)
        d_queries = after(d_queries, *first.last)
        d_queries = then(d_queries, parts[0], (down, 0), (up_1, 0), (up_1, 1), (up_2, 0), (up_2, 1))
    grad_rows = d_resid + dot_nt(d_queries, w_query)
    if custom:
        grad_rows = then(grad_rows, grad_rows, (first, 0), (first, 1), (first, 2))
    grad_rows = grad_rows + dot_nt(d_keys, w_key) + dot_nt(d_values, w_value)

    if custom:
        grad_rows = grad_rows.astype(LOW)
        d_w_down = jnp.concatenate(down.results(), axis=-1)
        d_w_up = jnp.concatenate(up_1.results() + up_2.results()[:1], axis=-1)
        d_w_out = up_2.results()[1]
        d_w_query, d_w_key, last = first.results()
        d_w_value, flat = last[:, :D], last[:, D:].reshape(-1)
    else:
        total = lambda grad: lax.psum_scatter(grad.astype(LOW), "dp", scatter_dimension=0, tiled=True).astype(FULL)
        grad_rows = grad_rows.astype(LOW)
        d_w_down = total(dot_tn(hidden, d_ffn))
        d_w_up = total(jnp.concatenate([dot_tn(first_low, pre) for pre in (pre_1, pre_2, pre_3)], axis=1))
        d_w_out = total(dot_tn(attn_rows, d_branch))
        d_w_query, d_w_key, d_w_value = [total(dot_tn(tokens, grad)) for grad in (d_queries, d_keys, d_values)]
        flat = total(packed.reshape(D, 128)).reshape(-1)
    vector = lambda col: flat[part * col : part * col + part]
    return (
        result,
        grad_rows,
        d_w_query,
        d_w_key,
        d_w_value,
        d_w_out,
        d_w_up,
        d_w_down,
        vector(0),
        vector(1),
        vector(2),
        flat[8 * part : 8 * part + wide // count],
        vector(3),
        vector(4),
        vector(5),
        vector(6),
        vector(7),
    )


def solution(mesh):
    placed = (
        P("dp", None),
        P("dp", None),
        P("dp", None),
        P("dp", None),
        P("dp", None),
        P("dp", None),
        P("dp", None),
        P("dp"),
        P("dp"),
        P("dp"),
        P("dp"),
        P("dp"),
        P("dp"),
        P("dp"),
        P("dp"),
        P("dp"),
        P("dp", None),
    )
    return jax.shard_map(
        local,
        mesh=mesh,
        in_specs=placed,
        out_specs=(
            P("dp", None),
            P("dp", None),
            P("dp", None),
            P("dp", None),
            P("dp", None),
            P("dp", None),
            P("dp", None),
            P("dp", None),
            P("dp"),
            P("dp"),
            P("dp"),
            P("dp"),
            P("dp"),
            P("dp"),
            P("dp"),
            P("dp"),
            P("dp"),
        ),
        check_vma=False,
    )
```

```python
import functools
import jax
import jax.numpy as jnp
from jax import lax
from jax.experimental import pallas as pl
from jax.experimental.pallas import tpu as pltpu
from jax.sharding import PartitionSpec as P

D = 1024
HEADS = 16
LEN = 512
EPS = 1e-12
LOW = jnp.bfloat16
FULL = jnp.float32
MIB = 1024 * 1024
WIDE = 512
STRIP = 256


def dot_nn(left_side, right_side):
    return lax.dot_general(left_side, right_side, (((1,), (0,)), ((), ())), preferred_element_type=FULL)


def dot_nt(left_side, right_side):
    return lax.dot_general(left_side, right_side, (((1,), (1,)), ((), ())), preferred_element_type=FULL)


def dot_tn(left_side, right_side):
    return lax.dot_general(left_side, right_side, (((0,), (0,)), ((), ())), preferred_element_type=FULL)


def head_mask(rows, head):
    lane = lax.broadcasted_iota(jnp.int32, (rows, 128), 1)
    return (lane // 64) == head


def attend_kernel(q_ref, k_ref, v_ref, probs_ref, rows_ref):
    scale = (D // HEADS) ** -0.5
    queries = (q_ref[...].astype(FULL) * scale).astype(LOW)
    keys, values = k_ref[...], v_ref[...]
    mixed = jnp.zeros((LEN, 128), FULL)
    for head in range(2):
        mask = head_mask(LEN, head)
        zero = jnp.zeros((), LOW)
        scores = dot_nt(queries, jnp.where(mask, keys, zero))
        maxima = jnp.max(scores, axis=-1, keepdims=True)
        exponent = jnp.exp(scores - maxima)
        total = jnp.sum(exponent, axis=-1, keepdims=True)
        probs = (exponent * (1.0 / total)).astype(LOW)
        probs_ref[0, head] = probs
        mixed = mixed + dot_nn(probs, jnp.where(mask, values, zero))
    rows_ref[...] = mixed.astype(LOW)


def placed(kernel, ins, count, *refs):
    kernel(*refs[:ins], *refs[ins + count :])


def continued(kernel, before, in_specs, out_specs, out_shape, **rest):
    aliases = {}
    if before:
        count = len(before)
        kernel = functools.partial(placed, kernel, len(in_specs), count)
        aliases = {len(in_specs) + index: index for index in range(count)}
        in_specs = list(in_specs) + [pl.BlockSpec(memory_space=pl.ANY)] * count
    call = pl.pallas_call(
        kernel, in_specs=in_specs, out_specs=out_specs, out_shape=out_shape, input_output_aliases=aliases, **rest
    )
    return lambda *operands: call(*operands, *before)


def attend(queries, keys, values, sequence, before=()):
    rows = queries.shape[0]
    column = pl.BlockSpec((LEN, 128), lambda p: (sequence, p))
    return continued(
        attend_kernel,
        before,
        grid=(HEADS // 2,),
        in_specs=[column] * 3,
        out_specs=[pl.BlockSpec((1, 2, LEN, LEN), lambda p: (sequence, p, 0, 0)), column],
        out_shape=[
            jax.ShapeDtypeStruct((rows // LEN, HEADS, LEN, LEN), LOW),
            jax.ShapeDtypeStruct((rows, D), LOW),
        ],
        compiler_params=pltpu.CompilerParams(vmem_limit_bytes=GRANT),
        cost_estimate=pl.CostEstimate(
            flops=12 * HEADS * LEN * LEN * 256, bytes_accessed=HEADS * LEN * LEN * 2 + LEN * D * 8,
            transcendentals=HEADS * LEN * LEN),
        name="attend",
    )(queries, keys, values)


def attend_back_kernel(q_ref, k_ref, v_ref, probs_ref, grad_ref, dq_ref, dk_ref, dv_ref):
    scale = (D // HEADS) ** -0.5
    queries, keys, values, grads = q_ref[...], k_ref[...], v_ref[...], grad_ref[...]
    zero = jnp.zeros((), LOW)
    d_queries = jnp.zeros((LEN, 128), FULL)
    d_keys = jnp.zeros((128, LEN), FULL)
    d_values = jnp.zeros((128, LEN), FULL)
    for head in range(2):
        mask = head_mask(LEN, head)
        probs = probs_ref[0, head]
        own_grads = jnp.where(mask, grads, zero)
        d_probs = dot_nt(own_grads, values).astype(LOW).astype(FULL)
        wide = probs.astype(FULL)
        product = d_probs * wide
        total = jnp.sum(product, axis=-1, keepdims=True)
        d_scores = (product - wide * total).astype(LOW)
        d_queries = d_queries + dot_nn(d_scores, jnp.where(mask, keys, zero))
        d_keys = d_keys + dot_tn(jnp.where(mask, queries, zero), d_scores)
        d_values = d_values + dot_tn(own_grads, probs)
    dq_ref[...] = (scale * d_queries).astype(LOW)
    dk_ref[...] = (scale * d_keys.T).astype(LOW)
    dv_ref[...] = d_values.T.astype(LOW)


def attend_back(queries, keys, values, probs, grads, sequence, before=()):
    rows = queries.shape[0]
    column = pl.BlockSpec((LEN, 128), lambda p: (sequence, p))
    return continued(
        attend_back_kernel,
        before,
        grid=(HEADS // 2,),
        in_specs=[column, column, column, pl.BlockSpec((1, 2, LEN, LEN), lambda p: (sequence, p, 0, 0)), column],
        out_specs=[column] * 3,
        out_shape=[jax.ShapeDtypeStruct((rows, D), LOW)] * 3,
        compiler_params=pltpu.CompilerParams(vmem_limit_bytes=GRANT),
        cost_estimate=pl.CostEstimate(
            flops=12 * HEADS * LEN * LEN * 256, bytes_accessed=HEADS * LEN * LEN * 2 + LEN * D * 14, transcendentals=0),
        name="attend_back",
    )(queries, keys, values, probs, grads)


def gelu_both(point):
    bell = jnp.exp(point * point * -0.5)
    ratio = 1.0 / (1.0 + (0.3275911 * 0.5**0.5) * jnp.abs(point))
    series = 0.5 * 1.061405429
    for factor in (-1.453152027, 1.421413741, -0.284496736, 0.254829592):
        series = series * ratio + 0.5 * factor
    below = series * ratio * bell
    normal = jnp.where(point < 0, below, 1.0 - below)
    return point * normal, normal + point * bell * 0.3989422804014327


def norm_rows(summed):
    centered = summed - jnp.mean(summed, axis=-1, keepdims=True)
    inverse = lax.rsqrt(jnp.mean(centered * centered, axis=-1, keepdims=True) + EPS)
    return centered * inverse, inverse


def norm_back_rows(scaled, normed, inverse):
    mean_grad = jnp.mean(scaled, axis=-1, keepdims=True)
    mean_cross = jnp.mean(scaled * normed, axis=-1, keepdims=True)
    return inverse * (scaled - mean_grad - normed * mean_cross)


def strips(rows, body):
    def step(index, carry):
        body(pl.ds(pl.multiple_of(index * STRIP, STRIP), STRIP))
        return carry

    lax.fori_loop(0, rows // STRIP, step, 0)


def fixed(array):
    return pl.BlockSpec(array.shape, lambda *place: (0,) * array.ndim, pipeline_mode=pl.Buffered(1))


def held(rows, cols):
    return pl.BlockSpec((rows, cols), lambda *place: (0, 0), pipeline_mode=pl.Buffered(1))


def branch_kernel(attn_ref, tokens_ref, wout_ref, bout_ref, gain_ref, shift_ref, normed_ref, inverse_ref, low_ref):
    summed = tokens_ref[...].astype(FULL) + dot_nn(attn_ref[...], wout_ref[...]) + bout_ref[...]
    normed, inverse = norm_rows(summed)
    normed_ref[...] = normed
    inverse_ref[...] = inverse
    low_ref[...] = (normed * gain_ref[...] + shift_ref[...]).astype(LOW)


def branch(attn_rows, tokens, w_out, b_out, gain, shift):
    rows = tokens.shape[0]
    strip = lambda cols: pl.BlockSpec((STRIP, cols), lambda i: (i, 0))
    return pl.pallas_call(
        branch_kernel,
        grid=(rows // STRIP,),
        in_specs=[strip(D), strip(D), fixed(w_out), fixed(b_out), fixed(gain), fixed(shift)],
        out_specs=[strip(D), strip(1), strip(D)],
        out_shape=[
            jax.ShapeDtypeStruct((rows, D), FULL), jax.ShapeDtypeStruct((rows, 1), FULL),
            jax.ShapeDtypeStruct((rows, D), LOW),
        ],
        compiler_params=pltpu.CompilerParams(vmem_limit_bytes=GRANT),
        cost_estimate=pl.CostEstimate(flops=4 * rows * D * D, bytes_accessed=rows * D * 10 + D * D * 2, transcendentals=0),
        name="branch",
    )(attn_rows, tokens, w_out, b_out, gain, shift)


def widen_kernel(low_ref, wup_ref, bup_ref, hidden_ref, slope_ref):
    def strip(rows):
        point = dot_nn(low_ref[rows, :], wup_ref[...]) + bup_ref[...]
        hidden, slope = gelu_both(point)
        hidden_ref[rows, :] = hidden.astype(LOW)
        slope_ref[rows, :] = slope.astype(LOW)

    strips(low_ref.shape[0], strip)


def widen(first_low, w_up, b_up, first, last, before=()):
    rows, width = first_low.shape[0], w_up.shape[1]
    chunk = lambda height: pl.BlockSpec((height, WIDE), lambda i: (0, i + first))
    return continued(
        widen_kernel,
        before,
        grid=(last - first,),
        in_specs=[fixed(first_low), chunk(D), chunk(1)],
        out_specs=[chunk(rows), chunk(rows)],
        out_shape=[jax.ShapeDtypeStruct((rows, width), LOW)] * 2,
        compiler_params=pltpu.CompilerParams(vmem_limit_bytes=GRANT),
        cost_estimate=pl.CostEstimate(
            flops=6 * rows * D * WIDE * (last - first), bytes_accessed=WIDE * (last - first) * (D * 2 + rows * 4),
            transcendentals=rows * WIDE * (last - first)),
        name="widen",
    )(first_low, w_up, b_up)


def fall_kernel(hidden_ref, wdown_ref, normed_ref, cot_ref, bdown_ref, gain1_ref, shift1_ref, gain2_ref, shift2_ref,
                out_ref, second_ref, ffn_ref, sums_ref, total):
    step = pl.program_id(0)

    @pl.when(step == 0)
    def _():
        total[...] = dot_nn(hidden_ref[...], wdown_ref[...])

    @pl.when(step > 0)
    def _():
        total[...] += dot_nn(hidden_ref[...], wdown_ref[...])

    @pl.when(step == pl.num_programs(0) - 1)
    def _():
        sums_ref[...] = jnp.zeros_like(sums_ref)

        def finish(rows):
            first_out = normed_ref[rows, :] * gain1_ref[...] + shift1_ref[...]
            normed, inverse = norm_rows(first_out + total[rows, :] + bdown_ref[...])
            out_ref[rows, :] = (normed * gain2_ref[...] + shift2_ref[...]).astype(LOW)
            upstream = cot_ref[rows, :].astype(FULL)
            second = norm_back_rows(upstream * gain2_ref[...], normed, inverse)
            low = second.astype(LOW)
            second_ref[rows, :] = second
            ffn_ref[rows, :] = low
            sums_ref[...] += jnp.concatenate([
                jnp.sum(part, axis=0, keepdims=True) for part in (upstream * normed, upstream, low.astype(FULL))
            ], axis=0)

        strips(out_ref.shape[0], finish)


def fall(hidden, w_down, normed, cotangent, b_down, gain1, shift1, gain2, shift2, chunk=1024):
    rows, width = hidden.shape
    return pl.pallas_call(
        fall_kernel,
        grid=(width // chunk,),
        in_specs=[
            pl.BlockSpec((rows, chunk), lambda i: (0, i)), pl.BlockSpec((chunk, D), lambda i: (i, 0)),
        ] + [fixed(a) for a in (normed, cotangent, b_down, gain1, shift1, gain2, shift2)],
        out_specs=[held(rows, D), held(rows, D), held(rows, D), held(3, D)],
        out_shape=[
            jax.ShapeDtypeStruct((rows, D), LOW), jax.ShapeDtypeStruct((rows, D), FULL),
            jax.ShapeDtypeStruct((rows, D), LOW), jax.ShapeDtypeStruct((3, D), FULL),
        ],
        scratch_shapes=[pltpu.VMEM((rows, D), FULL)],
        compiler_params=pltpu.CompilerParams(vmem_limit_bytes=GRANT),
        cost_estimate=pl.CostEstimate(
            flops=2 * rows * D * width, bytes_accessed=rows * (D * 14 + width * 2) + D * width * 2, transcendentals=0),
        name="fall",
    )(hidden, w_down, normed, cotangent, b_down, gain1, shift1, gain2, shift2)


def narrow_kernel(ffn_ref, slope_ref, wdown_ref, wup_ref, so_far_ref, pre_ref, wide_ref, total_ref):
    @pl.when(pl.program_id(0) == 0)
    def _():
        total_ref[...] = so_far_ref[...]

    wide_ref[...] = jnp.zeros_like(wide_ref)

    def strip(rows):
        d_hidden = dot_nt(ffn_ref[rows, :], wdown_ref[...])
        d_pre = (slope_ref[rows, :].astype(FULL) * d_hidden).astype(LOW)
        pre_ref[rows, :] = d_pre
        wide_ref[...] += jnp.sum(d_pre.astype(FULL), axis=0, keepdims=True)
        total_ref[rows, :] += dot_nt(d_pre, wup_ref[...])

    strips(ffn_ref.shape[0], strip)


def narrow(d_ffn, slope, w_down, w_up, so_far, first, last):
    rows, width = slope.shape[0], WIDE * (last - first)
    own = lambda height: pl.BlockSpec((height, WIDE), lambda i: (0, i))
    chunk = lambda height: pl.BlockSpec((height, WIDE), lambda i: (0, i + first))
    return pl.pallas_call(
        narrow_kernel,
        grid=(last - first,),
        in_specs=[
            fixed(d_ffn), chunk(rows), pl.BlockSpec((WIDE, D), lambda i: (i + first, 0)), chunk(D), fixed(so_far),
        ],
        out_specs=[own(rows), own(1), held(rows, D)],
        out_shape=[
            jax.ShapeDtypeStruct((rows, width), LOW), jax.ShapeDtypeStruct((1, width), FULL),
            jax.ShapeDtypeStruct((rows, D), FULL),
        ],
        compiler_params=pltpu.CompilerParams(vmem_limit_bytes=GRANT),
        cost_estimate=pl.CostEstimate(
            flops=6 * rows * D * WIDE * (last - first), bytes_accessed=WIDE * (last - first) * (D * 4 + rows * 4) + rows * D * 10,
            transcendentals=0),
        name="narrow",
    )(d_ffn, slope, w_down, w_up, so_far)


def resid_kernel(first_ref, normed_ref, inverse_ref, gain_ref, wout_ref, resid_ref, branch_ref, attn_ref, sums_ref):
    d_first, normed = first_ref[...], normed_ref[...]
    resid = norm_back_rows(d_first * gain_ref[...], normed, inverse_ref[...])
    low = resid.astype(LOW)
    resid_ref[...] = resid
    branch_ref[...] = low
    attn_ref[...] = dot_nt(low, wout_ref[...]).astype(LOW)
    sums = jnp.concatenate([
        jnp.sum(part, axis=0, keepdims=True) for part in (d_first * normed, d_first, low.astype(FULL))
    ], axis=0)

    @pl.when(pl.program_id(0) == 0)
    def _():
        sums_ref[...] = sums

    @pl.when(pl.program_id(0) > 0)
    def _():
        sums_ref[...] += sums


def resid_back(d_first, normed, inverse, gain, w_out):
    rows = d_first.shape[0]
    strip = lambda cols: pl.BlockSpec((STRIP, cols), lambda i: (i, 0))
    return pl.pallas_call(
        resid_kernel,
        grid=(rows // STRIP,),
        in_specs=[strip(D), strip(D), strip(1), fixed(gain), fixed(w_out)],
        out_specs=[strip(D), strip(D), strip(D), held(3, D)],
        out_shape=[
            jax.ShapeDtypeStruct((rows, D), FULL), jax.ShapeDtypeStruct((rows, D), LOW),
            jax.ShapeDtypeStruct((rows, D), LOW), jax.ShapeDtypeStruct((3, D), FULL),
        ],
        compiler_params=pltpu.CompilerParams(vmem_limit_bytes=GRANT),
        cost_estimate=pl.CostEstimate(flops=4 * rows * D * D, bytes_accessed=rows * D * 16 + D * D * 2, transcendentals=0),
        name="resid_back",
    )(d_first, normed, inverse, gain, w_out)


def tall_kernel(left_ref, right_ref, keep_ref, send_ref, product):
    core = lax.axis_index("dp") & 1
    product[...] = dot_tn(left_ref[...], right_ref[...]).astype(LOW).reshape(product.shape)
    for pair in range(2):
        keep_ref[pair] = product[pair, core]
        send_ref[pair] = product[pair, 1 - core]


def outer_tall(left, right, count):
    rows, width = left.shape
    cols, part = right.shape[1], width // count
    out = pl.BlockSpec((2, part, cols), lambda i: (i, 0, 0))
    return pl.pallas_call(
        tall_kernel,
        grid=(count // 4,),
        in_specs=[pl.BlockSpec((rows, 4 * part), lambda i: (0, i)), fixed(right)],
        out_specs=[out, out],
        out_shape=[jax.ShapeDtypeStruct((count // 2, part, cols), LOW)] * 2,
        scratch_shapes=[pltpu.VMEM((2, 2, part, cols), LOW)],
        compiler_params=pltpu.CompilerParams(vmem_limit_bytes=GRANT),
        cost_estimate=pl.CostEstimate(
            flops=2 * rows * width * cols, bytes_accessed=2 * (rows * (width + cols) + width * cols), transcendentals=0),
        name="outer_tall",
    )(left, right)


def wide_kernel(starts, *refs):
    pairs = len(starts) - 1
    lefts, rights, (keep, send, product) = refs[:pairs], refs[pairs : 2 * pairs], refs[2 * pairs :]
    step = pl.program_id(0)
    core = lax.axis_index("dp") & 1
    for left, right, low, high in zip(lefts, rights, starts, starts[1:]):
        @pl.when((step >= low) & (step < high))
        def _():
            product[...] = dot_tn(left[...], right[...]).astype(LOW).reshape(product.shape)

    keep[...] = product[:, core]
    send[...] = product[:, 1 - core]


def outer_wide(lefts, rights, count):
    rows, height = lefts[0].shape
    part = height // count
    starts = [0]
    for right in rights:
        starts.append(starts[-1] + right.shape[1] // WIDE)
    total = starts[-1]

    def strip(low, high):
        return pl.BlockSpec((rows, WIDE), lambda i: (0, jnp.clip(i - low, 0, high - low - 1)))

    out = pl.BlockSpec((count // 2, part, WIDE), lambda i: (0, 0, i))
    return pl.pallas_call(
        functools.partial(wide_kernel, starts),
        grid=(total,),
        in_specs=[fixed(left) for left in lefts] + [strip(low, high) for low, high in zip(starts, starts[1:])],
        out_specs=[out, out],
        out_shape=[jax.ShapeDtypeStruct((count // 2, part, WIDE * total), LOW)] * 2,
        scratch_shapes=[pltpu.VMEM((count // 2, 2, part, WIDE), LOW)],
        compiler_params=pltpu.CompilerParams(vmem_limit_bytes=GRANT),
        cost_estimate=pl.CostEstimate(
            flops=2 * rows * height * WIDE * total,
            bytes_accessed=2 * (rows * (height * len(lefts) + WIDE * total) + height * WIDE * total), transcendentals=0),
        name="outer_wide",
    )(*lefts, *rights)


FLIPS = {"c": 1, "x": 2, "y": 4}
TWO_WAYS = ("zyx", "xzy")
EARLY_WAYS = ("zyx", "xzy", "yzx")
GRANT = 58 * 1024 * 1024


def hop(array, dim, count):
    if dim in FLIPS:
        return lax.ppermute(array, "dp", [(place, place ^ FLIPS[dim]) for place in range(count)])
    step = 8 * (1 if dim == "z" else dim)
    return lax.ppermute(array, "dp", [(place, (place + step) % count) for place in range(count)])


def after(value, *earlier):
    return lax.optimization_barrier((value, earlier))[0] if earlier else value


def mine_of():
    me = lax.axis_index("dp")
    return {
        "z": lax.shift_right_logical(me, 3),
        "y": lax.shift_right_logical(me, 2) & 1,
        "x": lax.shift_right_logical(me, 1) & 1,
        "c": me & 1,
    }


def gather_steps(shard, order, count):
    stack = shard[None]
    gate = yield
    for dim in order[:2]:
        pieces = [stack]
        for _ in range(count // 8 - 1 if dim == "z" else 1):
            pieces.append(hop(after(pieces[-1], *gate), dim, count))
            gate = yield pieces[-1]
        stack = jnp.concatenate(pieces, axis=0)
    across = hop(after(stack, *gate), order[2], count)
    gate = yield across
    yield (stack, across, hop(after(stack, *gate), "c", count), hop(after(across, *gate), "c", count))


def gather_part(shard, order, count):
    steps = gather_steps(shard, order, count)
    next(steps)
    for _ in range(6):
        last = steps.send(())
    return last


def place_kernel(count, orders, cuts, bases, rows, *refs):
    pieces, outs = refs[: 4 * len(orders)], refs[4 * len(orders) :]
    ring = count // 8
    mine = mine_of()
    slot = pl.program_id(0)
    for part, order in enumerate(orders):
        left, right = cuts[part], cuts[part + 1]
        for which in range(4):
            digits = {"c": which // 2, order[2]: which % 2}
            rest = slot
            for dim in order[:2]:
                size = ring if dim == "z" else 2
                digits[dim] = lax.rem(rest, size)
                rest = lax.div(rest, size)
            owner = lax.rem(mine["z"] + ring - digits["z"], ring) * 8
            for dim, weight in (("y", 4), ("x", 2), ("c", 1)):
                owner = owner + weight * (mine[dim] ^ digits[dim])
            row = pl.ds(pl.multiple_of(owner * rows, rows), rows)
            for out, base, stop in zip(outs, bases, bases[1:]):
                low, high = max(left, base), min(right, stop)
                if low < high:
                    out[row, low - base : high - base] = pieces[4 * part + which][0, :, low - left : high - left]


def place(pieces, orders, cuts, widths, rows, count):
    bases = [sum(widths[:index]) for index in range(len(widths) + 1)]
    size = count * rows
    return pl.pallas_call(
        functools.partial(place_kernel, count, orders, cuts, bases, rows),
        grid=(count // 4,),
        in_specs=[pl.BlockSpec((1, rows, piece.shape[2]), lambda i: (i, 0, 0)) for piece in pieces],
        out_specs=[held(size, width) for width in widths],
        out_shape=[jax.ShapeDtypeStruct((size, width), LOW) for width in widths],
        compiler_params=pltpu.CompilerParams(vmem_limit_bytes=GRANT),
        cost_estimate=pl.CostEstimate(flops=0, bytes_accessed=4 * size * bases[-1], transcendentals=0),
        name="place",
    )(*pieces)


def whole_arrays(shard, widths):
    full = lax.all_gather(shard, "dp", axis=0, tiled=True)
    bases = [sum(widths[:index]) for index in range(len(widths) + 1)]
    return [full[:, low:high] for low, high in zip(bases, bases[1:])]


def gather_early(shard, widths, count):
    if count != 32:
        return whole_arrays(shard, widths)
    cuts = (0, D, 2 * D, sum(widths))
    pieces = ()
    for order, low, high in zip(EARLY_WAYS, cuts, cuts[1:]):
        pieces += tuple(gather_part(shard[:, low:high], order, count))
    return place(pieces, EARLY_WAYS, cuts, widths, shard.shape[0], count)


class Gathering:
    def __init__(self, shard, cut, count):
        self.count, self.cuts, self.rows = count, (0, cut, shard.shape[1]), shard.shape[0]
        self.steps = [
            gather_steps(shard[:, low:high], order, count)
            for order, low, high in zip(TWO_WAYS, self.cuts, self.cuts[1:])
        ]
        self.last = None

    def move(self, *gate):
        if self.last is None:
            [next(steps) for steps in self.steps]
        self.last = [steps.send(gate) for steps in self.steps]

    def result(self):
        return place(self.last[0] + self.last[1], TWO_WAYS, self.cuts, (self.cuts[-1],), self.rows, self.count)[0]


def add_low(left_side, right_side, kind=LOW):
    return (left_side.astype(FULL) + right_side.astype(FULL)).astype(kind)


def take(blocks, axis, index):
    return lax.dynamic_index_in_dim(blocks, index, axis, keepdims=False, allow_negative_indices=False)


def split_kernel(cut, keep_ref, came_ref, keep1_ref, send1_ref, keep2_ref, send2_ref):
    mine = mine_of()
    for side in range(2):
        for keep, send, dim, cols in (
            (keep1_ref, send1_ref, "x", slice(0, cut)),
            (keep2_ref, send2_ref, "y", slice(cut, None)),
        ):
            for out, index in ((keep, mine[dim]), (send, 1 - mine[dim])):
                where = (0, side, index, slice(None), cols) if dim == "x" else (0, index, side, slice(None), cols)
                out[0, side] = add_low(keep_ref[where], came_ref[where])


def turn_kernel(keep1_ref, came1_ref, keep2_ref, came2_ref, keep3_ref, send3_ref, keep4_ref, send4_ref):
    mine = mine_of()
    for kept, came, keep, send, dim in (
        (keep1_ref, came1_ref, keep3_ref, send3_ref, "y"),
        (keep2_ref, came2_ref, keep4_ref, send4_ref, "x"),
    ):
        for out, index in ((keep, mine[dim]), (send, 1 - mine[dim])):
            out[...] = add_low(kept[:, index], came[:, index])


def tower_kernel(cut, keep3_ref, came3_ref, keep4_ref, came4_ref, *outs):
    own = mine_of()["z"]
    ring = keep3_ref.shape[0]
    for distance, out in enumerate(outs):
        index = lax.rem(own + distance, ring)
        out[:, :cut] = add_low(keep3_ref[index], came3_ref[index])
        out[:, cut:] = add_low(keep4_ref[index], came4_ref[index])


def local_kernel(kernel, name, outs, grid, in_specs, out_specs, operands):
    size = sum(array.size * array.dtype.itemsize for array in operands)
    return pl.pallas_call(
        kernel,
        grid=grid,
        in_specs=in_specs,
        out_specs=out_specs,
        out_shape=outs,
        compiler_params=pltpu.CompilerParams(vmem_limit_bytes=GRANT),
        cost_estimate=pl.CostEstimate(flops=0, bytes_accessed=2 * size, transcendentals=0),
        name=name,
    )(*operands)


class Sums:
    def __init__(self, keep, send, count):
        self.count, self.ring = count, count // 8
        self.rows, self.cols = keep.shape[1:]
        self.cut = self.cols // 2
        self.stage = 0
        self.keeps, self.sends, self.dims = [keep], [send], ["c"]

    def start(self):
        self.came = [hop(send, dim, self.count) for send, dim in zip(self.sends, self.dims)]
        return self.sends

    def move(self, *gate):
        came = [after(array, *gate) for array in self.came]
        ring, rows, cut, rest = self.ring, self.rows, self.cut, self.cols - self.cut
        self.stage += 1
        if self.stage == 1:
            whole = lambda array: array.reshape(ring, 2, 2, rows, self.cols)
            block = pl.BlockSpec((1, 2, 2, rows, self.cols), lambda i: (i, 0, 0, 0, 0))
            widths = (cut, cut, rest, rest)
            self.pairs(local_kernel(
                functools.partial(split_kernel, cut), "split",
                [jax.ShapeDtypeStruct((ring, 2, rows, width), LOW) for width in widths], (ring,), [block] * 2,
                [pl.BlockSpec((1, 2, rows, width), lambda i: (i, 0, 0, 0)) for width in widths],
                [whole(self.keeps[0]), whole(came[0])],
            ), ["x", "y"])
        elif self.stage == 2:
            operands = [self.keeps[0], came[0], self.keeps[1], came[1]]
            self.pairs(local_kernel(
                turn_kernel, "turn",
                [jax.ShapeDtypeStruct((ring, rows, width), LOW) for width in (cut, cut, rest, rest)], (ring,),
                [pl.BlockSpec((1,) + array.shape[1:], lambda i: (i, 0, 0, 0)) for array in operands],
                [pl.BlockSpec((1, rows, width), lambda i: (i, 0, 0)) for width in (cut, cut, rest, rest)],
                operands,
            ), ["y", "x"])
        elif self.stage == 3:
            operands = [self.keeps[0], came[0], self.keeps[1], came[1]]
            outs = local_kernel(
                functools.partial(tower_kernel, cut), "tower",
                [jax.ShapeDtypeStruct((rows, self.cols), LOW)] * ring, (1,),
                [fixed(array) for array in operands], [held(rows, self.cols)] * ring, operands,
            )
            self.keeps, self.sends, self.dims = list(outs[:1]), list(outs[1:]), list(range(1, ring))
        else:
            self.total = self.keeps[0].astype(FULL)
            for array in came:
                self.total = self.total + array.astype(FULL)
            return [self.total]
        return self.start()

    def pairs(self, arrays, dims):
        self.keeps, self.sends, self.dims = [arrays[0], arrays[2]], [arrays[1], arrays[3]], dims


def sum_everywhere(rows, count):
    for dim in "cxy":
        rows = rows + hop(rows, dim, count)
    shifts = [hop(rows, distance, count) for distance in range(1, count // 8)]
    return functools.reduce(jnp.add, shifts, rows)


def local(
    tokens,
    w_query,
    w_key,
    w_value,
    w_out,
    w_up,
    w_down,
    b_query,
    b_value,
    b_out,
    b_up,
    b_down,
    gain_attn,
    shift_attn,
    gain_ffn,
    shift_ffn,
    cotangent,
):
    count = D // w_query.shape[0]
    part = D // count
    wide = w_up.shape[1]
    custom = count == 32
    small = (b_query, b_value, b_out, b_down, gain_attn, shift_attn, gain_ffn, shift_ffn)
    packed = sum(
        jnp.pad(array[None], ((row, 15 - row), (0, 128 - array.shape[0]))) for row, array in enumerate(small + (b_up,))
    )
    height = max(part, 16)
    tops = [jnp.pad(array, ((0, height - part), (0, 0))) for array in (w_query, w_key, w_value)]
    early = jnp.concatenate(tops + [jnp.pad(packed, ((0, height - 16), (0, 0)))], axis=1)
    w_query, w_key, w_value, packed = gather_early(early, (D, D, D, 128), count)
    if height > part:
        w_query, w_key, w_value = [
            array.reshape(count, height, D)[:, :part].reshape(D, D) for array in (w_query, w_key, w_value)
        ]
    w_up = lax.all_gather(w_up, "dp", axis=0, tiled=True)
    w_out = lax.all_gather(w_out, "dp", axis=0, tiled=True)
    packed = packed.reshape(count, height, 128)
    vector = lambda row: packed[:, row, :part].reshape(1, D).astype(FULL)
    b_query, b_value, b_out, b_down, gain_attn, shift_attn, gain_ffn, shift_ffn = map(vector, range(8))
    b_up = packed[:, 8, : wide // count].reshape(1, wide).astype(FULL)
    chunks = wide // WIDE
    sequences = tokens.shape[0] // LEN

    def under(value, gather, gate):
        if not custom:
            return value
        earlier = gather.last or ()
        gather.move(gate)
        return after(value, *earlier)

    down_gather = Gathering(w_down, D // 2, count) if custom else None
    tokens_in = under(tokens, down_gather, w_query)
    queries = (dot_nn(tokens_in, w_query) + b_query).astype(LOW)
    tokens_in = under(tokens, down_gather, queries)
    keys = dot_nn(tokens_in, w_key).astype(LOW)
    tokens_in = under(tokens, down_gather, keys)
    values = (dot_nn(tokens_in, w_value) + b_value).astype(LOW)
    values = under(values, down_gather, values)
    seen = ()
    for sequence in range(sequences):
        seen = attend(queries, keys, values, sequence, seen)
        if sequence == 0:
            values = under(values, down_gather, seen[1])
    probs, attn_rows = seen
    normed, inverse, first_low = branch(attn_rows, tokens, w_out, b_out, gain_attn, shift_attn)
    half = widen(first_low, w_up, b_up, 0, chunks // 2)
    first_low = under(first_low, down_gather, half[0])
    hidden, slope = widen(first_low, w_up, b_up, chunks // 2, chunks, half)
    w_down = down_gather.result() if custom else lax.all_gather(w_down, "dp", axis=0, tiled=True)
    result, second, d_ffn, sums_ffn = fall(
        hidden, w_down, normed, cotangent, b_down, gain_attn, shift_attn, gain_ffn, shift_ffn
    )

    if custom:
        down = Sums(*outer_tall(hidden, d_ffn, count), count)
        second = after(second, *down.start())
    pre_1, wide_1, d_first = narrow(d_ffn, slope, w_down, w_up, second, 0, 2)
    if custom:
        d_first = after(d_first, *down.move(wide_1))
    pre_2, wide_2, d_first = narrow(d_ffn, slope, w_down, w_up, d_first, 2, 5)
    pre_3, wide_3, d_first = narrow(d_ffn, slope, w_down, w_up, d_first, 5, chunks)
    if custom:
        d_first = after(d_first, *down.move(wide_3))
    d_resid, d_branch, d_attn, sums_attn = resid_back(d_first, normed, inverse, gain_attn, w_out)
    if custom:
        up = Sums(*outer_wide([first_low] * 3 + [attn_rows], [pre_1, pre_2, pre_3, d_branch], count), count)
        d_attn = after(d_attn, *up.start())
        d_attn = after(d_attn, *down.move(*up.keeps))
    seen = attend_back(queries, keys, values, probs, d_attn, 0)
    if custom:
        d_attn = after(d_attn, *up.move(seen[0]))
    for sequence in range(1, sequences):
        seen = attend_back(queries, keys, values, probs, d_attn, sequence, seen)
    d_queries, d_keys, d_values = seen
    if custom:
        first = Sums(*outer_wide([tokens] * 3, [d_queries, d_keys, d_values], count), count)
        d_queries = after(d_queries, *first.start())
        d_queries = after(d_queries, *down.move(*first.keeps))
        d_queries = after(d_queries, *up.move(*first.keeps))
    column_sum = lambda rows: jnp.sum(rows.astype(FULL), axis=0, keepdims=True)
    sums = jnp.concatenate([
        column_sum(d_queries), column_sum(d_values), sums_attn[2:], sums_ffn[2:], sums_attn[:2], sums_ffn[:2],
        jnp.concatenate([wide_1, wide_2, wide_3], axis=1).reshape(-1, D),
    ], axis=0)
    grad_rows = d_resid + dot_nt(d_queries, w_query)
    if custom:
        grad_rows = after(grad_rows, *first.move(grad_rows))
    grad_rows = (grad_rows + dot_nt(d_keys, w_key) + dot_nt(d_values, w_value)).astype(LOW)

    if custom:
        up.move(grad_rows)
        first.move(grad_rows)
        up.move()
        first.move()
        first.move()
        d_w_down, second, first = down.total, up.total, first.total
        d_w_up, d_w_out = second[:, :wide], second[:, wide:]
        d_w_query, d_w_key, d_w_value = first[:, :D], first[:, D : 2 * D], first[:, 2 * D :]
        sums = sum_everywhere(sums, count)
    else:
        total = lambda grad: lax.psum_scatter(grad.astype(LOW), "dp", scatter_dimension=0, tiled=True).astype(FULL)
        d_w_down = total(dot_tn(hidden, d_ffn))
        d_w_up = total(jnp.concatenate([dot_tn(first_low, pre) for pre in (pre_1, pre_2, pre_3)], axis=1))
        d_w_out = total(dot_tn(attn_rows, d_branch))
        d_w_query, d_w_key, d_w_value = [total(dot_tn(tokens, grad)) for grad in (d_queries, d_keys, d_values)]
        sums = lax.psum(sums, "dp")
    me = lax.axis_index("dp")
    own = lax.dynamic_slice_in_dim(sums[:8], me * part, part, axis=1, allow_negative_indices=False)
    vector = lambda row: own[row]
    d_b_up = lax.dynamic_slice_in_dim(
        sums[8:].reshape(-1), me * (wide // count), wide // count, allow_negative_indices=False
    )
    return (
        result,
        grad_rows,
        d_w_query,
        d_w_key,
        d_w_value,
        d_w_out,
        d_w_up,
        d_w_down,
        vector(0),
        vector(1),
        vector(2),
        d_b_up,
        vector(3),
        vector(4),
        vector(5),
        vector(6),
        vector(7),
    )


def solution(mesh):
    placed = (
        P("dp", None),
        P("dp", None),
        P("dp", None),
        P("dp", None),
        P("dp", None),
        P("dp", None),
        P("dp", None),
        P("dp"),
        P("dp"),
        P("dp"),
        P("dp"),
        P("dp"),
        P("dp"),
        P("dp"),
        P("dp"),
        P("dp"),
        P("dp", None),
    )
    return jax.shard_map(
        local,
        mesh=mesh,
        in_specs=placed,
        out_specs=(
            P("dp", None),
            P("dp", None),
            P("dp", None),
            P("dp", None),
            P("dp", None),
            P("dp", None),
            P("dp", None),
            P("dp", None),
            P("dp"),
            P("dp"),
            P("dp"),
            P("dp"),
            P("dp"),
            P("dp"),
            P("dp"),
            P("dp"),
            P("dp"),
        ),
        check_vma=False,
    )
```

```python
import functools
import jax
import jax.numpy as jnp
from jax import lax
from jax.experimental import pallas as pl
from jax.experimental.pallas import tpu as pltpu
from jax.sharding import PartitionSpec as P

D = 1024
HEADS = 16
LEN = 512
EPS = 1e-12
LOW = jnp.bfloat16
FULL = jnp.float32
MIB = 1024 * 1024
WIDE = 512
STRIP = 256
GRANT = 58 * MIB
WEIGHT = 16


def dot_nn(left_side, right_side):
    return lax.dot_general(left_side, right_side, (((1,), (0,)), ((), ())), preferred_element_type=FULL)


def dot_nt(left_side, right_side):
    return lax.dot_general(left_side, right_side, (((1,), (1,)), ((), ())), preferred_element_type=FULL)


def dot_tn(left_side, right_side):
    return lax.dot_general(left_side, right_side, (((0,), (0,)), ((), ())), preferred_element_type=FULL)


def head_mask(rows, head):
    lane = lax.broadcasted_iota(jnp.int32, (rows, 128), 1)
    return (lane // 64) == head


def attend_kernel(q_ref, k_ref, v_ref, probs_ref, rows_ref):
    scale = (D // HEADS) ** -0.5
    queries = (q_ref[...].astype(FULL) * scale).astype(LOW)
    keys, values = k_ref[...], v_ref[...]
    mixed = jnp.zeros((LEN, 128), FULL)
    for head in range(2):
        mask = head_mask(LEN, head)
        zero = jnp.zeros((), LOW)
        scores = dot_nt(queries, jnp.where(mask, keys, zero))
        maxima = jnp.max(scores, axis=-1, keepdims=True)
        exponent = jnp.exp(scores - maxima)
        total = jnp.sum(exponent, axis=-1, keepdims=True)
        probs = (exponent * (1.0 / total)).astype(LOW)
        probs_ref[0, head] = probs
        mixed = mixed + dot_nn(probs, jnp.where(mask, values, zero))
    rows_ref[...] = mixed.astype(LOW)


def placed(kernel, ins, count, *refs):
    kernel(*refs[:ins], *refs[ins + count :])


def continued(kernel, before, in_specs, out_specs, out_shape, **rest):
    aliases = {}
    if before:
        count = len(before)
        kernel = functools.partial(placed, kernel, len(in_specs), count)
        aliases = {len(in_specs) + index: index for index in range(count)}
        in_specs = list(in_specs) + [pl.BlockSpec(memory_space=pl.ANY)] * count
    call = pl.pallas_call(
        kernel, in_specs=in_specs, out_specs=out_specs, out_shape=out_shape, input_output_aliases=aliases, **rest
    )
    return lambda *operands: call(*operands, *before)


def attend(queries, keys, values, sequence, before=()):
    rows = queries.shape[0]
    column = pl.BlockSpec((LEN, 128), lambda p: (sequence, p))
    return continued(
        attend_kernel,
        before,
        grid=(HEADS // 2,),
        in_specs=[column] * 3,
        out_specs=[pl.BlockSpec((1, 2, LEN, LEN), lambda p: (sequence, p, 0, 0)), column],
        out_shape=[
            jax.ShapeDtypeStruct((rows // LEN, HEADS, LEN, LEN), LOW),
            jax.ShapeDtypeStruct((rows, D), LOW),
        ],
        compiler_params=pltpu.CompilerParams(vmem_limit_bytes=GRANT),
        cost_estimate=pl.CostEstimate(
            flops=12 * HEADS * LEN * LEN * 256, bytes_accessed=HEADS * LEN * LEN * 2 + LEN * D * 8,
            transcendentals=HEADS * LEN * LEN),
        name="attend",
    )(queries, keys, values)


def attend_back_kernel(q_ref, k_ref, v_ref, probs_ref, grad_ref, dq_ref, dk_ref, dv_ref):
    scale = (D // HEADS) ** -0.5
    queries, keys, values, grads = q_ref[...], k_ref[...], v_ref[...], grad_ref[...]
    zero = jnp.zeros((), LOW)
    d_queries = jnp.zeros((LEN, 128), FULL)
    d_keys = jnp.zeros((128, LEN), FULL)
    d_values = jnp.zeros((128, LEN), FULL)
    for head in range(2):
        mask = head_mask(LEN, head)
        probs = probs_ref[0, head]
        own_grads = jnp.where(mask, grads, zero)
        d_probs = dot_nt(own_grads, values).astype(LOW).astype(FULL)
        wide = probs.astype(FULL)
        product = d_probs * wide
        total = jnp.sum(product, axis=-1, keepdims=True)
        d_scores = (product - wide * total).astype(LOW)
        d_queries = d_queries + dot_nn(d_scores, jnp.where(mask, keys, zero))
        d_keys = d_keys + dot_tn(jnp.where(mask, queries, zero), d_scores)
        d_values = d_values + dot_tn(own_grads, probs)
    dq_ref[...] = (scale * d_queries).astype(LOW)
    dk_ref[...] = (scale * d_keys.T).astype(LOW)
    dv_ref[...] = d_values.T.astype(LOW)


def attend_back(queries, keys, values, probs, grads, sequence, before=()):
    rows = queries.shape[0]
    column = pl.BlockSpec((LEN, 128), lambda p: (sequence, p))
    return continued(
        attend_back_kernel,
        before,
        grid=(HEADS // 2,),
        in_specs=[column, column, column, pl.BlockSpec((1, 2, LEN, LEN), lambda p: (sequence, p, 0, 0)), column],
        out_specs=[column] * 3,
        out_shape=[jax.ShapeDtypeStruct((rows, D), LOW)] * 3,
        compiler_params=pltpu.CompilerParams(vmem_limit_bytes=GRANT),
        cost_estimate=pl.CostEstimate(
            flops=WEIGHT * 12 * HEADS * LEN * LEN * 256, bytes_accessed=HEADS * LEN * LEN * 2 + LEN * D * 14, transcendentals=0),
        name="attend_back",
    )(queries, keys, values, probs, grads)


def gelu_both(point):
    bell = jnp.exp(point * point * -0.5)
    ratio = 1.0 / (1.0 + (0.3275911 * 0.5**0.5) * jnp.abs(point))
    series = 0.5 * 1.061405429
    for factor in (-1.453152027, 1.421413741, -0.284496736, 0.254829592):
        series = series * ratio + 0.5 * factor
    below = series * ratio * bell
    normal = jnp.where(point < 0, below, 1.0 - below)
    return point * normal, normal + point * bell * 0.3989422804014327


def norm_rows(summed):
    centered = summed - jnp.mean(summed, axis=-1, keepdims=True)
    inverse = lax.rsqrt(jnp.mean(centered * centered, axis=-1, keepdims=True) + EPS)
    return centered * inverse, inverse


def norm_back_rows(scaled, normed, inverse):
    mean_grad = jnp.mean(scaled, axis=-1, keepdims=True)
    mean_cross = jnp.mean(scaled * normed, axis=-1, keepdims=True)
    return inverse * (scaled - mean_grad - normed * mean_cross)


def strips(rows, body):
    def step(index, carry):
        body(pl.ds(pl.multiple_of(index * STRIP, STRIP), STRIP))
        return carry

    lax.fori_loop(0, rows // STRIP, step, 0)


def fixed(array):
    return pl.BlockSpec(array.shape, lambda *place: (0,) * array.ndim, pipeline_mode=pl.Buffered(1))


def held(rows, cols):
    return pl.BlockSpec((rows, cols), lambda *place: (0, 0), pipeline_mode=pl.Buffered(1))


def branch_kernel(attn_ref, tokens_ref, wout_ref, bout_ref, gain_ref, shift_ref, normed_ref, inverse_ref, low_ref):
    summed = tokens_ref[...].astype(FULL) + dot_nn(attn_ref[...], wout_ref[...]) + bout_ref[...]
    normed, inverse = norm_rows(summed)
    normed_ref[...] = normed
    inverse_ref[...] = inverse
    low_ref[...] = (normed * gain_ref[...] + shift_ref[...]).astype(LOW)


def out_columns(w_rise):
    return pl.BlockSpec((D, D), lambda *place: (0, w_rise.shape[1] // D - 1), pipeline_mode=pl.Buffered(1))


def branch(attn_rows, tokens, w_rise, b_out, gain, shift):
    rows = tokens.shape[0]
    strip = lambda cols: pl.BlockSpec((STRIP, cols), lambda i: (i, 0))
    return pl.pallas_call(
        branch_kernel,
        grid=(rows // STRIP,),
        in_specs=[strip(D), strip(D), out_columns(w_rise), fixed(b_out), fixed(gain), fixed(shift)],
        out_specs=[strip(D), strip(1), strip(D)],
        out_shape=[
            jax.ShapeDtypeStruct((rows, D), FULL), jax.ShapeDtypeStruct((rows, 1), FULL),
            jax.ShapeDtypeStruct((rows, D), LOW),
        ],
        compiler_params=pltpu.CompilerParams(vmem_limit_bytes=GRANT),
        cost_estimate=pl.CostEstimate(flops=WEIGHT * 4 * rows * D * D, bytes_accessed=rows * D * 10 + D * D * 2, transcendentals=0),
        name="branch",
    )(attn_rows, tokens, w_rise, b_out, gain, shift)


def widen_kernel(low_ref, wup_ref, bup_ref, hidden_ref, slope_ref):
    def strip(rows):
        point = dot_nn(low_ref[rows, :], wup_ref[...]) + bup_ref[...]
        hidden, slope = gelu_both(point)
        hidden_ref[rows, :] = hidden.astype(LOW)
        slope_ref[rows, :] = slope.astype(LOW)

    strips(low_ref.shape[0], strip)


def widen(first_low, w_up, b_up, first, last, before=()):
    rows, width = first_low.shape[0], b_up.shape[1]
    chunk = lambda height: pl.BlockSpec((height, WIDE), lambda i: (0, i + first))
    return continued(
        widen_kernel,
        before,
        grid=(last - first,),
        in_specs=[fixed(first_low), chunk(D), chunk(1)],
        out_specs=[chunk(rows), chunk(rows)],
        out_shape=[jax.ShapeDtypeStruct((rows, width), LOW)] * 2,
        compiler_params=pltpu.CompilerParams(vmem_limit_bytes=GRANT),
        cost_estimate=pl.CostEstimate(
            flops=WEIGHT * 6 * rows * D * WIDE * (last - first), bytes_accessed=WIDE * (last - first) * (D * 2 + rows * 4),
            transcendentals=rows * WIDE * (last - first)),
        name="widen",
    )(first_low, w_up, b_up)


def fall_kernel(hidden_ref, wdown_ref, normed_ref, cot_ref, bdown_ref, gain1_ref, shift1_ref, gain2_ref, shift2_ref,
                out_ref, second_ref, ffn_ref, sums_ref, total):
    step = pl.program_id(0)

    @pl.when(step == 0)
    def _():
        total[...] = dot_nn(hidden_ref[...], wdown_ref[...])

    @pl.when(step > 0)
    def _():
        total[...] += dot_nn(hidden_ref[...], wdown_ref[...])

    @pl.when(step == pl.num_programs(0) - 1)
    def _():
        sums_ref[...] = jnp.zeros_like(sums_ref)

        def finish(rows):
            first_out = normed_ref[rows, :] * gain1_ref[...] + shift1_ref[...]
            normed, inverse = norm_rows(first_out + total[rows, :] + bdown_ref[...])
            out_ref[rows, :] = (normed * gain2_ref[...] + shift2_ref[...]).astype(LOW)
            upstream = cot_ref[rows, :].astype(FULL)
            second = norm_back_rows(upstream * gain2_ref[...], normed, inverse)
            low = second.astype(LOW)
            second_ref[rows, :] = second
            ffn_ref[rows, :] = low
            sums_ref[...] += jnp.concatenate([
                jnp.sum(part, axis=0, keepdims=True) for part in (upstream * normed, upstream, low.astype(FULL))
            ], axis=0)

        strips(out_ref.shape[0], finish)


def fall(hidden, w_down, normed, cotangent, b_down, gain1, shift1, gain2, shift2, chunk=1024):
    rows, width = hidden.shape
    return pl.pallas_call(
        fall_kernel,
        grid=(width // chunk,),
        in_specs=[
            pl.BlockSpec((rows, chunk), lambda i: (0, i)), pl.BlockSpec((chunk, D), lambda i: (i, 0)),
        ] + [fixed(a) for a in (normed, cotangent, b_down, gain1, shift1, gain2, shift2)],
        out_specs=[held(rows, D), held(rows, D), held(rows, D), held(3, D)],
        out_shape=[
            jax.ShapeDtypeStruct((rows, D), LOW), jax.ShapeDtypeStruct((rows, D), FULL),
            jax.ShapeDtypeStruct((rows, D), LOW), jax.ShapeDtypeStruct((3, D), FULL),
        ],
        scratch_shapes=[pltpu.VMEM((rows, D), FULL)],
        compiler_params=pltpu.CompilerParams(vmem_limit_bytes=GRANT),
        cost_estimate=pl.CostEstimate(
            flops=WEIGHT * 2 * rows * D * width, bytes_accessed=rows * (D * 14 + width * 2) + D * width * 2, transcendentals=0),
        name="fall",
    )(hidden, w_down, normed, cotangent, b_down, gain1, shift1, gain2, shift2)


def narrow_kernel(ffn_ref, slope_ref, wdown_ref, wup_ref, so_far_ref, pre_ref, wide_ref, total_ref):
    @pl.when(pl.program_id(0) == 0)
    def _():
        total_ref[...] = so_far_ref[...]

    wide_ref[...] = jnp.zeros_like(wide_ref)

    def strip(rows):
        d_hidden = dot_nt(ffn_ref[rows, :], wdown_ref[...])
        d_pre = (slope_ref[rows, :].astype(FULL) * d_hidden).astype(LOW)
        pre_ref[rows, :] = d_pre
        wide_ref[...] += jnp.sum(d_pre.astype(FULL), axis=0, keepdims=True)
        total_ref[rows, :] += dot_nt(d_pre, wup_ref[...])

    strips(ffn_ref.shape[0], strip)


def narrow(d_ffn, slope, w_down, w_up, so_far, first, last):
    rows, width = slope.shape[0], WIDE * (last - first)
    own = lambda height: pl.BlockSpec((height, WIDE), lambda i: (0, i))
    chunk = lambda height: pl.BlockSpec((height, WIDE), lambda i: (0, i + first))
    return pl.pallas_call(
        narrow_kernel,
        grid=(last - first,),
        in_specs=[
            fixed(d_ffn), chunk(rows), pl.BlockSpec((WIDE, D), lambda i: (i + first, 0)), chunk(D), fixed(so_far),
        ],
        out_specs=[own(rows), own(1), held(rows, D)],
        out_shape=[
            jax.ShapeDtypeStruct((rows, width), LOW), jax.ShapeDtypeStruct((1, width), FULL),
            jax.ShapeDtypeStruct((rows, D), FULL),
        ],
        compiler_params=pltpu.CompilerParams(vmem_limit_bytes=GRANT),
        cost_estimate=pl.CostEstimate(
            flops=WEIGHT * 6 * rows * D * WIDE * (last - first), bytes_accessed=WIDE * (last - first) * (D * 4 + rows * 4) + rows * D * 10,
            transcendentals=0),
        name="narrow",
    )(d_ffn, slope, w_down, w_up, so_far)


def resid_kernel(first_ref, normed_ref, inverse_ref, gain_ref, wout_ref, resid_ref, branch_ref, attn_ref, sums_ref):
    d_first, normed = first_ref[...], normed_ref[...]
    resid = norm_back_rows(d_first * gain_ref[...], normed, inverse_ref[...])
    low = resid.astype(LOW)
    resid_ref[...] = resid
    branch_ref[...] = low
    attn_ref[...] = dot_nt(low, wout_ref[...]).astype(LOW)
    sums = jnp.concatenate([
        jnp.sum(part, axis=0, keepdims=True) for part in (d_first * normed, d_first, low.astype(FULL))
    ], axis=0)

    @pl.when(pl.program_id(0) == 0)
    def _():
        sums_ref[...] = sums

    @pl.when(pl.program_id(0) > 0)
    def _():
        sums_ref[...] += sums


def resid_back(d_first, normed, inverse, gain, w_rise):
    rows = d_first.shape[0]
    strip = lambda cols: pl.BlockSpec((STRIP, cols), lambda i: (i, 0))
    return pl.pallas_call(
        resid_kernel,
        grid=(rows // STRIP,),
        in_specs=[strip(D), strip(D), strip(1), fixed(gain), out_columns(w_rise)],
        out_specs=[strip(D), strip(D), strip(D), held(3, D)],
        out_shape=[
            jax.ShapeDtypeStruct((rows, D), FULL), jax.ShapeDtypeStruct((rows, D), LOW),
            jax.ShapeDtypeStruct((rows, D), LOW), jax.ShapeDtypeStruct((3, D), FULL),
        ],
        compiler_params=pltpu.CompilerParams(vmem_limit_bytes=GRANT),
        cost_estimate=pl.CostEstimate(flops=WEIGHT * 4 * rows * D * D, bytes_accessed=rows * D * 16 + D * D * 2, transcendentals=0),
        name="resid_back",
    )(d_first, normed, inverse, gain, w_rise)


def tall_kernel(left_ref, right_ref, keep_ref, send_ref, product):
    core = lax.axis_index("dp") & 1
    product[...] = dot_tn(left_ref[...], right_ref[...]).astype(LOW).reshape(product.shape)
    for pair in range(2):
        keep_ref[pair] = product[pair, core]
        send_ref[pair] = product[pair, 1 - core]


def outer_tall(left, right, count):
    rows, width = left.shape
    cols, part = right.shape[1], width // count
    out = pl.BlockSpec((2, part, cols), lambda i: (i, 0, 0))
    return pl.pallas_call(
        tall_kernel,
        grid=(count // 4,),
        in_specs=[pl.BlockSpec((rows, 4 * part), lambda i: (0, i)), fixed(right)],
        out_specs=[out, out],
        out_shape=[jax.ShapeDtypeStruct((count // 2, part, cols), LOW)] * 2,
        scratch_shapes=[pltpu.VMEM((2, 2, part, cols), LOW)],
        compiler_params=pltpu.CompilerParams(vmem_limit_bytes=GRANT),
        cost_estimate=pl.CostEstimate(
            flops=WEIGHT * 2 * rows * width * cols, bytes_accessed=2 * (rows * (width + cols) + width * cols), transcendentals=0),
        name="outer_tall",
    )(left, right)


def wide_kernel(starts, owners, *refs):
    lefts, rights, (keep, send, product) = refs[: max(owners) + 1], refs[max(owners) + 1 : -3], refs[-3:]
    step = pl.program_id(0)
    core = lax.axis_index("dp") & 1
    for owner, right, low, high in zip(owners, rights, starts, starts[1:]):
        left = lefts[owner]

        @pl.when((step >= low) & (step < high))
        def _():
            product[...] = dot_tn(left[...], right[...]).astype(LOW).reshape(product.shape)

    keep[...] = product[:, core]
    send[...] = product[:, 1 - core]


def outer_wide(lefts, rights, owners, count, weight=WEIGHT):
    rows, height = lefts[0].shape
    part = height // count
    starts = [0]
    for right in rights:
        starts.append(starts[-1] + right.shape[1] // WIDE)
    total = starts[-1]

    def strip(low, high):
        return pl.BlockSpec((rows, WIDE), lambda i: (0, jnp.clip(i - low, 0, high - low - 1)))

    out = pl.BlockSpec((count // 2, part, WIDE), lambda i: (0, 0, i))
    return pl.pallas_call(
        functools.partial(wide_kernel, starts, owners),
        grid=(total,),
        in_specs=[fixed(left) for left in lefts] + [strip(low, high) for low, high in zip(starts, starts[1:])],
        out_specs=[out, out],
        out_shape=[jax.ShapeDtypeStruct((count // 2, part, WIDE * total), LOW)] * 2,
        scratch_shapes=[pltpu.VMEM((count // 2, 2, part, WIDE), LOW)],
        compiler_params=pltpu.CompilerParams(vmem_limit_bytes=GRANT),
        cost_estimate=pl.CostEstimate(
            flops=weight * 2 * rows * height * WIDE * total,
            bytes_accessed=2 * (rows * (height * len(lefts) + WIDE * total) + height * WIDE * total), transcendentals=0),
        name="outer_wide",
    )(*lefts, *rights)


def spread_kernel(pairs, so_far_ref, *refs):
    total = so_far_ref[...]
    for grad, weight in zip(refs[:pairs], refs[pairs:-1]):
        total = total + dot_nt(grad[...], weight[...])
    refs[-1][...] = total.astype(refs[-1].dtype)


def spread(so_far, grads, weights, kind):
    rows = so_far.shape[0]
    strip = pl.BlockSpec((STRIP, D), lambda i: (i, 0))
    return pl.pallas_call(
        functools.partial(spread_kernel, len(grads)),
        grid=(rows // STRIP,),
        in_specs=[strip] * (1 + len(grads)) + [fixed(weight) for weight in weights],
        out_specs=strip,
        out_shape=jax.ShapeDtypeStruct((rows, D), kind),
        compiler_params=pltpu.CompilerParams(vmem_limit_bytes=32 * MIB),
        cost_estimate=pl.CostEstimate(
            flops=WEIGHT * 2 * rows * D * D * len(grads), bytes_accessed=rows * D * 10 + D * D * 2 * len(grads),
            transcendentals=0),
        name="spread",
    )(so_far, *grads, *weights)


FLIPS = {"c": 1, "x": 2, "y": 4}


def hop(array, dim, count):
    if dim in FLIPS:
        return lax.ppermute(array, "dp", [(place, place ^ FLIPS[dim]) for place in range(count)])
    step = 8 * (1 if dim == "z" else dim)
    return lax.ppermute(array, "dp", [(place, (place + step) % count) for place in range(count)])


def after(value, *earlier):
    return lax.optimization_barrier((value, earlier))[0] if earlier else value


def mine_of():
    me = lax.axis_index("dp")
    return {
        "z": lax.shift_right_logical(me, 3),
        "y": lax.shift_right_logical(me, 2) & 1,
        "x": lax.shift_right_logical(me, 1) & 1,
        "c": me & 1,
    }


def place_kernel(count, cut, bases, rows, *refs):
    pieces, outs = refs[:8], refs[8:]
    ring = count // 8
    mine = mine_of()
    slot = pl.program_id(0)
    for part, (last, low_dim) in enumerate((("x", "y"), ("y", "x"))):
        left, right = (0, cut) if part == 0 else (cut, bases[-1])
        for which in range(4):
            digits = {"c": which // 2, last: which % 2, low_dim: lax.div(slot, ring)}
            owner = lax.rem(mine["z"] + ring - lax.rem(slot, ring), ring) * 8
            for dim, weight in (("y", 4), ("x", 2), ("c", 1)):
                owner = owner + weight * (mine[dim] ^ digits[dim])
            row = pl.ds(pl.multiple_of(owner * rows, rows), rows)
            for out, base, stop in zip(outs, bases, bases[1:]):
                low, high = max(left, base), min(right, stop)
                if low < high:
                    out[row, low - base : high - base] = pieces[4 * part + which][0, :, low - left : high - left]


def whole_arrays(shard, widths):
    full = lax.all_gather(shard, "dp", axis=0, tiled=True)
    bases = [sum(widths[:index]) for index in range(len(widths) + 1)]
    return [full[:, low:high] for low, high in zip(bases, bases[1:])]


class Gathering:
    def __init__(self, shard, cut, count):
        self.count, self.cut = count, cut
        self.rows, self.cols = shard.shape
        self.stacks, self.came, self.stage = [shard[None]], [], 0

    def move(self, *gate):
        self.stage += 1
        if self.stage <= 3:
            if self.stage == 2:
                whole = jnp.concatenate(self.stacks + self.came, axis=0)
                self.stacks = [whole[:, :, : self.cut], whole[:, :, self.cut :]]
            elif self.stage == 3:
                self.stacks = [jnp.concatenate(pair, axis=0) for pair in zip(self.stacks, self.came)]
        self.stacks = [after(stack, *gate) for stack in self.stacks]
        if self.stage == 1:
            self.came = [hop(self.stacks[0], distance, self.count) for distance in range(1, self.count // 8)]
        elif self.stage <= 3:
            dims = "yx" if self.stage == 2 else "xy"
            self.came = [hop(stack, dim, self.count) for stack, dim in zip(self.stacks, dims)]
        else:
            self.stacks = [(stack, came) for stack, came in zip(self.stacks, self.came)]
            self.came = [tuple(hop(after(array, *gate), "c", self.count) for array in pair) for pair in self.stacks]
            return [array for pair in self.stacks for array in pair]
        return self.stacks

    def result(self, widths):
        pieces = [array for own, came in zip(self.stacks, self.came) for array in own + came]
        bases = [sum(widths[:index]) for index in range(len(widths) + 1)]
        size = self.count * self.rows
        return pl.pallas_call(
            functools.partial(place_kernel, self.count, self.cut, bases, self.rows),
            grid=(self.count // 4,),
            in_specs=[pl.BlockSpec((1, self.rows, piece.shape[2]), lambda i: (i, 0, 0)) for piece in pieces],
            out_specs=[held(size, width) for width in widths],
            out_shape=[jax.ShapeDtypeStruct((size, width), LOW) for width in widths],
            compiler_params=pltpu.CompilerParams(vmem_limit_bytes=GRANT),
            cost_estimate=pl.CostEstimate(flops=0, bytes_accessed=4 * size * bases[-1], transcendentals=0),
            name="place",
        )(*pieces)


def add_low(left_side, right_side, kind=LOW):
    return (left_side.astype(FULL) + right_side.astype(FULL)).astype(kind)


def take(blocks, axis, index):
    return lax.dynamic_index_in_dim(blocks, index, axis, keepdims=False, allow_negative_indices=False)


def split_kernel(cut, keep_ref, came_ref, keep1_ref, send1_ref, keep2_ref, send2_ref):
    mine = mine_of()
    for side in range(2):
        for keep, send, dim, cols in (
            (keep1_ref, send1_ref, "x", slice(0, cut)),
            (keep2_ref, send2_ref, "y", slice(cut, None)),
        ):
            for out, index in ((keep, mine[dim]), (send, 1 - mine[dim])):
                where = (0, side, index, slice(None), cols) if dim == "x" else (0, index, side, slice(None), cols)
                out[0, side] = add_low(keep_ref[where], came_ref[where])


def turn_kernel(keep1_ref, came1_ref, keep2_ref, came2_ref, keep3_ref, send3_ref, keep4_ref, send4_ref):
    mine = mine_of()
    for kept, came, keep, send, dim in (
        (keep1_ref, came1_ref, keep3_ref, send3_ref, "y"),
        (keep2_ref, came2_ref, keep4_ref, send4_ref, "x"),
    ):
        for out, index in ((keep, mine[dim]), (send, 1 - mine[dim])):
            out[...] = add_low(kept[:, index], came[:, index])


def tower_kernel(cut, keep3_ref, came3_ref, keep4_ref, came4_ref, *outs):
    own = mine_of()["z"]
    ring = keep3_ref.shape[0]
    for distance, out in enumerate(outs):
        index = lax.rem(own + distance, ring)
        out[:, :cut] = add_low(keep3_ref[index], came3_ref[index])
        out[:, cut:] = add_low(keep4_ref[index], came4_ref[index])


def local_kernel(kernel, name, outs, grid, in_specs, out_specs, operands):
    size = sum(array.size * array.dtype.itemsize for array in operands)
    return pl.pallas_call(
        kernel,
        grid=grid,
        in_specs=in_specs,
        out_specs=out_specs,
        out_shape=outs,
        compiler_params=pltpu.CompilerParams(vmem_limit_bytes=GRANT),
        cost_estimate=pl.CostEstimate(flops=0, bytes_accessed=2 * size, transcendentals=0),
        name=name,
    )(*operands)


class Sums:
    def __init__(self, keep, send, count):
        self.count, self.ring = count, count // 8
        self.rows, self.cols = keep.shape[1:]
        self.cut = self.cols // 2
        self.stage = 0
        self.keeps, self.sends, self.dims = [keep], [send], ["c"]

    def start(self):
        self.came = [hop(send, dim, self.count) for send, dim in zip(self.sends, self.dims)]
        return self.sends

    def move(self, *gate):
        came = [after(array, *gate) for array in self.came]
        ring, rows, cut, rest = self.ring, self.rows, self.cut, self.cols - self.cut
        self.stage += 1
        if self.stage == 1:
            whole = lambda array: array.reshape(ring, 2, 2, rows, self.cols)
            block = pl.BlockSpec((1, 2, 2, rows, self.cols), lambda i: (i, 0, 0, 0, 0))
            widths = (cut, cut, rest, rest)
            self.pairs(local_kernel(
                functools.partial(split_kernel, cut), "split",
                [jax.ShapeDtypeStruct((ring, 2, rows, width), LOW) for width in widths], (ring,), [block] * 2,
                [pl.BlockSpec((1, 2, rows, width), lambda i: (i, 0, 0, 0)) for width in widths],
                [whole(self.keeps[0]), whole(came[0])],
            ), ["x", "y"])
        elif self.stage == 2:
            operands = [self.keeps[0], came[0], self.keeps[1], came[1]]
            self.pairs(local_kernel(
                turn_kernel, "turn",
                [jax.ShapeDtypeStruct((ring, rows, width), LOW) for width in (cut, cut, rest, rest)], (ring,),
                [pl.BlockSpec((1,) + array.shape[1:], lambda i: (i, 0, 0, 0)) for array in operands],
                [pl.BlockSpec((1, rows, width), lambda i: (i, 0, 0)) for width in (cut, cut, rest, rest)],
                operands,
            ), ["y", "x"])
        elif self.stage == 3:
            operands = [self.keeps[0], came[0], self.keeps[1], came[1]]
            outs = local_kernel(
                functools.partial(tower_kernel, cut), "tower",
                [jax.ShapeDtypeStruct((rows, self.cols), LOW)] * ring, (1,),
                [fixed(array) for array in operands], [held(rows, self.cols)] * ring, operands,
            )
            self.keeps, self.sends, self.dims = list(outs[:1]), list(outs[1:]), list(range(1, ring))
        else:
            self.total = self.keeps[0].astype(FULL)
            for array in came:
                self.total = self.total + array.astype(FULL)
            return [self.total]
        return self.start()

    def pairs(self, arrays, dims):
        self.keeps, self.sends, self.dims = [arrays[0], arrays[2]], [arrays[1], arrays[3]], dims


class EverySum:
    def __init__(self, rows, count):
        self.count, self.todo = count, ["c", "x", "y"]
        self.sent = [rows]
        self.came = [hop(rows, "c", count)]

    def move(self, *gate):
        came = [after(array, *gate) for array in self.came]
        self.sent = [functools.reduce(jnp.add, came, self.sent[0])]
        self.todo = self.todo[1:]
        dims = self.todo[:1] or list(range(1, self.count // 8))
        if self.came and len(self.came) == 1:
            self.came = [hop(self.sent[0], dim, self.count) for dim in dims]
        return self.sent


def local(
    tokens,
    w_query,
    w_key,
    w_value,
    w_out,
    w_up,
    w_down,
    b_query,
    b_value,
    b_out,
    b_up,
    b_down,
    gain_attn,
    shift_attn,
    gain_ffn,
    shift_ffn,
    cotangent,
):
    count = D // w_query.shape[0]
    part = D // count
    wide = w_up.shape[1]
    custom = count == 32
    small = (b_query, b_value, b_out, b_down, gain_attn, shift_attn, gain_ffn, shift_ffn)
    packed = sum(
        jnp.pad(array[None], ((row, 15 - row), (0, 128 - array.shape[0]))) for row, array in enumerate(small + (b_up,))
    )
    height = max(part, 16)
    tops = [jnp.pad(array, ((0, height - part), (0, 0))) for array in (w_query, w_key, w_value)]
    early = jnp.concatenate(tops + [jnp.pad(packed, ((0, height - 16), (0, 0)))], axis=1)
    widths = (D, D, D, 128)
    w_rise = jnp.concatenate([w_up, w_out], axis=1)
    if custom:
        first_gather = Gathering(early, 3 * D // 2 + 128, count)
        for stage in range(4):
            first_gather.move()
            if stage == 1:
                w_rise = after(w_rise, *first_gather.stacks)
        w_query, w_key, w_value, packed = first_gather.result(widths)
    else:
        w_query, w_key, w_value, packed = whole_arrays(early, widths)
    if height > part:
        w_query, w_key, w_value = [
            array.reshape(count, height, D)[:, :part].reshape(D, D) for array in (w_query, w_key, w_value)
        ]
    w_rise = lax.all_gather(w_rise, "dp", axis=0, tiled=True)
    packed = packed.reshape(count, height, 128)
    vector = lambda row: packed[:, row, :part].reshape(1, D).astype(FULL)
    b_query, b_value, b_out, b_down, gain_attn, shift_attn, gain_ffn, shift_ffn = map(vector, range(8))
    b_up = packed[:, 8, : wide // count].reshape(1, wide).astype(FULL)
    chunks = wide // WIDE
    sequences = tokens.shape[0] // LEN

    down_gather = Gathering(w_down, D // 2, count) if custom else None

    def under(value, *gate):
        return after(value, *down_gather.move(*gate)) if custom else value

    tokens_in = under(tokens, w_query)
    queries = (dot_nn(tokens_in, w_query) + b_query).astype(LOW)
    keys = dot_nn(tokens_in, w_key).astype(LOW)
    values = (dot_nn(tokens_in, w_value) + b_value).astype(LOW)
    seen = attend(queries, keys, values, 0)
    values = under(values, seen[1])
    for sequence in range(1, sequences):
        seen = attend(queries, keys, values, sequence, seen)
    probs, attn_rows = seen
    attn_rows = under(attn_rows, attn_rows)
    normed, inverse, first_low = branch(attn_rows, tokens, w_rise, b_out, gain_attn, shift_attn)
    half = widen(first_low, w_rise, b_up, 0, chunks // 2)
    half_low = under(first_low, half[0])
    hidden, slope = widen(half_low, w_rise, b_up, chunks // 2, chunks, half)
    if custom:
        (w_down,) = down_gather.result((D,))
    else:
        w_down = lax.all_gather(w_down, "dp", axis=0, tiled=True)
    result, second, d_ffn, sums_ffn = fall(
        hidden, w_down, normed, cotangent, b_down, gain_attn, shift_attn, gain_ffn, shift_ffn
    )

    if custom:
        down = Sums(*outer_tall(hidden, d_ffn, count), count)
        second = after(second, *down.start())
    pre_1, wide_1, d_first = narrow(d_ffn, slope, w_down, w_rise, second, 0, 2)
    if custom:
        d_first = after(d_first, *down.move(wide_1))
    pre_2, wide_2, d_first = narrow(d_ffn, slope, w_down, w_rise, d_first, 2, chunks)
    if custom:
        d_first = after(d_first, *down.move(wide_2))
    d_resid, d_branch, d_attn, sums_attn = resid_back(d_first, normed, inverse, gain_attn, w_rise)
    if custom:
        d_branch = after(d_branch, *down.move(sums_attn))
        up = Sums(*outer_wide([first_low, attn_rows], [pre_1, pre_2, d_branch], (0, 0, 1), count), count)
        d_attn = after(d_attn, *up.start())
        d_attn = after(d_attn, *down.move(*up.keeps))
    seen = attend_back(queries, keys, values, probs, d_attn, 0)
    if custom:
        d_attn = after(d_attn, *up.move(seen[0]))
    for sequence in range(1, sequences):
        seen = attend_back(queries, keys, values, probs, d_attn, sequence, seen)
    d_queries, d_keys, d_values = seen
    column_sum = lambda rows: jnp.sum(rows.astype(FULL), axis=0, keepdims=True)
    sums = jnp.concatenate([
        column_sum(d_queries), column_sum(d_values), sums_attn[2:], sums_ffn[2:], sums_attn[:2], sums_ffn[:2],
        jnp.concatenate([wide_1, wide_2], axis=1).reshape(-1, D),
    ], axis=0)
    if custom:
        sums = EverySum(sums, count)
        d_queries = after(d_queries, *sums.sent)
        first = Sums(*outer_wide([tokens], [d_queries, d_keys, d_values], (0, 0, 0), count, 0), count)
        d_queries = after(d_queries, *first.start())
        d_queries = after(d_queries, *up.move(*first.keeps))
        d_queries = after(d_queries, *sums.move(*first.keeps))
    grad_rows = spread(d_resid, [d_queries], [w_query], FULL)
    if custom:
        grad_rows = after(grad_rows, *first.move(grad_rows))
        grad_rows = after(grad_rows, *sums.move(grad_rows))
    grad_rows = spread(grad_rows, [d_keys, d_values], [w_key, w_value], LOW)

    if custom:
        up.move(grad_rows)
        first.move(grad_rows)
        sums.move(grad_rows)
        first.move()
        sums = sums.move()[0]
        up.move()
        first.move()
        d_w_down, second, first = down.total, up.total, first.total
        d_w_up, d_w_out = second[:, :wide], second[:, wide:]
        d_w_query, d_w_key, d_w_value = first[:, :D], first[:, D : 2 * D], first[:, 2 * D :]
    else:
        total = lambda grad: lax.psum_scatter(grad.astype(LOW), "dp", scatter_dimension=0, tiled=True).astype(FULL)
        d_w_down = total(dot_tn(hidden, d_ffn))
        d_w_up = total(jnp.concatenate([dot_tn(first_low, pre) for pre in (pre_1, pre_2)], axis=1))
        d_w_out = total(dot_tn(attn_rows, d_branch))
        d_w_query, d_w_key, d_w_value = [total(dot_tn(tokens, grad)) for grad in (d_queries, d_keys, d_values)]
        sums = lax.psum(sums, "dp")
    me = lax.axis_index("dp")
    own = lax.dynamic_slice_in_dim(sums[:8], me * part, part, axis=1, allow_negative_indices=False)
    vector = lambda row: own[row]
    d_b_up = lax.dynamic_slice_in_dim(
        sums[8:].reshape(-1), me * (wide // count), wide // count, allow_negative_indices=False
    )
    return (
        result,
        grad_rows,
        d_w_query,
        d_w_key,
        d_w_value,
        d_w_out,
        d_w_up,
        d_w_down,
        vector(0),
        vector(1),
        vector(2),
        d_b_up,
        vector(3),
        vector(4),
        vector(5),
        vector(6),
        vector(7),
    )


def solution(mesh):
    placed = (
        P("dp", None),
        P("dp", None),
        P("dp", None),
        P("dp", None),
        P("dp", None),
        P("dp", None),
        P("dp", None),
        P("dp"),
        P("dp"),
        P("dp"),
        P("dp"),
        P("dp"),
        P("dp"),
        P("dp"),
        P("dp"),
        P("dp"),
        P("dp", None),
    )
    return jax.shard_map(
        local,
        mesh=mesh,
        in_specs=placed,
        out_specs=(
            P("dp", None),
            P("dp", None),
            P("dp", None),
            P("dp", None),
            P("dp", None),
            P("dp", None),
            P("dp", None),
            P("dp", None),
            P("dp"),
            P("dp"),
            P("dp"),
            P("dp"),
            P("dp"),
            P("dp"),
            P("dp"),
            P("dp"),
            P("dp"),
        ),
        check_vma=False,
    )
```

```python
import functools
import jax
import jax.numpy as jnp
from jax import lax
from jax.experimental import pallas as pl
from jax.experimental.pallas import tpu as pltpu
from jax.sharding import PartitionSpec as P

D = 1024
HEADS = 16
LEN = 512
EPS = 1e-12
LOW = jnp.bfloat16
FULL = jnp.float32
MIB = 1024 * 1024
WIDE = 512
STRIP = 256
GRANT = 58 * MIB
WEIGHT = 16


def dot_nn(left_side, right_side):
    return lax.dot_general(left_side, right_side, (((1,), (0,)), ((), ())), preferred_element_type=FULL)


def dot_nt(left_side, right_side):
    return lax.dot_general(left_side, right_side, (((1,), (1,)), ((), ())), preferred_element_type=FULL)


def dot_tn(left_side, right_side):
    return lax.dot_general(left_side, right_side, (((0,), (0,)), ((), ())), preferred_element_type=FULL)


def head_mask(rows, head):
    lane = lax.broadcasted_iota(jnp.int32, (rows, 128), 1)
    return (lane // 64) == head


def attend_kernel(q_ref, k_ref, v_ref, probs_ref, rows_ref):
    scale = (D // HEADS) ** -0.5
    queries = (q_ref[...].astype(FULL) * scale).astype(LOW)
    keys, values = k_ref[...], v_ref[...]
    mixed = jnp.zeros((LEN, 128), FULL)
    for head in range(2):
        mask = head_mask(LEN, head)
        zero = jnp.zeros((), LOW)
        scores = dot_nt(queries, jnp.where(mask, keys, zero))
        maxima = jnp.max(scores, axis=-1, keepdims=True)
        exponent = jnp.exp(scores - maxima)
        total = jnp.sum(exponent, axis=-1, keepdims=True)
        probs = (exponent * (1.0 / total)).astype(LOW)
        probs_ref[0, head] = probs
        mixed = mixed + dot_nn(probs, jnp.where(mask, values, zero))
    rows_ref[...] = mixed.astype(LOW)


def placed(kernel, ins, count, *refs):
    kernel(*refs[:ins], *refs[ins + count :])


def continued(kernel, before, in_specs, out_specs, out_shape, **rest):
    aliases = {}
    if before:
        count = len(before)
        kernel = functools.partial(placed, kernel, len(in_specs), count)
        aliases = {len(in_specs) + index: index for index in range(count)}
        in_specs = list(in_specs) + [pl.BlockSpec(memory_space=pl.ANY)] * count
    call = pl.pallas_call(
        kernel, in_specs=in_specs, out_specs=out_specs, out_shape=out_shape, input_output_aliases=aliases, **rest
    )
    return lambda *operands: call(*operands, *before)


def attend(queries, keys, values, sequence, before=()):
    rows = queries.shape[0]
    column = pl.BlockSpec((LEN, 128), lambda p: (sequence, p))
    return continued(
        attend_kernel,
        before,
        grid=(HEADS // 2,),
        in_specs=[column] * 3,
        out_specs=[pl.BlockSpec((1, 2, LEN, LEN), lambda p: (sequence, p, 0, 0)), column],
        out_shape=[
            jax.ShapeDtypeStruct((rows // LEN, HEADS, LEN, LEN), LOW),
            jax.ShapeDtypeStruct((rows, D), LOW),
        ],
        compiler_params=pltpu.CompilerParams(vmem_limit_bytes=GRANT),
        cost_estimate=pl.CostEstimate(
            flops=12 * HEADS * LEN * LEN * 256, bytes_accessed=HEADS * LEN * LEN * 2 + LEN * D * 8,
            transcendentals=HEADS * LEN * LEN),
        name="attend",
    )(queries, keys, values)


def attend_back_kernel(q_ref, k_ref, v_ref, probs_ref, grad_ref, dq_ref, dk_ref, dv_ref):
    scale = (D // HEADS) ** -0.5
    queries, keys, values, grads = q_ref[...], k_ref[...], v_ref[...], grad_ref[...]
    zero = jnp.zeros((), LOW)
    d_queries = jnp.zeros((LEN, 128), FULL)
    d_keys = jnp.zeros((128, LEN), FULL)
    d_values = jnp.zeros((128, LEN), FULL)
    for head in range(2):
        mask = head_mask(LEN, head)
        probs = probs_ref[0, head]
        own_grads = jnp.where(mask, grads, zero)
        d_probs = dot_nt(own_grads, values).astype(LOW).astype(FULL)
        wide = probs.astype(FULL)
        product = d_probs * wide
        total = jnp.sum(product, axis=-1, keepdims=True)
        d_scores = (product - wide * total).astype(LOW)
        d_queries = d_queries + dot_nn(d_scores, jnp.where(mask, keys, zero))
        d_keys = d_keys + dot_tn(jnp.where(mask, queries, zero), d_scores)
        d_values = d_values + dot_tn(own_grads, probs)
    dq_ref[...] = (scale * d_queries).astype(LOW)
    dk_ref[...] = (scale * d_keys.T).astype(LOW)
    dv_ref[...] = d_values.T.astype(LOW)


def attend_back(queries, keys, values, probs, grads, sequence, before=()):
    rows = queries.shape[0]
    column = pl.BlockSpec((LEN, 128), lambda p: (sequence, p))
    return continued(
        attend_back_kernel,
        before,
        grid=(HEADS // 2,),
        in_specs=[column, column, column, pl.BlockSpec((1, 2, LEN, LEN), lambda p: (sequence, p, 0, 0)), column],
        out_specs=[column] * 3,
        out_shape=[jax.ShapeDtypeStruct((rows, D), LOW)] * 3,
        compiler_params=pltpu.CompilerParams(vmem_limit_bytes=GRANT),
        cost_estimate=pl.CostEstimate(
            flops=WEIGHT * 12 * HEADS * LEN * LEN * 256, bytes_accessed=HEADS * LEN * LEN * 2 + LEN * D * 14, transcendentals=0),
        name="attend_back",
    )(queries, keys, values, probs, grads)


def gelu_both(point):
    bell = jnp.exp(point * point * -0.5)
    ratio = 1.0 / (1.0 + (0.3275911 * 0.5**0.5) * jnp.abs(point))
    series = 0.5 * 1.061405429
    for factor in (-1.453152027, 1.421413741, -0.284496736, 0.254829592):
        series = series * ratio + 0.5 * factor
    below = series * ratio * bell
    normal = jnp.where(point < 0, below, 1.0 - below)
    return point * normal, normal + point * bell * 0.3989422804014327


def norm_rows(summed):
    centered = summed - jnp.mean(summed, axis=-1, keepdims=True)
    inverse = lax.rsqrt(jnp.mean(centered * centered, axis=-1, keepdims=True) + EPS)
    return centered * inverse, inverse


def norm_back_rows(scaled, normed, inverse):
    mean_grad = jnp.mean(scaled, axis=-1, keepdims=True)
    mean_cross = jnp.mean(scaled * normed, axis=-1, keepdims=True)
    return inverse * (scaled - mean_grad - normed * mean_cross)


def strips(rows, body):
    def step(index, carry):
        body(pl.ds(pl.multiple_of(index * STRIP, STRIP), STRIP))
        return carry

    lax.fori_loop(0, rows // STRIP, step, 0)


def fixed(array):
    return pl.BlockSpec(array.shape, lambda *place: (0,) * array.ndim, pipeline_mode=pl.Buffered(1))


def held(rows, cols):
    return pl.BlockSpec((rows, cols), lambda *place: (0, 0), pipeline_mode=pl.Buffered(1))


def branch_kernel(attn_ref, tokens_ref, wout_ref, bout_ref, gain_ref, shift_ref, normed_ref, inverse_ref, low_ref):
    summed = tokens_ref[...].astype(FULL) + dot_nn(attn_ref[...], wout_ref[...]) + bout_ref[...]
    normed, inverse = norm_rows(summed)
    normed_ref[...] = normed
    inverse_ref[...] = inverse
    low_ref[...] = (normed * gain_ref[...] + shift_ref[...]).astype(LOW)


def out_columns(w_rise):
    return pl.BlockSpec((D, D), lambda *place: (0, w_rise.shape[1] // D - 1), pipeline_mode=pl.Buffered(1))


def branch(attn_rows, tokens, w_rise, b_out, gain, shift):
    rows = tokens.shape[0]
    strip = lambda cols: pl.BlockSpec((STRIP, cols), lambda i: (i, 0))
    return pl.pallas_call(
        branch_kernel,
        grid=(rows // STRIP,),
        in_specs=[strip(D), strip(D), out_columns(w_rise), fixed(b_out), fixed(gain), fixed(shift)],
        out_specs=[strip(D), strip(1), strip(D)],
        out_shape=[
            jax.ShapeDtypeStruct((rows, D), FULL), jax.ShapeDtypeStruct((rows, 1), FULL),
            jax.ShapeDtypeStruct((rows, D), LOW),
        ],
        compiler_params=pltpu.CompilerParams(vmem_limit_bytes=GRANT),
        cost_estimate=pl.CostEstimate(flops=WEIGHT * 4 * rows * D * D, bytes_accessed=rows * D * 10 + D * D * 2, transcendentals=0),
        name="branch",
    )(attn_rows, tokens, w_rise, b_out, gain, shift)


def widen_kernel(low_ref, wup_ref, bup_ref, hidden_ref, slope_ref):
    hidden, slope = gelu_both(dot_nn(low_ref[...], wup_ref[...]) + bup_ref[...])
    hidden_ref[...] = hidden.astype(LOW)
    slope_ref[...] = slope.astype(LOW)


def widen(first_low, w_up, b_up, first, last, before=()):
    rows, width = first_low.shape[0], b_up.shape[1]
    chunk = lambda height: pl.BlockSpec((height, WIDE), lambda i: (0, i + first))
    return continued(
        widen_kernel,
        before,
        grid=(last - first,),
        in_specs=[fixed(first_low), chunk(D), chunk(1)],
        out_specs=[chunk(rows), chunk(rows)],
        out_shape=[jax.ShapeDtypeStruct((rows, width), LOW)] * 2,
        compiler_params=pltpu.CompilerParams(vmem_limit_bytes=GRANT),
        cost_estimate=pl.CostEstimate(
            flops=WEIGHT * 6 * rows * D * WIDE * (last - first), bytes_accessed=WIDE * (last - first) * (D * 2 + rows * 4),
            transcendentals=rows * WIDE * (last - first)),
        name="widen",
    )(first_low, w_up, b_up)


def fall_kernel(hidden_ref, wdown_ref, normed_ref, cot_ref, bdown_ref, gain1_ref, shift1_ref, gain2_ref, shift2_ref,
                out_ref, second_ref, ffn_ref, sums_ref, total):
    step = pl.program_id(0)

    @pl.when(step == 0)
    def _():
        total[...] = dot_nn(hidden_ref[...], wdown_ref[...])

    @pl.when(step > 0)
    def _():
        total[...] += dot_nn(hidden_ref[...], wdown_ref[...])

    @pl.when(step == pl.num_programs(0) - 1)
    def _():
        sums_ref[...] = jnp.zeros_like(sums_ref)

        def finish(rows):
            first_out = normed_ref[rows, :] * gain1_ref[...] + shift1_ref[...]
            normed, inverse = norm_rows(first_out + total[rows, :] + bdown_ref[...])
            out_ref[rows, :] = (normed * gain2_ref[...] + shift2_ref[...]).astype(LOW)
            upstream = cot_ref[rows, :].astype(FULL)
            second = norm_back_rows(upstream * gain2_ref[...], normed, inverse)
            low = second.astype(LOW)
            second_ref[rows, :] = second
            ffn_ref[rows, :] = low
            sums_ref[...] += jnp.concatenate([
                jnp.sum(part, axis=0, keepdims=True) for part in (upstream * normed, upstream, low.astype(FULL))
            ], axis=0)

        strips(out_ref.shape[0], finish)


def fall(hidden, w_down, normed, cotangent, b_down, gain1, shift1, gain2, shift2, chunk=1024):
    rows, width = hidden.shape
    return pl.pallas_call(
        fall_kernel,
        grid=(width // chunk,),
        in_specs=[
            pl.BlockSpec((rows, chunk), lambda i: (0, i)), pl.BlockSpec((chunk, D), lambda i: (i, 0)),
        ] + [fixed(a) for a in (normed, cotangent, b_down, gain1, shift1, gain2, shift2)],
        out_specs=[held(rows, D), held(rows, D), held(rows, D), held(3, D)],
        out_shape=[
            jax.ShapeDtypeStruct((rows, D), LOW), jax.ShapeDtypeStruct((rows, D), FULL),
            jax.ShapeDtypeStruct((rows, D), LOW), jax.ShapeDtypeStruct((3, D), FULL),
        ],
        scratch_shapes=[pltpu.VMEM((rows, D), FULL)],
        compiler_params=pltpu.CompilerParams(vmem_limit_bytes=GRANT),
        cost_estimate=pl.CostEstimate(
            flops=WEIGHT * 2 * rows * D * width, bytes_accessed=rows * (D * 14 + width * 2) + D * width * 2, transcendentals=0),
        name="fall",
    )(hidden, w_down, normed, cotangent, b_down, gain1, shift1, gain2, shift2)


def narrow_kernel(ffn_ref, slope_ref, wdown_ref, wup_ref, so_far_ref, pre_ref, wide_ref, total_ref):
    d_hidden = dot_nt(ffn_ref[...], wdown_ref[...])
    d_pre = (slope_ref[...].astype(FULL) * d_hidden).astype(LOW)
    pre_ref[...] = d_pre
    wide_ref[...] = jnp.sum(d_pre.astype(FULL), axis=0, keepdims=True)
    step = dot_nt(d_pre, wup_ref[...])

    @pl.when(pl.program_id(0) == 0)
    def _():
        total_ref[...] = so_far_ref[...] + step

    @pl.when(pl.program_id(0) > 0)
    def _():
        total_ref[...] += step


def narrow(d_ffn, slope, w_down, w_up, so_far, first, last):
    rows, width = slope.shape[0], WIDE * (last - first)
    own = lambda height: pl.BlockSpec((height, WIDE), lambda i: (0, i))
    chunk = lambda height: pl.BlockSpec((height, WIDE), lambda i: (0, i + first))
    return pl.pallas_call(
        narrow_kernel,
        grid=(last - first,),
        in_specs=[
            fixed(d_ffn), chunk(rows), pl.BlockSpec((WIDE, D), lambda i: (i + first, 0)), chunk(D), fixed(so_far),
        ],
        out_specs=[own(rows), own(1), held(rows, D)],
        out_shape=[
            jax.ShapeDtypeStruct((rows, width), LOW), jax.ShapeDtypeStruct((1, width), FULL),
            jax.ShapeDtypeStruct((rows, D), FULL),
        ],
        compiler_params=pltpu.CompilerParams(vmem_limit_bytes=GRANT),
        cost_estimate=pl.CostEstimate(
            flops=WEIGHT * 6 * rows * D * WIDE * (last - first), bytes_accessed=WIDE * (last - first) * (D * 4 + rows * 4) + rows * D * 10,
            transcendentals=0),
        name="narrow",
    )(d_ffn, slope, w_down, w_up, so_far)


def resid_kernel(first_ref, normed_ref, inverse_ref, gain_ref, wout_ref, resid_ref, branch_ref, attn_ref, sums_ref):
    d_first, normed = first_ref[...], normed_ref[...]
    resid = norm_back_rows(d_first * gain_ref[...], normed, inverse_ref[...])
    low = resid.astype(LOW)
    resid_ref[...] = resid
    branch_ref[...] = low
    attn_ref[...] = dot_nt(low, wout_ref[...]).astype(LOW)
    sums = jnp.concatenate([
        jnp.sum(part, axis=0, keepdims=True) for part in (d_first * normed, d_first, low.astype(FULL))
    ], axis=0)

    @pl.when(pl.program_id(0) == 0)
    def _():
        sums_ref[...] = sums

    @pl.when(pl.program_id(0) > 0)
    def _():
        sums_ref[...] += sums


def resid_back(d_first, normed, inverse, gain, w_rise):
    rows = d_first.shape[0]
    strip = lambda cols: pl.BlockSpec((STRIP, cols), lambda i: (i, 0))
    return pl.pallas_call(
        resid_kernel,
        grid=(rows // STRIP,),
        in_specs=[strip(D), strip(D), strip(1), fixed(gain), out_columns(w_rise)],
        out_specs=[strip(D), strip(D), strip(D), held(3, D)],
        out_shape=[
            jax.ShapeDtypeStruct((rows, D), FULL), jax.ShapeDtypeStruct((rows, D), LOW),
            jax.ShapeDtypeStruct((rows, D), LOW), jax.ShapeDtypeStruct((3, D), FULL),
        ],
        compiler_params=pltpu.CompilerParams(vmem_limit_bytes=GRANT),
        cost_estimate=pl.CostEstimate(flops=WEIGHT * 4 * rows * D * D, bytes_accessed=rows * D * 16 + D * D * 2, transcendentals=0),
        name="resid_back",
    )(d_first, normed, inverse, gain, w_rise)


def tall_kernel(left_ref, right_ref, keep_ref, send_ref, product):
    core = lax.axis_index("dp") & 1
    product[...] = dot_tn(left_ref[...], right_ref[...]).astype(LOW).reshape(product.shape)
    for pair in range(2):
        keep_ref[pair] = product[pair, core]
        send_ref[pair] = product[pair, 1 - core]


def outer_tall(left, right, count):
    rows, width = left.shape
    cols, part = right.shape[1], width // count
    out = pl.BlockSpec((2, part, cols), lambda i: (i, 0, 0))
    return pl.pallas_call(
        tall_kernel,
        grid=(count // 4,),
        in_specs=[pl.BlockSpec((rows, 4 * part), lambda i: (0, i)), fixed(right)],
        out_specs=[out, out],
        out_shape=[jax.ShapeDtypeStruct((count // 2, part, cols), LOW)] * 2,
        scratch_shapes=[pltpu.VMEM((2, 2, part, cols), LOW)],
        compiler_params=pltpu.CompilerParams(vmem_limit_bytes=GRANT),
        cost_estimate=pl.CostEstimate(
            flops=WEIGHT * 2 * rows * width * cols, bytes_accessed=2 * (rows * (width + cols) + width * cols), transcendentals=0),
        name="outer_tall",
    )(left, right)


def wide_kernel(starts, owners, *refs):
    lefts, rights, (keep, send, product) = refs[: max(owners) + 1], refs[max(owners) + 1 : -3], refs[-3:]
    step = pl.program_id(0)
    core = lax.axis_index("dp") & 1
    for owner, right, low, high in zip(owners, rights, starts, starts[1:]):
        left = lefts[owner]

        @pl.when((step >= low) & (step < high))
        def _():
            product[...] = dot_tn(left[...], right[...]).astype(LOW).reshape(product.shape)

    keep[...] = product[:, core]
    send[...] = product[:, 1 - core]


def outer_wide(lefts, rights, owners, count, weight=WEIGHT):
    rows, height = lefts[0].shape
    part = height // count
    starts = [0]
    for right in rights:
        starts.append(starts[-1] + right.shape[1] // WIDE)
    total = starts[-1]

    def strip(low, high):
        return pl.BlockSpec((rows, WIDE), lambda i: (0, jnp.clip(i - low, 0, high - low - 1)))

    out = pl.BlockSpec((count // 2, part, WIDE), lambda i: (0, 0, i))
    return pl.pallas_call(
        functools.partial(wide_kernel, starts, owners),
        grid=(total,),
        in_specs=[fixed(left) for left in lefts] + [strip(low, high) for low, high in zip(starts, starts[1:])],
        out_specs=[out, out],
        out_shape=[jax.ShapeDtypeStruct((count // 2, part, WIDE * total), LOW)] * 2,
        scratch_shapes=[pltpu.VMEM((count // 2, 2, part, WIDE), LOW)],
        compiler_params=pltpu.CompilerParams(vmem_limit_bytes=GRANT),
        cost_estimate=pl.CostEstimate(
            flops=weight * 2 * rows * height * WIDE * total,
            bytes_accessed=2 * (rows * (height * len(lefts) + WIDE * total) + height * WIDE * total), transcendentals=0),
        name="outer_wide",
    )(*lefts, *rights)


def spread_kernel(pairs, so_far_ref, *refs):
    total = so_far_ref[...]
    for grad, weight in zip(refs[:pairs], refs[pairs:-1]):
        total = total + dot_nt(grad[...], weight[...])
    refs[-1][...] = total.astype(refs[-1].dtype)


def spread(so_far, grads, weights, kind):
    rows = so_far.shape[0]
    strip = pl.BlockSpec((STRIP, D), lambda i: (i, 0))
    return pl.pallas_call(
        functools.partial(spread_kernel, len(grads)),
        grid=(rows // STRIP,),
        in_specs=[strip] * (1 + len(grads)) + [fixed(weight) for weight in weights],
        out_specs=strip,
        out_shape=jax.ShapeDtypeStruct((rows, D), kind),
        compiler_params=pltpu.CompilerParams(vmem_limit_bytes=32 * MIB),
        cost_estimate=pl.CostEstimate(
            flops=WEIGHT * 2 * rows * D * D * len(grads), bytes_accessed=rows * D * 10 + D * D * 2 * len(grads),
            transcendentals=0),
        name="spread",
    )(so_far, *grads, *weights)


FLIPS = {"c": 1, "x": 2, "y": 4}


def hop(array, dim, count):
    if dim in FLIPS:
        return lax.ppermute(array, "dp", [(place, place ^ FLIPS[dim]) for place in range(count)])
    step = 8 * (1 if dim == "z" else dim)
    return lax.ppermute(array, "dp", [(place, (place + step) % count) for place in range(count)])


def after(value, *earlier):
    return lax.optimization_barrier((value, earlier))[0] if earlier else value


def mine_of():
    me = lax.axis_index("dp")
    return {
        "z": lax.shift_right_logical(me, 3),
        "y": lax.shift_right_logical(me, 2) & 1,
        "x": lax.shift_right_logical(me, 1) & 1,
        "c": me & 1,
    }


def place_kernel(count, cut, bases, rows, *refs):
    pieces, outs = refs[:8], refs[8:]
    ring = count // 8
    mine = mine_of()
    slot = pl.program_id(0)
    for part, (last, low_dim) in enumerate((("x", "y"), ("y", "x"))):
        left, right = (0, cut) if part == 0 else (cut, bases[-1])
        for which in range(4):
            digits = {"c": which // 2, last: which % 2, low_dim: lax.div(slot, ring)}
            owner = lax.rem(mine["z"] + ring - lax.rem(slot, ring), ring) * 8
            for dim, weight in (("y", 4), ("x", 2), ("c", 1)):
                owner = owner + weight * (mine[dim] ^ digits[dim])
            row = pl.ds(pl.multiple_of(owner * rows, rows), rows)
            for out, base, stop in zip(outs, bases, bases[1:]):
                low, high = max(left, base), min(right, stop)
                if low < high:
                    out[row, low - base : high - base] = pieces[4 * part + which][0, :, low - left : high - left]


def whole_arrays(shard, widths):
    full = lax.all_gather(shard, "dp", axis=0, tiled=True)
    bases = [sum(widths[:index]) for index in range(len(widths) + 1)]
    return [full[:, low:high] for low, high in zip(bases, bases[1:])]


class Gathering:
    def __init__(self, shard, cut, count):
        self.count, self.cut = count, cut
        self.rows, self.cols = shard.shape
        self.stacks, self.came, self.stage = [shard[None]], [], 0

    def move(self, *gate):
        self.stage += 1
        if self.stage <= 3:
            if self.stage == 2:
                whole = jnp.concatenate(self.stacks + self.came, axis=0)
                self.stacks = [whole[:, :, : self.cut], whole[:, :, self.cut :]]
            elif self.stage == 3:
                self.stacks = [jnp.concatenate(pair, axis=0) for pair in zip(self.stacks, self.came)]
        self.stacks = [after(stack, *gate) for stack in self.stacks]
        if self.stage == 1:
            self.came = [hop(self.stacks[0], distance, self.count) for distance in range(1, self.count // 8)]
        elif self.stage <= 3:
            dims = "yx" if self.stage == 2 else "xy"
            self.came = [hop(stack, dim, self.count) for stack, dim in zip(self.stacks, dims)]
        else:
            self.stacks = [(stack, came) for stack, came in zip(self.stacks, self.came)]
            self.came = [tuple(hop(after(array, *gate), "c", self.count) for array in pair) for pair in self.stacks]
            return [array for pair in self.stacks for array in pair]
        return self.stacks

    def result(self, widths):
        pieces = [array for own, came in zip(self.stacks, self.came) for array in own + came]
        bases = [sum(widths[:index]) for index in range(len(widths) + 1)]
        size = self.count * self.rows
        return pl.pallas_call(
            functools.partial(place_kernel, self.count, self.cut, bases, self.rows),
            grid=(self.count // 4,),
            in_specs=[pl.BlockSpec((1, self.rows, piece.shape[2]), lambda i: (i, 0, 0)) for piece in pieces],
            out_specs=[held(size, width) for width in widths],
            out_shape=[jax.ShapeDtypeStruct((size, width), LOW) for width in widths],
            compiler_params=pltpu.CompilerParams(vmem_limit_bytes=24 * MIB),
            cost_estimate=pl.CostEstimate(flops=0, bytes_accessed=4 * size * bases[-1], transcendentals=0),
            name="place",
        )(*pieces)


def add_low(left_side, right_side, kind=LOW):
    return (left_side.astype(FULL) + right_side.astype(FULL)).astype(kind)


def take(blocks, axis, index):
    return lax.dynamic_index_in_dim(blocks, index, axis, keepdims=False, allow_negative_indices=False)


def split_kernel(cut, keep_ref, came_ref, keep1_ref, send1_ref, keep2_ref, send2_ref):
    mine = mine_of()
    for side in range(2):
        for keep, send, dim, cols in (
            (keep1_ref, send1_ref, "x", slice(0, cut)),
            (keep2_ref, send2_ref, "y", slice(cut, None)),
        ):
            for out, index in ((keep, mine[dim]), (send, 1 - mine[dim])):
                where = (0, side, index, slice(None), cols) if dim == "x" else (0, index, side, slice(None), cols)
                out[0, side] = add_low(keep_ref[where], came_ref[where])


def turn_kernel(keep1_ref, came1_ref, keep2_ref, came2_ref, keep3_ref, send3_ref, keep4_ref, send4_ref):
    mine = mine_of()
    for kept, came, keep, send, dim in (
        (keep1_ref, came1_ref, keep3_ref, send3_ref, "y"),
        (keep2_ref, came2_ref, keep4_ref, send4_ref, "x"),
    ):
        for out, index in ((keep, mine[dim]), (send, 1 - mine[dim])):
            out[...] = add_low(kept[:, index], came[:, index])


def tower_kernel(cut, keep3_ref, came3_ref, keep4_ref, came4_ref, *outs):
    own = mine_of()["z"]
    ring = keep3_ref.shape[0]
    for distance, out in enumerate(outs):
        index = lax.rem(own + distance, ring)
        out[:, :cut] = add_low(keep3_ref[index], came3_ref[index])
        out[:, cut:] = add_low(keep4_ref[index], came4_ref[index])


def local_kernel(kernel, name, outs, grid, in_specs, out_specs, operands):
    size = sum(array.size * array.dtype.itemsize for array in operands)
    return pl.pallas_call(
        kernel,
        grid=grid,
        in_specs=in_specs,
        out_specs=out_specs,
        out_shape=outs,
        compiler_params=pltpu.CompilerParams(vmem_limit_bytes=GRANT),
        cost_estimate=pl.CostEstimate(
            flops=WEIGHT * 10**10 if name == "turn" else 0, bytes_accessed=2 * size, transcendentals=0),
        name=name,
    )(*operands)


class Sums:
    def __init__(self, keep, send, count):
        self.count, self.ring = count, count // 8
        self.rows, self.cols = keep.shape[1:]
        self.cut = self.cols // 2
        self.stage = 0
        self.keeps, self.sends, self.dims = [keep], [send], ["c"]

    def start(self):
        self.came = [hop(send, dim, self.count) for send, dim in zip(self.sends, self.dims)]
        return self.sends

    def move(self, *gate):
        came = [after(array, *gate) for array in self.came]
        ring, rows, cut, rest = self.ring, self.rows, self.cut, self.cols - self.cut
        self.stage += 1
        if self.stage == 1:
            whole = lambda array: array.reshape(ring, 2, 2, rows, self.cols)
            block = pl.BlockSpec((1, 2, 2, rows, self.cols), lambda i: (i, 0, 0, 0, 0))
            widths = (cut, cut, rest, rest)
            self.pairs(local_kernel(
                functools.partial(split_kernel, cut), "split",
                [jax.ShapeDtypeStruct((ring, 2, rows, width), LOW) for width in widths], (ring,), [block] * 2,
                [pl.BlockSpec((1, 2, rows, width), lambda i: (i, 0, 0, 0)) for width in widths],
                [whole(self.keeps[0]), whole(came[0])],
            ), ["x", "y"])
        elif self.stage == 2:
            operands = [self.keeps[0], came[0], self.keeps[1], came[1]]
            self.pairs(local_kernel(
                turn_kernel, "turn",
                [jax.ShapeDtypeStruct((ring, rows, width), LOW) for width in (cut, cut, rest, rest)], (ring,),
                [pl.BlockSpec((1,) + array.shape[1:], lambda i: (i, 0, 0, 0)) for array in operands],
                [pl.BlockSpec((1, rows, width), lambda i: (i, 0, 0)) for width in (cut, cut, rest, rest)],
                operands,
            ), ["y", "x"])
        elif self.stage == 3:
            operands = [self.keeps[0], came[0], self.keeps[1], came[1]]
            outs = local_kernel(
                functools.partial(tower_kernel, cut), "tower",
                [jax.ShapeDtypeStruct((rows, self.cols), LOW)] * ring, (1,),
                [fixed(array) for array in operands], [held(rows, self.cols)] * ring, operands,
            )
            self.keeps, self.sends, self.dims = list(outs[:1]), list(outs[1:]), list(range(1, ring))
        else:
            self.total = self.keeps[0].astype(FULL)
            for array in came:
                self.total = self.total + array.astype(FULL)
            return [self.total]
        return self.start()

    def pairs(self, arrays, dims):
        self.keeps, self.sends, self.dims = [arrays[0], arrays[2]], [arrays[1], arrays[3]], dims


class EverySum:
    def __init__(self, rows, count):
        self.count, self.todo = count, ["c", "x", "y"]
        self.sent = [rows]
        self.came = [hop(rows, "c", count)]

    def move(self, *gate):
        came = [after(array, *gate) for array in self.came]
        self.sent = [functools.reduce(jnp.add, came, self.sent[0])]
        self.todo = self.todo[1:]
        dims = self.todo[:1] or list(range(1, self.count // 8))
        if self.came and len(self.came) == 1:
            self.came = [hop(self.sent[0], dim, self.count) for dim in dims]
        return self.sent


def local(
    tokens,
    w_query,
    w_key,
    w_value,
    w_out,
    w_up,
    w_down,
    b_query,
    b_value,
    b_out,
    b_up,
    b_down,
    gain_attn,
    shift_attn,
    gain_ffn,
    shift_ffn,
    cotangent,
):
    count = D // w_query.shape[0]
    part = D // count
    wide = w_up.shape[1]
    custom = count == 32
    small = (b_query, b_value, b_out, b_down, gain_attn, shift_attn, gain_ffn, shift_ffn)
    packed = sum(
        jnp.pad(array[None], ((row, 15 - row), (0, 128 - array.shape[0]))) for row, array in enumerate(small + (b_up,))
    )
    height = max(part, 16)
    tops = [jnp.pad(array, ((0, height - part), (0, 0))) for array in (w_query, w_key, w_value)]
    early = jnp.concatenate(tops + [jnp.pad(packed, ((0, height - 16), (0, 0)))], axis=1)
    widths = (D, D, D, 128)
    w_rise = jnp.concatenate([w_up, w_out], axis=1)
    if custom:
        first_gather = Gathering(early, 3 * D // 2 + 128, count)
        for stage in range(4):
            first_gather.move()
            if stage == 1:
                w_rise = after(w_rise, *first_gather.stacks)
        w_query, w_key, w_value, packed = first_gather.result(widths)
    else:
        w_query, w_key, w_value, packed = whole_arrays(early, widths)
    if height > part:
        w_query, w_key, w_value = [
            array.reshape(count, height, D)[:, :part].reshape(D, D) for array in (w_query, w_key, w_value)
        ]
    w_rise = lax.all_gather(w_rise, "dp", axis=0, tiled=True)
    packed = packed.reshape(count, height, 128)
    vector = lambda row: packed[:, row, :part].reshape(1, D).astype(FULL)
    b_query, b_value, b_out, b_down, gain_attn, shift_attn, gain_ffn, shift_ffn = map(vector, range(8))
    b_up = packed[:, 8, : wide // count].reshape(1, wide).astype(FULL)
    chunks = wide // WIDE
    sequences = tokens.shape[0] // LEN

    down_gather = Gathering(w_down, D // 2, count) if custom else None

    def under(value, *gate):
        return after(value, *down_gather.move(*gate)) if custom else value

    tokens_in = under(tokens, w_query)
    queries = (dot_nn(tokens_in, w_query) + b_query).astype(LOW)
    keys = dot_nn(tokens_in, w_key).astype(LOW)
    values = (dot_nn(tokens_in, w_value) + b_value).astype(LOW)
    seen = attend(queries, keys, values, 0)
    values = under(values, seen[1])
    for sequence in range(1, sequences):
        seen = attend(queries, keys, values, sequence, seen)
    probs, attn_rows = seen
    attn_rows = under(attn_rows, attn_rows)
    normed, inverse, first_low = branch(attn_rows, tokens, w_rise, b_out, gain_attn, shift_attn)
    half = widen(first_low, w_rise, b_up, 0, chunks // 2)
    half_low = under(first_low, half[0])
    hidden, slope = widen(half_low, w_rise, b_up, chunks // 2, chunks, half)
    if custom:
        (w_down,) = down_gather.result((D,))
    else:
        w_down = lax.all_gather(w_down, "dp", axis=0, tiled=True)
    result, second, d_ffn, sums_ffn = fall(
        hidden, w_down, normed, cotangent, b_down, gain_attn, shift_attn, gain_ffn, shift_ffn
    )

    if custom:
        down = Sums(*outer_tall(hidden, d_ffn, count), count)
        second = after(second, *down.start())
    d_pre, d_wide, d_first = narrow(d_ffn, slope, w_down, w_rise, second, 0, chunks)
    if custom:
        d_first = after(d_first, *down.move(d_wide))
    d_resid, d_branch, d_attn, sums_attn = resid_back(d_first, normed, inverse, gain_attn, w_rise)
    if custom:
        up = Sums(*outer_wide([first_low, attn_rows], [d_pre, d_branch], (0, 1), count), count)
        d_attn = after(d_attn, *up.start())
        d_attn = after(d_attn, *down.move(*up.keeps))
    seen = attend_back(queries, keys, values, probs, d_attn, 0)
    if custom:
        d_attn = after(d_attn, *up.move(seen[0]))
        d_attn = after(d_attn, *down.move(seen[0]))
    for sequence in range(1, sequences):
        seen = attend_back(queries, keys, values, probs, d_attn, sequence, seen)
    d_queries, d_keys, d_values = seen
    column_sum = lambda rows: jnp.sum(rows.astype(FULL), axis=0, keepdims=True)
    sums = jnp.concatenate([
        column_sum(d_queries), column_sum(d_values), sums_attn[2:], sums_ffn[2:], sums_attn[:2], sums_ffn[:2],
        d_wide.reshape(-1, D),
    ], axis=0)
    if custom:
        sums = EverySum(sums, count)
        d_queries = after(d_queries, *sums.sent)
        first = Sums(*outer_wide([tokens], [d_queries, d_keys, d_values], (0, 0, 0), count, 0), count)
        d_queries = after(d_queries, *first.start())
        down.move(*first.keeps)
        d_queries = after(d_queries, *sums.move(*first.keeps))
        d_queries = after(d_queries, *up.move(*first.keeps))
        d_queries = after(d_queries, *first.move(*up.keeps))
    grad_rows = spread(d_resid, [d_queries, d_keys, d_values], [w_query, w_key, w_value], LOW)

    if custom:
        up.move(grad_rows)
        first.move(*up.keeps)
        sums.move(grad_rows)
        first.move()
        sums.move()
        sums = sums.move()[0]
        up.move()
        first.move()
        d_w_down, second, first = down.total, up.total, first.total
        d_w_up, d_w_out = second[:, :wide], second[:, wide:]
        d_w_query, d_w_key, d_w_value = first[:, :D], first[:, D : 2 * D], first[:, 2 * D :]
    else:
        total = lambda grad: lax.psum_scatter(grad.astype(LOW), "dp", scatter_dimension=0, tiled=True).astype(FULL)
        d_w_down = total(dot_tn(hidden, d_ffn))
        d_w_up = total(dot_tn(first_low, d_pre))
        d_w_out = total(dot_tn(attn_rows, d_branch))
        d_w_query, d_w_key, d_w_value = [total(dot_tn(tokens, grad)) for grad in (d_queries, d_keys, d_values)]
        sums = lax.psum(sums, "dp")
    me = lax.axis_index("dp")
    own = lax.dynamic_slice_in_dim(sums[:8], me * part, part, axis=1, allow_negative_indices=False)
    vector = lambda row: own[row]
    d_b_up = lax.dynamic_slice_in_dim(
        sums[8:].reshape(-1), me * (wide // count), wide // count, allow_negative_indices=False
    )
    return (
        result,
        grad_rows,
        d_w_query,
        d_w_key,
        d_w_value,
        d_w_out,
        d_w_up,
        d_w_down,
        vector(0),
        vector(1),
        vector(2),
        d_b_up,
        vector(3),
        vector(4),
        vector(5),
        vector(6),
        vector(7),
    )


def solution(mesh):
    placed = (
        P("dp", None),
        P("dp", None),
        P("dp", None),
        P("dp", None),
        P("dp", None),
        P("dp", None),
        P("dp", None),
        P("dp"),
        P("dp"),
        P("dp"),
        P("dp"),
        P("dp"),
        P("dp"),
        P("dp"),
        P("dp"),
        P("dp"),
        P("dp", None),
    )
    return jax.shard_map(
        local,
        mesh=mesh,
        in_specs=placed,
        out_specs=(
            P("dp", None),
            P("dp", None),
            P("dp", None),
            P("dp", None),
            P("dp", None),
            P("dp", None),
            P("dp", None),
            P("dp", None),
            P("dp"),
            P("dp"),
            P("dp"),
            P("dp"),
            P("dp"),
            P("dp"),
            P("dp"),
            P("dp"),
            P("dp"),
        ),
        check_vma=False,
    )
```
